128 devices in a mesh: frame: 16 (over z, x), head: 8 (over y, core).
Axes of the slice: x: 4, y: 4, z: 4, core: 2. Of those that a mesh axis runs over, the one named last changes fastest.
Arguments:
- fresh_queries: bfloat16 [16, 256, 5120], P('frame', 'head'), may hold values from -35 to 35
- fresh_keys: bfloat16 [16, 256, 5120], P('frame', 'head'), may hold values from -35 to 35
- fresh_values: bfloat16 [16, 256, 5120], P('frame', 'head'), may hold values from -6 to 6
- key_cache: bfloat16 [16, 3584, 5120], P('frame', None, 'head'), may hold values from -6 to 6
- value_cache: bfloat16 [16, 3584, 5120], P('frame', None, 'head'), may hold values from -6 to 6
- masked_blocks: int32 [16, 2], replicated, may hold values from 0 to 27, as said below
- masked_count: int32 [16], replicated, may hold values from 1 to 2, as said below
- radial_counts: int32 [15], replicated, may hold values from 1 to 3, as said below
Outputs:
- edited: bfloat16 [16, 256, 5120], P('frame', 'head')
The draws below stay inside these ranges and needn't reach their ends.
Inputs may be any that keep to these rules, and one draw needn't show every extreme that they name: `masked_blocks`: the 2 block numbers of one frame are different. `masked_count`: some frame has 2. `radial_counts`: entry d - 1 belongs to frame distance d; distance 1 has 3.
All inputs are finite; a program needn't handle non-finite values.
Results may differ from the reference program's by a relative error of at most 0.0095.
Values may be sent and summed in bfloat16 or wider, within the bound.
No kernel may reach another device: no remote copies, remote signals or barrier semaphores. Data moves between devices by JAX's collectives and lax.ppermute only.
A program may use at most 256 MiB of HBM per device.

```python
import math
import jax
import jax.numpy as jnp
from jax import lax

H = 40
HD = 128
BLK = 128
NBLK = 28
MB = 2
CMAX = 3
FRAMES = 16
TOKF = 3584


def draw_fresh_queries(key, part):
    full_shape = (FRAMES, MB * BLK, H * HD)
    noise_field = 1.5 * jnp.clip(jax.random.normal(jax.random.fold_in(key, 12), full_shape, jnp.float32), -5.0, 5.0)
    return noise_field.astype(jnp.bfloat16)


def draw_fresh_keys(key, part):
    full_shape = (FRAMES, MB * BLK, H * HD)
    noise_field = jnp.clip(jax.random.normal(jax.random.fold_in(key, 13), full_shape, jnp.float32), -5.0, 5.0)
    return noise_field.astype(jnp.bfloat16)


def draw_masked_blocks(key, part):
    frame_keys = jax.random.split(jax.random.fold_in(key, 21), FRAMES)
    return jax.vmap(lambda one_key: jax.random.permutation(one_key, NBLK)[:MB])(frame_keys).astype(jnp.int32)


def draw_masked_count(key, part):
    counts = jax.random.randint(jax.random.fold_in(key, 22), (FRAMES,), 1, MB + 1).astype(jnp.int32)
    fullest = jax.random.randint(jax.random.fold_in(key, 23), (), 0, FRAMES)
    return counts.at[fullest].set(MB)


def draw_radial_counts(key, part):
    counts = jax.random.randint(jax.random.fold_in(key, 24), (FRAMES - 1,), 1, CMAX + 1).astype(jnp.int32)
    return counts.at[0].set(CMAX)


def block_levels(stream_key, extent, shards, smallest, high):
    def one(position, blocks):
        draws = jax.random.uniform(jax.random.fold_in(jax.random.fold_in(stream_key, 6), position), (blocks,), jnp.float32, smallest / len(shards), high / len(shards))
        return jnp.repeat(jnp.exp(draws), extent[position] // blocks).reshape((-1,) + (1,) * (len(extent) - position - 1))

    level = one(*shards[0])
    for cut in shards[1:]:
        level = level * one(*cut)
    return level


def normal_values(key, shape, deviation, limit, pieces=(), kind=jnp.bfloat16):
    drawn = deviation * jax.random.normal(key, shape, jnp.float32)
    if pieces:
        drawn = drawn * block_levels(key, shape, pieces, -0.22, 0.18)
    return jnp.clip(drawn, -limit, limit).astype(kind)


def setup_inputs(seed: int = 0) -> dict:
    arg_keys = jax.random.split(jax.random.key(seed), 9)
    fresh_queries = draw_fresh_queries(jax.random.fold_in(arg_keys[8], 71), 0)
    fresh_keys = draw_fresh_keys(jax.random.fold_in(arg_keys[8], 71), 0)
    fresh_values = normal_values(arg_keys[2], (FRAMES, MB * BLK, H * HD), 1.0, 6.0, ((0, 16), (1, 8)))
    key_cache = normal_values(arg_keys[3], (FRAMES, TOKF, H * HD), 1.0, 6.0, ((0, 16), (2, 8)))
    value_cache = normal_values(arg_keys[4], (FRAMES, TOKF, H * HD), 1.0, 6.0, ((0, 16), (2, 8)))
    masked_blocks = draw_masked_blocks(jax.random.fold_in(arg_keys[8], 71), 0)
    masked_count = draw_masked_count(jax.random.fold_in(arg_keys[8], 71), 0)
    radial_counts = draw_radial_counts(jax.random.fold_in(arg_keys[8], 71), 0)
    return dict(fresh_queries=fresh_queries, fresh_keys=fresh_keys, fresh_values=fresh_values, key_cache=key_cache, value_cache=value_cache, masked_blocks=masked_blocks, masked_count=masked_count, radial_counts=radial_counts)


neg_fill = -1e+30

def renew(entries):
    key_rows, value_rows, new_keys, new_values, blocks, live_count = entries
    for slot_index in range(MB):
        offset = (blocks[slot_index] * BLK).astype(jnp.int32)
        is_live = slot_index < live_count
        key_piece = jnp.where(is_live, new_keys[slot_index * BLK:(slot_index + 1) * BLK], lax.dynamic_slice_in_dim(key_rows, offset, BLK, 0))
        key_rows = lax.dynamic_update_slice_in_dim(key_rows, key_piece, offset, 0)
        value_piece = jnp.where(is_live, new_values[slot_index * BLK:(slot_index + 1) * BLK], lax.dynamic_slice_in_dim(value_rows, offset, BLK, 0))
        value_rows = lax.dynamic_update_slice_in_dim(value_rows, value_piece, offset, 0)
    return (key_rows, value_rows)

def reference(fresh_queries, fresh_keys, fresh_values, key_cache, value_cache, masked_blocks, masked_count, radial_counts):
    frame_total = fresh_queries.shape[0]
    window_width = CMAX * BLK
    score_scale = 1.0 / math.sqrt(HD)
    all_keys, all_values = lax.map(renew, (key_cache, value_cache, fresh_keys, fresh_values, masked_blocks, masked_count))
    frame_ids = jnp.arange(frame_total, dtype=jnp.int32)
    offsets = jnp.arange(window_width, dtype=jnp.int32)

    def attend(entries):
        query_rows, blocks, frame_id, live_count = entries
        distance = jnp.abs(frame_id - frame_ids)
        seen_count = jnp.where(distance == 0, 0, radial_counts[jnp.maximum(distance - 1, 0)]).astype(jnp.int32)
        own_keys = lax.dynamic_index_in_dim(all_keys, frame_id, 0, keepdims=False).astype(jnp.float32).reshape(NBLK * BLK, H, HD)
        own_values = lax.dynamic_index_in_dim(all_values, frame_id, 0, keepdims=False).astype(jnp.float32).reshape(NBLK * BLK, H, HD)
        usable = (offsets // BLK)[None, :] < seen_count[:, None]
        results = []
        for slot_index in range(MB):
            query_heads = query_rows[slot_index * BLK:(slot_index + 1) * BLK].astype(jnp.float32).reshape(BLK, H, HD)
            first_block = jnp.mod(blocks[slot_index] - seen_count // 2, NBLK).astype(jnp.int32)
            row_index = jnp.mod(first_block[:, None] * BLK + offsets[None, :], NBLK * BLK).astype(jnp.int32)
            window_keys = all_keys[frame_ids[:, None], row_index].astype(jnp.float32).reshape(frame_total, window_width, H, HD)
            window_values = all_values[frame_ids[:, None], row_index].astype(jnp.float32).reshape(frame_total, window_width, H, HD)
            far_scores = jnp.einsum('qhd,fkhd->hqfk', query_heads, window_keys) * score_scale
            far_scores = jnp.where(usable[None, None], far_scores, neg_fill)
            near_scores = jnp.einsum('qhd,khd->hqk', query_heads, own_keys) * score_scale
            maximum = jnp.maximum(lax.optimization_barrier(jnp.max(far_scores, axis=(2, 3))), lax.optimization_barrier(jnp.max(near_scores, axis=2)))
            far_weights = jnp.exp(far_scores - maximum[:, :, None, None])
            near_weights = jnp.exp(near_scores - maximum[:, :, None])
            totals = lax.optimization_barrier(jnp.sum(far_weights, axis=(2, 3))) + lax.optimization_barrier(jnp.sum(near_weights, axis=2))
            far_rounded = lax.optimization_barrier(far_weights.astype(jnp.bfloat16)).astype(jnp.float32)
            near_rounded = lax.optimization_barrier(near_weights.astype(jnp.bfloat16)).astype(jnp.float32)
            summed = jnp.einsum('hqfk,fkhd->qhd', far_rounded, window_values) + jnp.einsum('hqk,khd->qhd', near_rounded, own_values)
            ratio = summed / jnp.transpose(totals)[:, :, None]
            ratio = jnp.where(slot_index < live_count, ratio, 0.0)
            results.append(ratio.reshape(BLK, H * HD).astype(jnp.bfloat16))
        return jnp.concatenate(results, axis=0)
    return lax.map(attend, (fresh_queries, masked_blocks, frame_ids, masked_count))
```

```python
import functools
import math

import jax
import jax.numpy as jnp
from jax import lax
from jax.experimental import pallas as pl
from jax.experimental.pallas import tpu as pltpu
from jax.sharding import PartitionSpec as P

HD = 128
BLK = 128
NBLK = 28
MB = 2
CMAX = 3
HEADS = 5
WIDE = HEADS * HD
SIDE = 4
STAT = 16
PAY = SIDE * BLK + STAT
EXPO = math.log2(math.e) / math.sqrt(HD)
LOW = -1e30
VMEM_LIMIT = 50 * 1024 * 1024


def lanes(h):
    return slice(h * HD, (h + 1) * HD)


def params(**kw):
    return pltpu.CompilerParams(vmem_limit_bytes=VMEM_LIMIT, **kw)


def split_kernel(*refs):
    n = len(refs) // 2
    for src, dst in zip(refs[:n], refs[n:]):
        for j in range(8):
            dst[j] = src[:, j * WIDE : (j + 1) * WIDE]


def split_heads(*arrays):
    rows = arrays[0].shape[0]
    return pl.pallas_call(
        split_kernel,
        out_shape=[jax.ShapeDtypeStruct((8, rows, WIDE), jnp.bfloat16)] * len(arrays),
        compiler_params=params(),
        name="split_heads",
    )(*arrays)


def join_kernel(src, dst):
    for j in range(8):
        dst[:, j * WIDE : (j + 1) * WIDE] = src[j]


def join_heads(x):
    return pl.pallas_call(
        join_kernel,
        out_shape=jax.ShapeDtypeStruct((x.shape[1], 8 * WIDE), jnp.bfloat16),
        compiler_params=params(),
        name="join_heads",
    )(x)


NEAR_BLOCKS = 4
NEAR_ROWS = NEAR_BLOCKS * BLK


def near_kernel(
    mine, q_ref, nk_ref, nv_ref, kc_ref, vc_ref, k_out, vt_out, o_out, s_out, acc, top, tot, vbuf
):
    step = pl.program_id(0)

    @pl.when(step == 0)
    def _():
        acc[...] = jnp.zeros_like(acc)
        top[...] = jnp.full_like(top, LOW)
        tot[...] = jnp.zeros_like(tot)

    k_out[...] = kc_ref[...]
    vbuf[...] = vc_ref[...]
    for s in range(MB):
        spot = mine[s] - step * NEAR_BLOCKS
        live = (mine[MB] > s) & (spot >= 0) & (spot < NEAR_BLOCKS)

        @pl.when(live)
        def _():
            rows = pl.ds(pl.multiple_of(spot * BLK, BLK), BLK)
            k_out[rows, :] = nk_ref[s * BLK : (s + 1) * BLK, :]
            vbuf[rows, :] = nv_ref[s * BLK : (s + 1) * BLK, :]

    for h in range(HEADS):
        for b in range(NEAR_BLOCKS):
            vt_out[b, lanes(h), :] = vbuf[b * BLK : (b + 1) * BLK, lanes(h)].T
        scores = lax.dot_general(
            k_out[:, lanes(h)],
            q_ref[:, lanes(h)],
            (((1,), (1,)), ((), ())),
            preferred_element_type=jnp.float32,
        )
        old = top[h : h + 1, :]
        new = jnp.maximum(old, jnp.max(scores, axis=0, keepdims=True))
        weights = jnp.exp2((scores - new) * EXPO)
        shrink = jnp.exp2((old - new) * EXPO)
        top[h : h + 1, :] = new
        tot[h : h + 1, :] = tot[h : h + 1, :] * shrink + jnp.sum(weights, axis=0, keepdims=True)
        values = jnp.concatenate([vt_out[b, lanes(h), :] for b in range(NEAR_BLOCKS)], axis=1)
        acc[h] = acc[h] * shrink + jnp.dot(
            values, weights.astype(jnp.bfloat16), preferred_element_type=jnp.float32
        )

    @pl.when(step == NBLK // NEAR_BLOCKS - 1)
    def _():
        for h in range(HEADS):
            total = tot[h : h + 1, :]
            part = acc[h] * (1.0 / total)
            level = top[h : h + 1, :] * EXPO + jnp.log2(total)
            for s in range(MB):
                o_out[s, :, lanes(h)] = part[:, s * BLK : (s + 1) * BLK].astype(jnp.bfloat16)
                s_out[s : s + 1, lanes(h)] = level[:, s * BLK : (s + 1) * BLK]


def near(mine, q, new_k, new_v, key_cache, value_cache):
    steps = NBLK // NEAR_BLOCKS
    whole = lambda shape: pl.BlockSpec(shape, lambda i, *_: (0,) * len(shape))
    piece = pl.BlockSpec((NEAR_ROWS, WIDE), lambda i, *_: (i, 0))
    rows = MB * BLK
    return pl.pallas_call(
        near_kernel,
        grid_spec=pltpu.PrefetchScalarGridSpec(
            num_scalar_prefetch=1,
            grid=(steps,),
            in_specs=[whole((rows, WIDE)), whole((rows, WIDE)), whole((rows, WIDE)), piece, piece],
            out_specs=[
                piece,
                pl.BlockSpec((NEAR_BLOCKS, WIDE, BLK), lambda i, *_: (i, 0, 0)),
                whole((MB, HD, WIDE)),
                whole((8, WIDE)),
            ],
            scratch_shapes=[
                pltpu.VMEM((HEADS, HD, rows), jnp.float32),
                pltpu.VMEM((8, rows), jnp.float32),
                pltpu.VMEM((8, rows), jnp.float32),
                pltpu.VMEM((NEAR_ROWS, WIDE), jnp.bfloat16),
            ],
        ),
        out_shape=[
            jax.ShapeDtypeStruct((NBLK * BLK, WIDE), jnp.bfloat16),
            jax.ShapeDtypeStruct((NBLK, WIDE, BLK), jnp.bfloat16),
            jax.ShapeDtypeStruct((MB, HD, WIDE), jnp.bfloat16),
            jax.ShapeDtypeStruct((8, WIDE), jnp.float32),
        ],
        compiler_params=params(),
        cost_estimate=pl.CostEstimate(
            flops=4 * rows * NBLK * BLK * WIDE * 4, bytes_accessed=19_000_000, transcendentals=4_600_000
        ),
        name="near",
    )(mine, q, new_k, new_v, key_cache, value_cache)


def put_stats(stat, index, h, level):
    high = level.astype(jnp.bfloat16).astype(jnp.float32)
    rest = level - high
    mid = rest.astype(jnp.bfloat16).astype(jnp.float32)
    row = lax.broadcasted_iota(jnp.int32, (STAT, HD), 0) - index
    tile = stat[:, lanes(h)]
    for place, piece in ((0, high), (SIDE, mid), (2 * SIDE, rest - mid)):
        tile = jnp.where(row == place, piece, tile)
    stat[:, lanes(h)] = tile


def far_kernel(frame_of, slot, skip, first, seen, alive, q_ref, *rest):
    keys, values, out, stat = rest[:CMAX], rest[CMAX : 2 * CMAX], rest[-2], rest[-1]
    item = pl.program_id(0) + skip
    frame = frame_of(item, alive)
    count = seen[frame]
    live = alive[frame] > slot

    @pl.when(pl.program_id(0) == 0)
    def _():
        stat[...] = jnp.zeros_like(stat)

    rows = pl.ds(pl.multiple_of(item * BLK, BLK), BLK)
    for n in range(1, CMAX + 1):

        @pl.when(live & (count == n))
        def _():
            for h in range(HEADS):
                key = jnp.concatenate([keys[j][:, lanes(h)] for j in range(n)], axis=0)
                scores = lax.dot_general(
                    key,
                    q_ref[:, lanes(h)],
                    (((1,), (1,)), ((), ())),
                    preferred_element_type=jnp.float32,
                )
                top = jnp.max(scores, axis=0, keepdims=True)
                weights = jnp.exp2((scores - top) * EXPO)
                total = jnp.sum(weights, axis=0, keepdims=True)
                value = jnp.concatenate([values[j][0, lanes(h), :] for j in range(n)], axis=1)
                part = jnp.dot(value, weights.astype(jnp.bfloat16), preferred_element_type=jnp.float32)
                out[rows, lanes(h)] = (part * (1.0 / total)).astype(jnp.bfloat16)
                put_stats(stat, item, h, top * EXPO + jnp.log2(total))

    @pl.when(pl.program_id(0) == pl.num_programs(0) - 1)
    def _():
        out[SIDE * BLK :, :] = stat[...].astype(jnp.bfloat16)


def far(table, q, keys, values, shift, slot, skip):
    first, seen, alive = table

    def frame_of(item, alive_ref):
        me = alive_ref[SIDE * SIDE]
        z, x = me // SIDE, me % SIDE
        if slot == 0:
            z, x = (z + shift) % SIDE, (x + item) % SIDE
        else:
            z, x = (z + item) % SIDE, (x + shift) % SIDE
        return z * SIDE + x

    def block(j, item, first_ref, seen_ref, alive_ref):
        frame = frame_of(item + skip, alive_ref)
        spot = first_ref[frame * MB + slot] + jnp.minimum(j, seen_ref[frame] - 1)
        return jnp.where(spot >= NBLK, spot - NBLK, spot)

    items = SIDE - skip
    key_specs = [
        pl.BlockSpec((BLK, WIDE), lambda i, *r, j=j: (block(j, i, *r), 0)) for j in range(CMAX)
    ]
    value_specs = [
        pl.BlockSpec((1, WIDE, BLK), lambda i, *r, j=j: (block(j, i, *r), 0, 0)) for j in range(CMAX)
    ]
    return pl.pallas_call(
        functools.partial(far_kernel, frame_of, slot, skip),
        grid_spec=pltpu.PrefetchScalarGridSpec(
            num_scalar_prefetch=3,
            grid=(items,),
            in_specs=[pl.BlockSpec((BLK, WIDE), lambda i, *_: (i, 0))] + key_specs + value_specs,
            out_specs=pl.BlockSpec((PAY, WIDE), lambda i, *_: (0, 0)),
            scratch_shapes=[pltpu.VMEM((STAT, WIDE), jnp.float32)],
        ),
        out_shape=jax.ShapeDtypeStruct((PAY, WIDE), jnp.bfloat16),
        compiler_params=params(),
        cost_estimate=pl.CostEstimate(
            flops=4 * items * BLK * CMAX * BLK * WIDE * 4,
            bytes_accessed=items * 4 * CMAX * BLK * WIDE,
            transcendentals=items * BLK * CMAX * BLK * HEADS,
        ),
        name="far",
    )(first, seen, alive, q, *([keys] * CMAX), *([values] * CMAX))


def read_level(ref, base, index):
    tile = ref[base : base + STAT, :].astype(jnp.float32)
    return (
        tile[index : index + 1]
        + tile[SIDE + index : SIDE + index + 1]
        + tile[2 * SIDE + index : 2 * SIDE + index + 1]
    )


def merge(levels, parts):
    top = functools.reduce(jnp.maximum, levels)
    shares = [jnp.exp2(level - top) for level in levels]
    total = functools.reduce(jnp.add, shares)
    scale = 1.0 / total
    out = None
    for share, part in zip(shares, parts):
        term = part() * (share * scale)
        out = term if out is None else out + term
    return out, top + jnp.log2(total)


def first_merge_kernel(slot, near_ref, near_stat, local, one, two, three, *outs):
    *outs, stat = outs
    for d in range(SIDE):
        sources = [one, two, three]
        levels = [read_level(r, SIDE * BLK, d) for r in sources]
        parts = [
            functools.partial(lambda r: r[d * BLK : (d + 1) * BLK, :].astype(jnp.float32), r)
            for r in sources
        ]
        if d == 0:
            levels.append(near_stat[slot : slot + 1, :])
            parts.append(lambda: near_ref[slot].astype(jnp.float32))
        else:
            levels.append(read_level(local, SIDE * BLK, d))
            parts.append(lambda: local[d * BLK : (d + 1) * BLK, :].astype(jnp.float32))
        value, level = merge(levels, parts)
        outs[d][:BLK, :] = value.astype(jnp.bfloat16)
        stat[...] = jnp.zeros_like(stat)
        for h in range(HEADS):
            put_stats(stat, 0, h, level[:, lanes(h)])
        outs[d][BLK:, :] = stat[...].astype(jnp.bfloat16)


def first_merge(slot, near_part, near_stat, local, received):
    return pl.pallas_call(
        functools.partial(first_merge_kernel, slot),
        out_shape=[jax.ShapeDtypeStruct((BLK + STAT, WIDE), jnp.bfloat16)] * SIDE,
        scratch_shapes=[pltpu.VMEM((STAT, WIDE), jnp.float32)],
        compiler_params=params(),
        cost_estimate=pl.CostEstimate(flops=8_000_000, bytes_accessed=3_500_000, transcendentals=0),
        name="first_merge",
    )(near_part, near_stat, local, *received)


def last_merge_kernel(mine, *refs):
    *refs, out = refs
    for slot in range(MB):
        sources = refs[slot * SIDE : (slot + 1) * SIDE]
        live = mine[MB] > slot

        @pl.when(live)
        def _():
            levels = [read_level(r, BLK, 0) for r in sources]
            parts = [
                functools.partial(lambda r: r[:BLK, :].astype(jnp.float32), r) for r in sources
            ]
            value, _ = merge(levels, parts)
            for h in range(HEADS):
                out[slot * BLK : (slot + 1) * BLK, lanes(h)] = value[:, lanes(h)].T.astype(jnp.bfloat16)

        @pl.when(jnp.logical_not(live))
        def _():
            out[slot * BLK : (slot + 1) * BLK, :] = jnp.zeros((BLK, WIDE), jnp.bfloat16)


def last_merge(mine, parts):
    vmem = pl.BlockSpec(memory_space=pltpu.VMEM)
    return pl.pallas_call(
        last_merge_kernel,
        in_specs=[pl.BlockSpec(memory_space=pltpu.SMEM)] + [vmem] * len(parts),
        out_specs=vmem,
        out_shape=jax.ShapeDtypeStruct((MB * BLK, WIDE), jnp.bfloat16),
        compiler_params=params(),
        name="last_merge",
    )(mine, *parts)


def shift_to(x, dz, dx):
    pairs = [
        (z * SIDE + c, ((z + dz) % SIDE) * SIDE + (c + dx) % SIDE)
        for z in range(SIDE)
        for c in range(SIDE)
    ]
    return lax.ppermute(x, "frame", pairs)


def fetch(x, slot, k, step):
    along_x = (slot == 0) == (step == 1)
    return shift_to(x, 0, -k) if along_x else shift_to(x, -k, 0)


def give(x, slot, k, step):
    along_x = (slot == 0) == (step == 1)
    return shift_to(x, 0, k) if along_x else shift_to(x, k, 0)


ORDER = (1, 3, 2)


def body(
    fresh_queries,
    fresh_keys,
    fresh_values,
    key_cache,
    value_cache,
    masked_blocks,
    masked_count,
    radial_counts,
):
    me = lax.axis_index("frame").astype(jnp.int32)
    frames = jnp.arange(SIDE * SIDE, dtype=jnp.int32)
    spread = jnp.maximum(jnp.abs(frames - me) - 1, 0)
    seen = jnp.sum(
        jnp.where(spread[:, None] == jnp.arange(radial_counts.shape[0]), radial_counts, 0), axis=1
    ).astype(jnp.int32)
    first = jnp.mod(masked_blocks - (seen // 2)[:, None], NBLK).reshape(-1).astype(jnp.int32)
    alive = jnp.concatenate([masked_count, me[None]])
    table = (first, seen, alive)
    mine = jnp.concatenate(
        [
            lax.dynamic_index_in_dim(masked_blocks, me, 0, keepdims=False),
            lax.dynamic_index_in_dim(masked_count, me, 0),
        ]
    )

    (q_split,) = split_heads(fresh_queries[0])
    q = lax.all_to_all(q_split, "head", 0, 0, tiled=True).reshape(MB * BLK, WIDE)
    halves = [q[:BLK], q[BLK:]]
    ring = [[None] * SIDE for _ in range(MB)]
    for k in ORDER:
        for slot in range(MB):
            ring[slot][k] = fetch(halves[slot], slot, k, 1)
    k_split, v_split = split_heads(fresh_keys[0], fresh_values[0])
    new_k = lax.all_to_all(k_split, "head", 0, 0, tiled=True).reshape(MB * BLK, WIDE)
    new_v = lax.all_to_all(v_split, "head", 0, 0, tiled=True).reshape(MB * BLK, WIDE)

    others = [jnp.concatenate(ring[slot][1:], axis=0) for slot in range(MB)]
    full = [jnp.concatenate([halves[slot], others[slot]], axis=0) for slot in range(MB)]
    queries = [[None] * SIDE for _ in range(MB)]
    for k in ORDER:
        for slot in range(MB):
            queries[slot][k] = fetch(full[slot], slot, k, 2)

    keys, values, near_part, near_stat = near(mine, q, new_k, new_v, key_cache[0], value_cache[0])
    local = [far(table, others[slot], keys, values, 0, slot, 1) for slot in range(MB)]
    back = [[] for _ in range(MB)]
    for k in ORDER:
        for slot in range(MB):
            part = far(table, queries[slot][k], keys, values, k, slot, 0)
            back[slot].append(give(part, slot, k, 2))
    final = []
    for slot in range(MB):
        merged = first_merge(slot, near_part, near_stat, local[slot], back[slot])
        final.append(merged[0])
        for k in ORDER:
            final.append(give(merged[k], slot, k, 1))
    edited = last_merge(mine, final).reshape(8, MB * BLK // 8, WIDE)
    edited = lax.all_to_all(edited, "head", 0, 0, tiled=True)
    return join_heads(edited)[None]


def solution(mesh):
    placed = (
        P("frame", "head", None),
        P("frame", "head", None),
        P("frame", "head", None),
        P("frame", None, "head"),
        P("frame", None, "head"),
        P(),
        P(),
        P(),
    )
    return jax.shard_map(
        body, mesh=mesh, in_specs=placed, out_specs=P("frame", "head", None), check_vma=False
    )
```

```python
import functools
import math

import jax
import jax.numpy as jnp
from jax import lax
from jax.experimental import pallas as pl
from jax.experimental.pallas import tpu as pltpu
from jax.sharding import PartitionSpec as P

HD = 128
BLK = 128
NBLK = 28
MB = 2
CMAX = 3
HEADS = 5
WIDE = HEADS * HD
SIDE = 4
STAT = 16
PAY = SIDE * BLK + STAT
EXPO = math.log2(math.e) / math.sqrt(HD)
LOW = -1e30
VMEM_LIMIT = 16 * 1024 * 1024


def lanes(h):
    return slice(h * HD, (h + 1) * HD)


def params(**kw):
    return pltpu.CompilerParams(vmem_limit_bytes=VMEM_LIMIT, **kw)


def split_kernel(*refs):
    *sources, dst = refs
    for i, src in enumerate(sources):
        rows = src.shape[0]
        for j in range(8):
            dst[j, i * rows : (i + 1) * rows, :] = src[:, j * WIDE : (j + 1) * WIDE]


def split_heads(*arrays):
    rows = sum(a.shape[0] for a in arrays)
    return pl.pallas_call(
        split_kernel,
        out_shape=jax.ShapeDtypeStruct((8, rows, WIDE), jnp.bfloat16),
        compiler_params=params(),
        name="split_heads",
    )(*arrays)


def stack_kernel(*refs):
    *sources, dst = refs
    for i, src in enumerate(sources):
        dst[i * BLK : (i + 1) * BLK, :] = src[...]


def stack(*arrays):
    return pl.pallas_call(
        stack_kernel,
        out_shape=jax.ShapeDtypeStruct((len(arrays) * BLK, WIDE), jnp.bfloat16),
        compiler_params=params(),
        name="stack",
    )(*arrays)


def join_kernel(src, dst):
    for j in range(8):
        dst[:, j * WIDE : (j + 1) * WIDE] = src[j]


def join_heads(x):
    return pl.pallas_call(
        join_kernel,
        out_shape=jax.ShapeDtypeStruct((x.shape[1], 8 * WIDE), jnp.bfloat16),
        compiler_params=params(),
        name="join_heads",
    )(x)


def fold(x, op, groups):
    rows = x.shape[0] // groups
    out = x[:rows]
    for g in range(1, groups):
        out = op(out, x[g * rows : (g + 1) * rows])
    return out


def col_max(x, groups=8):
    return jnp.max(fold(x, jnp.maximum, groups), axis=0, keepdims=True)


def col_sum(x, groups=8):
    return jnp.sum(fold(x, jnp.add, groups), axis=0, keepdims=True)


NEAR_BLOCKS = 7
NEAR_ROWS = NEAR_BLOCKS * BLK


def eighths(x, op):
    out = x[:8]
    for g in range(1, x.shape[0] // 8):
        out = op(out, x[g * 8 : (g + 1) * 8])
    return out


def near_kernel(
    mine,
    q_ref,
    fresh_ref,
    kc_ref,
    vc_ref,
    k_out,
    vt_out,
    o_out,
    s_out,
    acc,
    top,
    tot,
    sbuf,
    pbuf,
    vbuf,
    k_sems,
    v_sems,
):
    pieces = NBLK // NEAR_BLOCKS

    def rows_of(p):
        return pl.ds(p * NEAR_ROWS, NEAR_ROWS)

    v_copies = [
        pltpu.make_async_copy(vc_ref.at[rows_of(p), :], vbuf.at[rows_of(p), :], v_sems.at[p])
        for p in range(pieces)
    ]
    k_copies = [
        pltpu.make_async_copy(kc_ref.at[rows_of(p), :], k_out.at[rows_of(p), :], k_sems.at[p])
        for p in range(pieces)
    ]
    for copy in v_copies + k_copies:
        copy.start()
    acc[...] = jnp.zeros_like(acc)
    top[...] = jnp.full_like(top, LOW)
    tot[...] = jnp.zeros_like(tot)
    for p in range(pieces):
        v_copies[p].wait()

        def turn(b, carry):
            span = pl.ds(pl.multiple_of(b * BLK, BLK), BLK)
            for h in range(HEADS):
                vt_out[b, lanes(h), :] = vbuf[span, lanes(h)].T
            return carry

        lax.fori_loop(p * NEAR_BLOCKS, (p + 1) * NEAR_BLOCKS, turn, 0)
    for copy in k_copies:
        copy.wait()
    part_rows = fresh_ref.shape[1] // 2
    parts = BLK // part_rows
    for s in range(MB):

        @pl.when(mine[MB] > s)
        def _():
            for i in range(parts):
                rows = pl.ds(pl.multiple_of(mine[s] * BLK + i * part_rows, part_rows), part_rows)
                k_out[rows, :] = fresh_ref[s * parts + i, :part_rows, :]
            for h in range(HEADS):
                tile = jnp.concatenate(
                    [fresh_ref[s * parts + i, part_rows:, lanes(h)] for i in range(parts)], axis=0
                )
                vt_out[mine[s], lanes(h), :] = tile.T

    def chunk(step, carry):
        def score(h):
            high = None
            for b in range(NEAR_BLOCKS):
                part = lax.dot_general(
                    k_out[pl.ds(pl.multiple_of((step * NEAR_BLOCKS + b) * BLK, BLK), BLK), lanes(h)],
                    q_ref[:, lanes(h)],
                    (((1,), (1,)), ((), ())),
                    preferred_element_type=jnp.float32,
                )
                sbuf[h % 2, b * BLK : (b + 1) * BLK, :] = part
                peak = eighths(part, jnp.maximum)
                high = peak if high is None else jnp.maximum(high, peak)
            return jnp.max(high, axis=0, keepdims=True)

        ahead = score(0)
        for h in range(HEADS):
            high = ahead
            if h + 1 < HEADS:
                ahead = score(h + 1)
            old = top[h : h + 1, :]
            new = jnp.maximum(old, high)
            shrink = jnp.exp2((old - new) * EXPO)
            top[h : h + 1, :] = new
            added = None
            for b in range(NEAR_BLOCKS):
                weights = jnp.exp2((sbuf[h % 2, b * BLK : (b + 1) * BLK, :] - new) * EXPO)
                pbuf[h % 2, b * BLK : (b + 1) * BLK, :] = weights.astype(jnp.bfloat16)
                part = eighths(weights, jnp.add)
                added = part if added is None else added + part
            tot[h : h + 1, :] = tot[h : h + 1, :] * shrink + jnp.sum(added, axis=0, keepdims=True)
            values = jnp.concatenate(
                [vt_out[step * NEAR_BLOCKS + b, lanes(h), :] for b in range(NEAR_BLOCKS)], axis=1
            )
            acc[h] = acc[h] * shrink + jnp.dot(
                values, pbuf[h % 2], preferred_element_type=jnp.float32
            )
        return carry

    lax.fori_loop(0, NBLK // NEAR_BLOCKS, chunk, 0)
    for h in range(HEADS):
        total = tot[h : h + 1, :]
        part = acc[h] * (1.0 / total)
        level = top[h : h + 1, :] * EXPO + jnp.log2(total)
        for s in range(MB):
            o_out[s, :, lanes(h)] = part[:, s * BLK : (s + 1) * BLK].astype(jnp.bfloat16)
            s_out[s : s + 1, lanes(h)] = level[:, s * BLK : (s + 1) * BLK]


def near(mine, q, fresh, key_cache, value_cache):
    rows = MB * BLK
    vmem = pl.BlockSpec(memory_space=pltpu.VMEM)
    hbm = pl.BlockSpec(memory_space=pltpu.HBM)
    pieces = NBLK // NEAR_BLOCKS
    return pl.pallas_call(
        near_kernel,
        in_specs=[pl.BlockSpec(memory_space=pltpu.SMEM), vmem, vmem, hbm, hbm],
        out_specs=[vmem] * 4,
        scratch_shapes=[
            pltpu.VMEM((HEADS, HD, rows), jnp.float32),
            pltpu.VMEM((8, rows), jnp.float32),
            pltpu.VMEM((8, rows), jnp.float32),
            pltpu.VMEM((2, NEAR_ROWS, rows), jnp.float32),
            pltpu.VMEM((2, NEAR_ROWS, rows), jnp.bfloat16),
            pltpu.VMEM((NBLK * BLK, WIDE), jnp.bfloat16),
            pltpu.SemaphoreType.DMA((pieces,)),
            pltpu.SemaphoreType.DMA((pieces,)),
        ],
        out_shape=[
            jax.ShapeDtypeStruct((NBLK * BLK, WIDE), jnp.bfloat16),
            jax.ShapeDtypeStruct((NBLK, WIDE, BLK), jnp.bfloat16),
            jax.ShapeDtypeStruct((MB, HD, WIDE), jnp.bfloat16),
            jax.ShapeDtypeStruct((8, WIDE), jnp.float32),
        ],
        compiler_params=pltpu.CompilerParams(vmem_limit_bytes=46 * 1024 * 1024),
        cost_estimate=pl.CostEstimate(
            flops=4 * rows * NBLK * BLK * WIDE * 4, bytes_accessed=10_000_000, transcendentals=4_600_000
        ),
        name="near",
    )(mine, q, fresh, key_cache, value_cache)


def put_stats(stat, index, h, level):
    high = level.astype(jnp.bfloat16).astype(jnp.float32)
    rest = level - high
    mid = rest.astype(jnp.bfloat16).astype(jnp.float32)
    row = lax.broadcasted_iota(jnp.int32, (STAT, HD), 0) - index
    tile = stat[:, lanes(h)]
    for place, piece in ((0, high), (SIDE, mid), (2 * SIDE, rest - mid)):
        tile = jnp.where(row == place, piece, tile)
    stat[:, lanes(h)] = tile


def frame_at(me, item, slot, shift):
    z, x = me // SIDE, me % SIDE
    if slot == 0:
        z, x = (z + shift) % SIDE, (x + item) % SIDE
    else:
        z, x = (z + item) % SIDE, (x + shift) % SIDE
    return z * SIDE + x


def far_kernel(groups, first, seen, alive, *refs):
    n_groups = len(groups)
    queries, (keys, values) = refs[:n_groups], refs[n_groups : n_groups + 2]
    outs, stats = refs[n_groups + 2 : 2 * n_groups + 2], refs[2 * n_groups + 2 :]
    me = alive[SIDE * SIDE]
    for (slot, shift, skip), q_ref, out, stat in zip(groups, queries, outs, stats):
        stat[...] = jnp.zeros_like(stat)

        def step(i, carry):
            frame = frame_at(me, i + skip, slot, shift)
            count = jnp.where(alive[frame] > slot, seen[frame], 0)
            spots = [first[frame * MB + slot] + j for j in range(CMAX)]
            spots = [jnp.where(spot >= NBLK, spot - NBLK, spot) for spot in spots]
            rows = pl.ds(pl.multiple_of((i + skip) * BLK, BLK), BLK)
            for n in range(1, CMAX + 1):

                @pl.when(count == n)
                def _():
                    def score(h):
                        return [
                            lax.dot_general(
                                keys[pl.ds(pl.multiple_of(spots[j] * BLK, BLK), BLK), lanes(h)],
                                q_ref[rows, lanes(h)],
                                (((1,), (1,)), ((), ())),
                                preferred_element_type=jnp.float32,
                            )
                            for j in range(n)
                        ]

                    scores = [score(h) for h in range(HEADS)]
                    tops, totals, probs = [], [], []
                    for h in range(HEADS):
                        peaks = [eighths(x, jnp.maximum) for x in scores[h]]
                        top = jnp.max(functools.reduce(jnp.maximum, peaks), axis=0, keepdims=True)
                        weights = [jnp.exp2((x - top) * EXPO) for x in scores[h]]
                        sums = [eighths(x, jnp.add) for x in weights]
                        totals.append(jnp.sum(functools.reduce(jnp.add, sums), axis=0, keepdims=True))
                        tops.append(top)
                        probs.append(jnp.concatenate([x.astype(jnp.bfloat16) for x in weights], axis=0))
                    parts = [
                        jnp.dot(
                            jnp.concatenate([values[spots[j], lanes(h), :] for j in range(n)], axis=1),
                            probs[h],
                            preferred_element_type=jnp.float32,
                        )
                        for h in range(HEADS)
                    ]
                    for h in range(HEADS):
                        out[rows, lanes(h)] = (parts[h] * (1.0 / totals[h])).astype(jnp.bfloat16)
                        put_stats(stat, i + skip, h, tops[h] * EXPO + jnp.log2(totals[h]))

            return carry

        lax.fori_loop(0, SIDE - skip, step, 0)
        out[SIDE * BLK :, :] = stat[...].astype(jnp.bfloat16)


def far(table, queries, keys, values, groups):
    items = sum(SIDE - skip for _, _, skip in groups)
    smem = pl.BlockSpec(memory_space=pltpu.SMEM)
    vmem = pl.BlockSpec(memory_space=pltpu.VMEM)
    return pl.pallas_call(
        functools.partial(far_kernel, groups),
        in_specs=[smem] * 3 + [vmem] * (len(groups) + 2),
        out_specs=[vmem] * len(groups),
        scratch_shapes=[pltpu.VMEM((STAT, WIDE), jnp.float32)] * len(groups),
        out_shape=[jax.ShapeDtypeStruct((PAY, WIDE), jnp.bfloat16)] * len(groups),
        compiler_params=params(),
        cost_estimate=pl.CostEstimate(
            flops=4 * items * BLK * CMAX * BLK * WIDE * 4,
            bytes_accessed=items * 4 * CMAX * BLK * WIDE,
            transcendentals=items * BLK * CMAX * BLK * HEADS,
        ),
        name="far",
    )(*table, *queries, keys, values)


def read_level(ref, base, index):
    tile = ref[base : base + STAT, :].astype(jnp.float32)
    return (
        tile[index : index + 1]
        + tile[SIDE + index : SIDE + index + 1]
        + tile[2 * SIDE + index : 2 * SIDE + index + 1]
    )


def merge(levels, parts):
    top = functools.reduce(jnp.maximum, levels)
    shares = [jnp.exp2(level - top) for level in levels]
    total = functools.reduce(jnp.add, shares)
    scale = 1.0 / total
    out = None
    for share, part in zip(shares, parts):
        term = part() * (share * scale)
        out = term if out is None else out + term
    return out, top + jnp.log2(total)


def first_merge_kernel(slot, near_ref, near_stat, local, one, two, three, *outs):
    *outs, stat = outs
    for d in range(SIDE):
        sources = [one, two, three]
        levels = [read_level(r, SIDE * BLK, d) for r in sources]
        parts = [
            functools.partial(lambda r: r[d * BLK : (d + 1) * BLK, :].astype(jnp.float32), r)
            for r in sources
        ]
        if d == 0:
            levels.append(near_stat[slot : slot + 1, :])
            parts.append(lambda: near_ref[slot].astype(jnp.float32))
        else:
            levels.append(read_level(local, SIDE * BLK, d))
            parts.append(lambda: local[d * BLK : (d + 1) * BLK, :].astype(jnp.float32))
        value, level = merge(levels, parts)
        outs[d][:BLK, :] = value.astype(jnp.bfloat16)
        stat[...] = jnp.zeros_like(stat)
        for h in range(HEADS):
            put_stats(stat, 0, h, level[:, lanes(h)])
        outs[d][BLK:, :] = stat[...].astype(jnp.bfloat16)


def first_merge(slot, near_part, near_stat, local, received):
    return pl.pallas_call(
        functools.partial(first_merge_kernel, slot),
        out_shape=[jax.ShapeDtypeStruct((BLK + STAT, WIDE), jnp.bfloat16)] * SIDE,
        scratch_shapes=[pltpu.VMEM((STAT, WIDE), jnp.float32)],
        compiler_params=params(),
        cost_estimate=pl.CostEstimate(flops=8_000_000, bytes_accessed=3_500_000, transcendentals=0),
        name="first_merge",
    )(near_part, near_stat, local, *received)


def last_merge_kernel(mine, *refs):
    *refs, out = refs
    for slot in range(MB):
        sources = refs[slot * SIDE : (slot + 1) * SIDE]
        live = mine[MB] > slot

        @pl.when(live)
        def _():
            levels = [read_level(r, BLK, 0) for r in sources]
            parts = [
                functools.partial(lambda r: r[:BLK, :].astype(jnp.float32), r) for r in sources
            ]
            value, _ = merge(levels, parts)
            for h in range(HEADS):
                out[slot * BLK : (slot + 1) * BLK, lanes(h)] = value[:, lanes(h)].T.astype(jnp.bfloat16)

        @pl.when(jnp.logical_not(live))
        def _():
            out[slot * BLK : (slot + 1) * BLK, :] = jnp.zeros((BLK, WIDE), jnp.bfloat16)


def last_merge(mine, parts):
    vmem = pl.BlockSpec(memory_space=pltpu.VMEM)
    return pl.pallas_call(
        last_merge_kernel,
        in_specs=[pl.BlockSpec(memory_space=pltpu.SMEM)] + [vmem] * len(parts),
        out_specs=vmem,
        out_shape=jax.ShapeDtypeStruct((MB * BLK, WIDE), jnp.bfloat16),
        compiler_params=params(),
        name="last_merge",
    )(mine, *parts)


def shift_to(x, dz, dx):
    pairs = [
        (z * SIDE + c, ((z + dz) % SIDE) * SIDE + (c + dx) % SIDE)
        for z in range(SIDE)
        for c in range(SIDE)
    ]
    return lax.ppermute(x, "frame", pairs)


def fetch(x, slot, k, step):
    along_x = (slot == 0) == (step == 1)
    return shift_to(x, 0, -k) if along_x else shift_to(x, -k, 0)


def give(x, slot, k, step):
    along_x = (slot == 0) == (step == 1)
    return shift_to(x, 0, k) if along_x else shift_to(x, k, 0)


ORDER = (1, 3, 2)


def body(
    fresh_queries,
    fresh_keys,
    fresh_values,
    key_cache,
    value_cache,
    masked_blocks,
    masked_count,
    radial_counts,
):
    me = lax.axis_index("frame").astype(jnp.int32)
    frames = jnp.arange(SIDE * SIDE, dtype=jnp.int32)
    spread = jnp.maximum(jnp.abs(frames - me) - 1, 0)
    seen = jnp.sum(
        jnp.where(spread[:, None] == jnp.arange(radial_counts.shape[0]), radial_counts, 0), axis=1
    ).astype(jnp.int32)
    first = jnp.mod(masked_blocks - (seen // 2)[:, None], NBLK).reshape(-1).astype(jnp.int32)
    alive = jnp.concatenate([masked_count, me[None]])
    table = (first, seen, alive)
    mine = jnp.concatenate(
        [
            lax.dynamic_index_in_dim(masked_blocks, me, 0, keepdims=False),
            lax.dynamic_index_in_dim(masked_count, me, 0),
        ]
    )

    q_split = split_heads(fresh_queries[0])
    q = lax.all_to_all(q_split, "head", 0, 0, tiled=True).reshape(MB * BLK, WIDE)
    fresh = lax.all_to_all(
        split_heads(fresh_keys[0], fresh_values[0]), "head", 0, 0, tiled=True
    )
    halves = [q[:BLK], q[BLK:]]
    ring = [[halves[slot]] + [None] * (SIDE - 1) for slot in range(MB)]
    for k in ORDER:
        for slot in range(MB):
            ring[slot][k] = fetch(halves[slot], slot, k, 1)
    full = [stack(*ring[slot]) for slot in range(MB)]
    queries = [[None] * SIDE for _ in range(MB)]
    for k in ORDER:
        for slot in range(MB):
            queries[slot][k] = fetch(full[slot], slot, k, 2)

    keys, values, near_part, near_stat = near(mine, q, fresh, key_cache[0], value_cache[0])
    local = far(table, full, keys, values, ((0, 0, 1), (1, 0, 1)))
    back = [[] for _ in range(MB)]
    for k in ORDER:
        for slot in range(MB):
            (part,) = far(table, [queries[slot][k]], keys, values, ((slot, k, 0),))
            back[slot].append(give(part, slot, k, 2))
    final = []
    for slot in range(MB):
        merged = first_merge(slot, near_part, near_stat, local[slot], back[slot])
        final.append(merged[0])
        for k in ORDER:
            final.append(give(merged[k], slot, k, 1))
    edited = last_merge(mine, final).reshape(8, MB * BLK // 8, WIDE)
    edited = lax.all_to_all(edited, "head", 0, 0, tiled=True)
    return join_heads(edited)[None]


def solution(mesh):
    placed = (
        P("frame", "head", None),
        P("frame", "head", None),
        P("frame", "head", None),
        P("frame", None, "head"),
        P("frame", None, "head"),
        P(),
        P(),
        P(),
    )
    return jax.shard_map(
        body, mesh=mesh, in_specs=placed, out_specs=P("frame", "head", None), check_vma=False
    )
```

```python
import functools
import math

import jax
import jax.numpy as jnp
from jax import lax
from jax.experimental import pallas as pl
from jax.experimental.pallas import tpu as pltpu
from jax.sharding import PartitionSpec as P

HD = 128
BLK = 128
NBLK = 28
MB = 2
CMAX = 3
HEADS = 5
WIDE = HEADS * HD
SIDE = 4
STAT = 16
PAY = SIDE * BLK + STAT
EXPO = math.log2(math.e) / math.sqrt(HD)
LOW = -1e30
FRAMES = SIDE * SIDE
COUNTS = FRAMES * MB
RADIAL = COUNTS + FRAMES
ME = RADIAL + FRAMES - 1
VMEM_LIMIT = 16 * 1024 * 1024


def lanes(h):
    return slice(h * HD, (h + 1) * HD)


def params(**kw):
    return pltpu.CompilerParams(vmem_limit_bytes=VMEM_LIMIT, **kw)


def split_kernel(*refs):
    *sources, dst = refs
    for i, src in enumerate(sources):
        rows = src.shape[0]
        for j in range(8):
            dst[j, i * rows : (i + 1) * rows, :] = src[:, j * WIDE : (j + 1) * WIDE]


def split_heads(*arrays):
    rows = sum(a.shape[0] for a in arrays)
    return pl.pallas_call(
        split_kernel,
        out_shape=jax.ShapeDtypeStruct((8, rows, WIDE), jnp.bfloat16),
        compiler_params=params(),
        name="split_heads",
    )(*arrays)


def stack_kernel(*refs):
    *sources, dst = refs
    for i, src in enumerate(sources):
        dst[i * BLK : (i + 1) * BLK, :] = src[...]


def stack(*arrays):
    return pl.pallas_call(
        stack_kernel,
        out_shape=jax.ShapeDtypeStruct((len(arrays) * BLK, WIDE), jnp.bfloat16),
        compiler_params=params(),
        name="stack",
    )(*arrays)


def join_kernel(src, dst):
    for j in range(8):
        dst[:, j * WIDE : (j + 1) * WIDE] = src[j]


def join_heads(x):
    return pl.pallas_call(
        join_kernel,
        out_shape=jax.ShapeDtypeStruct((x.shape[1], 8 * WIDE), jnp.bfloat16),
        compiler_params=params(),
        name="join_heads",
    )(x)


def fold(x, op, groups):
    rows = x.shape[0] // groups
    out = x[:rows]
    for g in range(1, groups):
        out = op(out, x[g * rows : (g + 1) * rows])
    return out


def col_max(x, groups=8):
    return jnp.max(fold(x, jnp.maximum, groups), axis=0, keepdims=True)


def col_sum(x, groups=8):
    return jnp.sum(fold(x, jnp.add, groups), axis=0, keepdims=True)


NEAR_BLOCKS = 7
NEAR_ROWS = NEAR_BLOCKS * BLK


def eighths(x, op):
    out = x[:8]
    for g in range(1, x.shape[0] // 8):
        out = op(out, x[g * 8 : (g + 1) * 8])
    return out


def near_kernel(
    table,
    q_ref,
    fresh_ref,
    kc_ref,
    vc_ref,
    k_out,
    vt_out,
    o_out,
    s_out,
    acc,
    top,
    tot,
    sbuf,
    pbuf,
    vbuf,
    k_sems,
    v_sems,
):
    pieces = NBLK // NEAR_BLOCKS

    def rows_of(p):
        return pl.ds(p * NEAR_ROWS, NEAR_ROWS)

    v_copies = [
        pltpu.make_async_copy(vc_ref.at[rows_of(p), :], vbuf.at[rows_of(p), :], v_sems.at[p])
        for p in range(pieces)
    ]
    k_copies = [
        pltpu.make_async_copy(kc_ref.at[rows_of(p), :], k_out.at[rows_of(p), :], k_sems.at[p])
        for p in range(pieces)
    ]
    for p in range(pieces):
        k_copies[p].start()
        v_copies[p].start()
    acc[...] = jnp.zeros_like(acc)
    top[...] = jnp.full_like(top, LOW)
    tot[...] = jnp.zeros_like(tot)
    part_rows = fresh_ref.shape[1] // 2
    parts = BLK // part_rows
    me = table[ME]

    def chunk(step, carry):
        span = pl.ds(pl.multiple_of(step * NEAR_ROWS, NEAR_ROWS), NEAR_ROWS)
        pltpu.make_async_copy(vc_ref.at[span, :], vbuf.at[span, :], v_sems.at[step]).wait()
        pltpu.make_async_copy(kc_ref.at[span, :], k_out.at[span, :], k_sems.at[step]).wait()
        for s in range(MB):
            spot = table[me * MB + s]
            here = (spot >= step * NEAR_BLOCKS) & (spot < (step + 1) * NEAR_BLOCKS)

            @pl.when(here & (table[COUNTS + me] > s))
            def _():
                for i in range(parts):
                    rows = pl.ds(pl.multiple_of(spot * BLK + i * part_rows, part_rows), part_rows)
                    k_out[rows, :] = fresh_ref[s * parts + i, :part_rows, :]
                    vbuf[rows, :] = fresh_ref[s * parts + i, part_rows:, :]

        def score(h):
            high = None
            for b in range(NEAR_BLOCKS):
                part = lax.dot_general(
                    k_out[pl.ds(pl.multiple_of((step * NEAR_BLOCKS + b) * BLK, BLK), BLK), lanes(h)],
                    q_ref[:, lanes(h)],
                    (((1,), (1,)), ((), ())),
                    preferred_element_type=jnp.float32,
                )
                sbuf[h % 2, b * BLK : (b + 1) * BLK, :] = part
                peak = eighths(part, jnp.maximum)
                high = peak if high is None else jnp.maximum(high, peak)
            return jnp.max(high, axis=0, keepdims=True)

        ahead = score(0)
        for h in range(HEADS):
            high = ahead
            if h + 1 < HEADS:
                ahead = score(h + 1)
            old = top[h : h + 1, :]
            new = jnp.maximum(old, high)
            shrink = jnp.exp2((old - new) * EXPO)
            top[h : h + 1, :] = new
            added = None
            for b in range(NEAR_BLOCKS):
                weights = jnp.exp2((sbuf[h % 2, b * BLK : (b + 1) * BLK, :] - new) * EXPO)
                pbuf[h % 2, b * BLK : (b + 1) * BLK, :] = weights.astype(jnp.bfloat16)
                part = eighths(weights, jnp.add)
                added = part if added is None else added + part
            tot[h : h + 1, :] = tot[h : h + 1, :] * shrink + jnp.sum(added, axis=0, keepdims=True)
            turned = [
                vbuf[
                    pl.ds(pl.multiple_of((step * NEAR_BLOCKS + b) * BLK, BLK), BLK), lanes(h)
                ].T
                for b in range(NEAR_BLOCKS)
            ]
            for b in range(NEAR_BLOCKS):
                vt_out[step * NEAR_BLOCKS + b, lanes(h), :] = turned[b]
            values = jnp.concatenate(turned, axis=1)
            acc[h] = acc[h] * shrink + jnp.dot(
                values, pbuf[h % 2], preferred_element_type=jnp.float32
            )
        return carry

    lax.fori_loop(0, NBLK // NEAR_BLOCKS, chunk, 0)
    for h in range(HEADS):
        total = tot[h : h + 1, :]
        part = acc[h] * (1.0 / total)
        level = top[h : h + 1, :] * EXPO + jnp.log2(total)
        for s in range(MB):
            o_out[s, :, lanes(h)] = part[:, s * BLK : (s + 1) * BLK].astype(jnp.bfloat16)
            s_out[s : s + 1, lanes(h)] = level[:, s * BLK : (s + 1) * BLK]


def near(table, q, fresh, key_cache, value_cache):
    rows = MB * BLK
    vmem = pl.BlockSpec(memory_space=pltpu.VMEM)
    hbm = pl.BlockSpec(memory_space=pltpu.HBM)
    pieces = NBLK // NEAR_BLOCKS
    return pl.pallas_call(
        near_kernel,
        in_specs=[pl.BlockSpec(memory_space=pltpu.SMEM), vmem, vmem, hbm, hbm],
        out_specs=[vmem] * 4,
        scratch_shapes=[
            pltpu.VMEM((HEADS, HD, rows), jnp.float32),
            pltpu.VMEM((8, rows), jnp.float32),
            pltpu.VMEM((8, rows), jnp.float32),
            pltpu.VMEM((2, NEAR_ROWS, rows), jnp.float32),
            pltpu.VMEM((2, NEAR_ROWS, rows), jnp.bfloat16),
            pltpu.VMEM((NBLK * BLK, WIDE), jnp.bfloat16),
            pltpu.SemaphoreType.DMA((pieces,)),
            pltpu.SemaphoreType.DMA((pieces,)),
        ],
        out_shape=[
            jax.ShapeDtypeStruct((NBLK * BLK, WIDE), jnp.bfloat16),
            jax.ShapeDtypeStruct((NBLK, WIDE, BLK), jnp.bfloat16),
            jax.ShapeDtypeStruct((MB, HD, WIDE), jnp.bfloat16),
            jax.ShapeDtypeStruct((8, WIDE), jnp.float32),
        ],
        compiler_params=pltpu.CompilerParams(vmem_limit_bytes=44 * 1024 * 1024),
        cost_estimate=pl.CostEstimate(
            flops=4 * rows * NBLK * BLK * WIDE * 4, bytes_accessed=10_000_000, transcendentals=4_600_000
        ),
        name="near",
    )(table, q, fresh, key_cache, value_cache)


def put_stats(stat, index, h, level):
    high = level.astype(jnp.bfloat16).astype(jnp.float32)
    rest = level - high
    mid = rest.astype(jnp.bfloat16).astype(jnp.float32)
    row = lax.broadcasted_iota(jnp.int32, (STAT, HD), 0) - index
    tile = stat[:, lanes(h)]
    for place, piece in ((0, high), (SIDE, mid), (2 * SIDE, rest - mid)):
        tile = jnp.where(row == place, piece, tile)
    stat[:, lanes(h)] = tile


def frame_at(me, item, slot, shift):
    z, x = me // SIDE, me % SIDE
    if slot == 0:
        z, x = (z + shift) % SIDE, (x + item) % SIDE
    else:
        z, x = (z + item) % SIDE, (x + shift) % SIDE
    return z * SIDE + x


def far_kernel(groups, table, *refs):
    n_groups = len(groups)
    queries, (keys, values) = refs[:n_groups], refs[n_groups : n_groups + 2]
    outs, stats = refs[n_groups + 2 : 2 * n_groups + 2], refs[2 * n_groups + 2 :]
    me = table[ME]
    for (slot, shift, skip), q_ref, out, stat in zip(groups, queries, outs, stats):
        stat[...] = jnp.zeros_like(stat)

        def step(i, carry):
            frame = frame_at(me, i + skip, slot, shift)
            count = table[RADIAL + jnp.maximum(jnp.abs(frame - me) - 1, 0)]
            start = table[frame * MB + slot] - lax.shift_right_logical(count, 1)
            start = jnp.where(start < 0, start + NBLK, start)
            spots = [start + j for j in range(CMAX)]
            spots = [jnp.where(spot >= NBLK, spot - NBLK, spot) for spot in spots]
            count = jnp.where(table[COUNTS + frame] > slot, count, 0)
            rows = pl.ds(pl.multiple_of((i + skip) * BLK, BLK), BLK)
            for n in range(1, CMAX + 1):

                @pl.when(count == n)
                def _():
                    def score(h):
                        return [
                            lax.dot_general(
                                keys[pl.ds(pl.multiple_of(spots[j] * BLK, BLK), BLK), lanes(h)],
                                q_ref[rows, lanes(h)],
                                (((1,), (1,)), ((), ())),
                                preferred_element_type=jnp.float32,
                            )
                            for j in range(n)
                        ]

                    scores = [score(h) for h in range(HEADS)]
                    tops, totals, probs = [], [], []
                    for h in range(HEADS):
                        peaks = [eighths(x, jnp.maximum) for x in scores[h]]
                        top = jnp.max(functools.reduce(jnp.maximum, peaks), axis=0, keepdims=True)
                        weights = [jnp.exp2((x - top) * EXPO) for x in scores[h]]
                        sums = [eighths(x, jnp.add) for x in weights]
                        totals.append(jnp.sum(functools.reduce(jnp.add, sums), axis=0, keepdims=True))
                        tops.append(top)
                        probs.append(jnp.concatenate([x.astype(jnp.bfloat16) for x in weights], axis=0))
                    parts = [
                        jnp.dot(
                            jnp.concatenate([values[spots[j], lanes(h), :] for j in range(n)], axis=1),
                            probs[h],
                            preferred_element_type=jnp.float32,
                        )
                        for h in range(HEADS)
                    ]
                    for h in range(HEADS):
                        out[rows, lanes(h)] = (parts[h] * (1.0 / totals[h])).astype(jnp.bfloat16)
                        put_stats(stat, i + skip, h, tops[h] * EXPO + jnp.log2(totals[h]))

            return carry

        lax.fori_loop(0, SIDE - skip, step, 0)
        out[SIDE * BLK :, :] = stat[...].astype(jnp.bfloat16)


def far(table, queries, keys, values, groups):
    items = sum(SIDE - skip for _, _, skip in groups)
    smem = pl.BlockSpec(memory_space=pltpu.SMEM)
    vmem = pl.BlockSpec(memory_space=pltpu.VMEM)
    return pl.pallas_call(
        functools.partial(far_kernel, groups),
        in_specs=[smem] + [vmem] * (len(groups) + 2),
        out_specs=[vmem] * len(groups),
        scratch_shapes=[pltpu.VMEM((STAT, WIDE), jnp.float32)] * len(groups),
        out_shape=[jax.ShapeDtypeStruct((PAY, WIDE), jnp.bfloat16)] * len(groups),
        compiler_params=params(),
        cost_estimate=pl.CostEstimate(
            flops=4 * items * BLK * CMAX * BLK * WIDE * 4,
            bytes_accessed=items * 4 * CMAX * BLK * WIDE,
            transcendentals=items * BLK * CMAX * BLK * HEADS,
        ),
        name="far",
    )(table, *queries, keys, values)


def read_level(ref, base, index):
    tile = ref[base : base + STAT, :].astype(jnp.float32)
    return (
        tile[index : index + 1]
        + tile[SIDE + index : SIDE + index + 1]
        + tile[2 * SIDE + index : 2 * SIDE + index + 1]
    )


def merge(levels, parts):
    top = functools.reduce(jnp.maximum, levels)
    shares = [jnp.exp2(level - top) for level in levels]
    total = functools.reduce(jnp.add, shares)
    scale = 1.0 / total
    out = None
    for share, part in zip(shares, parts):
        term = part() * (share * scale)
        out = term if out is None else out + term
    return out, top + jnp.log2(total)


def first_merge_kernel(slot, near_ref, near_stat, local, one, two, three, *outs):
    *outs, stat = outs
    for d in range(SIDE):
        sources = [one, two, three]
        levels = [read_level(r, SIDE * BLK, d) for r in sources]
        parts = [
            functools.partial(lambda r: r[d * BLK : (d + 1) * BLK, :].astype(jnp.float32), r)
            for r in sources
        ]
        if d == 0:
            levels.append(near_stat[slot : slot + 1, :])
            parts.append(lambda: near_ref[slot].astype(jnp.float32))
        else:
            levels.append(read_level(local, SIDE * BLK, d))
            parts.append(lambda: local[d * BLK : (d + 1) * BLK, :].astype(jnp.float32))
        value, level = merge(levels, parts)
        outs[d][:BLK, :] = value.astype(jnp.bfloat16)
        stat[...] = jnp.zeros_like(stat)
        for h in range(HEADS):
            put_stats(stat, 0, h, level[:, lanes(h)])
        outs[d][BLK:, :] = stat[...].astype(jnp.bfloat16)


def first_merge(slot, near_part, near_stat, local, received):
    return pl.pallas_call(
        functools.partial(first_merge_kernel, slot),
        out_shape=[jax.ShapeDtypeStruct((BLK + STAT, WIDE), jnp.bfloat16)] * SIDE,
        scratch_shapes=[pltpu.VMEM((STAT, WIDE), jnp.float32)],
        compiler_params=params(),
        cost_estimate=pl.CostEstimate(flops=8_000_000, bytes_accessed=3_500_000, transcendentals=0),
        name="first_merge",
    )(near_part, near_stat, local, *received)


def last_merge_kernel(table, *refs):
    *refs, out = refs
    for slot in range(MB):
        sources = refs[slot * SIDE : (slot + 1) * SIDE]
        live = table[COUNTS + table[ME]] > slot

        @pl.when(live)
        def _():
            levels = [read_level(r, BLK, 0) for r in sources]
            parts = [
                functools.partial(lambda r: r[:BLK, :].astype(jnp.float32), r) for r in sources
            ]
            value, _ = merge(levels, parts)
            for h in range(HEADS):
                out[slot * BLK : (slot + 1) * BLK, lanes(h)] = value[:, lanes(h)].T.astype(jnp.bfloat16)

        @pl.when(jnp.logical_not(live))
        def _():
            out[slot * BLK : (slot + 1) * BLK, :] = jnp.zeros((BLK, WIDE), jnp.bfloat16)


def last_merge(table, parts):
    vmem = pl.BlockSpec(memory_space=pltpu.VMEM)
    return pl.pallas_call(
        last_merge_kernel,
        in_specs=[pl.BlockSpec(memory_space=pltpu.SMEM)] + [vmem] * len(parts),
        out_specs=vmem,
        out_shape=jax.ShapeDtypeStruct((MB * BLK, WIDE), jnp.bfloat16),
        compiler_params=params(),
        name="last_merge",
    )(table, *parts)


def shift_to(x, dz, dx):
    pairs = [
        (z * SIDE + c, ((z + dz) % SIDE) * SIDE + (c + dx) % SIDE)
        for z in range(SIDE)
        for c in range(SIDE)
    ]
    return lax.ppermute(x, "frame", pairs)


def fetch(x, slot, k, step):
    along_x = (slot == 0) == (step == 1)
    return shift_to(x, 0, -k) if along_x else shift_to(x, -k, 0)


def give(x, slot, k, step):
    along_x = (slot == 0) == (step == 1)
    return shift_to(x, 0, k) if along_x else shift_to(x, k, 0)


ORDER = (1, 3, 2)


def body(
    fresh_queries,
    fresh_keys,
    fresh_values,
    key_cache,
    value_cache,
    masked_blocks,
    masked_count,
    radial_counts,
):
    me = lax.axis_index("frame").astype(jnp.int32)
    table = jnp.concatenate([masked_blocks.reshape(-1), masked_count, radial_counts, me[None]])
    q_split = split_heads(fresh_queries[0])
    q = lax.all_to_all(q_split, "head", 0, 0, tiled=True).reshape(MB * BLK, WIDE)
    fresh = lax.all_to_all(
        split_heads(fresh_keys[0], fresh_values[0]), "head", 0, 0, tiled=True
    )
    halves = [q[:BLK], q[BLK:]]
    ring = [[halves[slot]] + [None] * (SIDE - 1) for slot in range(MB)]
    for k in ORDER:
        for slot in range(MB):
            ring[slot][k] = fetch(halves[slot], slot, k, 1)
    full = [stack(*ring[slot]) for slot in range(MB)]
    queries = [[None] * SIDE for _ in range(MB)]
    for k in ORDER[:2]:
        for slot in range(MB):
            queries[slot][k] = fetch(full[slot], slot, k, 2)
    keys, values, near_part, near_stat = near(table, q, fresh, key_cache[0], value_cache[0])
    *late, near_stat = lax.optimization_barrier((*full, near_stat))
    for slot in range(MB):
        queries[slot][2] = fetch(late[slot], slot, 2, 2)
    local = far(table, full, keys, values, ((0, 0, 1), (1, 0, 1)))
    back = [[] for _ in range(MB)]
    for k in ORDER:
        for slot in range(MB):
            (part,) = far(table, [queries[slot][k]], keys, values, ((slot, k, 0),))
            back[slot].append(give(part, slot, k, 2))
    final = []
    for slot in range(MB):
        merged = first_merge(slot, near_part, near_stat, local[slot], back[slot])
        final.append(merged[0])
        for k in ORDER:
            final.append(give(merged[k], slot, k, 1))
    edited = last_merge(table, final).reshape(8, MB * BLK // 8, WIDE)
    edited = lax.all_to_all(edited, "head", 0, 0, tiled=True)
    return join_heads(edited)[None]


def solution(mesh):
    placed = (
        P("frame", "head", None),
        P("frame", "head", None),
        P("frame", "head", None),
        P("frame", None, "head"),
        P("frame", None, "head"),
        P(),
        P(),
        P(),
    )
    return jax.shard_map(
        body, mesh=mesh, in_specs=placed, out_specs=P("frame", "head", None), check_vma=False
    )
```

```python
import functools
import math

import jax
import jax.numpy as jnp
from jax import lax
from jax.experimental import pallas as pl
from jax.experimental.pallas import tpu as pltpu
from jax.sharding import PartitionSpec as P

HD = 128
BLK = 128
NBLK = 28
MB = 2
CMAX = 3
HEADS = 5
WIDE = HEADS * HD
SIDE = 4
STAT = 16
PAY = SIDE * BLK + STAT
EXPO = math.log2(math.e) / math.sqrt(HD)
LOW = -1e30
FRAMES = SIDE * SIDE
COUNTS = FRAMES * MB
RADIAL = COUNTS + FRAMES
ME = RADIAL + FRAMES - 1
VMEM_LIMIT = 16 * 1024 * 1024
STAGE_LIMIT = 42 * 1024 * 1024


def lanes(h):
    return slice(h * HD, (h + 1) * HD)


def params(**kw):
    return pltpu.CompilerParams(vmem_limit_bytes=VMEM_LIMIT, **kw)


def split_kernel(*refs):
    *sources, dst = refs
    for i, src in enumerate(sources):
        rows = src.shape[0]
        for j in range(8):
            dst[j, i * rows : (i + 1) * rows, :] = src[:, j * WIDE : (j + 1) * WIDE]


def split_heads(*arrays):
    rows = sum(a.shape[0] for a in arrays)
    return pl.pallas_call(
        split_kernel,
        out_shape=jax.ShapeDtypeStruct((8, rows, WIDE), jnp.bfloat16),
        compiler_params=params(),
        name="split_heads",
    )(*arrays)


def stack_kernel(*refs):
    *sources, dst = refs
    for i, src in enumerate(sources):
        dst[i * BLK : (i + 1) * BLK, :] = src[...]


def stack(*arrays):
    return pl.pallas_call(
        stack_kernel,
        out_shape=jax.ShapeDtypeStruct((len(arrays) * BLK, WIDE), jnp.bfloat16),
        compiler_params=params(),
        name="stack",
    )(*arrays)


def join_kernel(src, dst):
    for j in range(8):
        dst[:, j * WIDE : (j + 1) * WIDE] = src[j]


def join_heads(x):
    return pl.pallas_call(
        join_kernel,
        out_shape=jax.ShapeDtypeStruct((x.shape[1], 8 * WIDE), jnp.bfloat16),
        compiler_params=params(),
        name="join_heads",
    )(x)


def fold(x, op, groups):
    rows = x.shape[0] // groups
    out = x[:rows]
    for g in range(1, groups):
        out = op(out, x[g * rows : (g + 1) * rows])
    return out


def col_max(x, groups=8):
    return jnp.max(fold(x, jnp.maximum, groups), axis=0, keepdims=True)


def col_sum(x, groups=8):
    return jnp.sum(fold(x, jnp.add, groups), axis=0, keepdims=True)


NEAR_BLOCKS = 7
NEAR_ROWS = NEAR_BLOCKS * BLK


def eighths(x, op):
    out = x[:8]
    for g in range(1, x.shape[0] // 8):
        out = op(out, x[g * 8 : (g + 1) * 8])
    return out


def stage_kernel(table, fresh_ref, kc_ref, vc_ref, k_out, vt_out, vbuf, k_sems, v_sems):
    pieces = NBLK // NEAR_BLOCKS
    part_rows = fresh_ref.shape[1] // 2
    parts = BLK // part_rows
    me = table[ME]

    def rows_of(p):
        return pl.ds(p * NEAR_ROWS, NEAR_ROWS)

    v_copies = [
        pltpu.make_async_copy(vc_ref.at[rows_of(p), :], vbuf.at[rows_of(p), :], v_sems.at[p])
        for p in range(pieces)
    ]
    k_copies = [
        pltpu.make_async_copy(kc_ref.at[rows_of(p), :], k_out.at[rows_of(p), :], k_sems.at[p])
        for p in range(pieces)
    ]
    for copy in v_copies + k_copies:
        copy.start()
    for p in range(pieces):
        v_copies[p].wait()

        def turn(b, carry):
            span = pl.ds(pl.multiple_of(b * BLK, BLK), BLK)
            for h in range(HEADS):
                vt_out[b, lanes(h), :] = vbuf[span, lanes(h)].T
            return carry

        lax.fori_loop(p * NEAR_BLOCKS, (p + 1) * NEAR_BLOCKS, turn, 0)
    for copy in k_copies:
        copy.wait()
    for s in range(MB):
        spot = table[me * MB + s]

        @pl.when(table[COUNTS + me] > s)
        def _():
            for i in range(parts):
                rows = pl.ds(pl.multiple_of(spot * BLK + i * part_rows, part_rows), part_rows)
                k_out[rows, :] = fresh_ref[s * parts + i, :part_rows, :]
            for h in range(HEADS):
                tile = jnp.concatenate(
                    [fresh_ref[s * parts + i, part_rows:, lanes(h)] for i in range(parts)], axis=0
                )
                vt_out[spot, lanes(h), :] = tile.T


def stage(table, fresh, key_cache, value_cache):
    vmem = pl.BlockSpec(memory_space=pltpu.VMEM)
    hbm = pl.BlockSpec(memory_space=pltpu.HBM)
    pieces = NBLK // NEAR_BLOCKS
    return pl.pallas_call(
        stage_kernel,
        in_specs=[pl.BlockSpec(memory_space=pltpu.SMEM), vmem, hbm, hbm],
        out_specs=[vmem] * 2,
        scratch_shapes=[
            pltpu.VMEM((NBLK * BLK, WIDE), jnp.bfloat16),
            pltpu.SemaphoreType.DMA((pieces,)),
            pltpu.SemaphoreType.DMA((pieces,)),
        ],
        out_shape=[
            jax.ShapeDtypeStruct((NBLK * BLK, WIDE), jnp.bfloat16),
            jax.ShapeDtypeStruct((NBLK, WIDE, BLK), jnp.bfloat16),
        ],
        compiler_params=pltpu.CompilerParams(vmem_limit_bytes=STAGE_LIMIT),
        cost_estimate=pl.CostEstimate(flops=0, bytes_accessed=15_000_000, transcendentals=0),
        name="stage",
    )(table, fresh, key_cache, value_cache)


def near_kernel(q_ref, k_ref, vt_ref, o_out, s_out, acc, top, tot, sbuf, pbuf):
    acc[...] = jnp.zeros_like(acc)
    top[...] = jnp.full_like(top, LOW)
    tot[...] = jnp.zeros_like(tot)

    def chunk(step, carry):
        def score(h):
            high = None
            for b in range(NEAR_BLOCKS):
                part = lax.dot_general(
                    k_ref[pl.ds(pl.multiple_of((step * NEAR_BLOCKS + b) * BLK, BLK), BLK), lanes(h)],
                    q_ref[:, lanes(h)],
                    (((1,), (1,)), ((), ())),
                    preferred_element_type=jnp.float32,
                )
                sbuf[h % 2, b * BLK : (b + 1) * BLK, :] = part
                peak = eighths(part, jnp.maximum)
                high = peak if high is None else jnp.maximum(high, peak)
            return jnp.max(high, axis=0, keepdims=True)

        ahead = score(0)
        for h in range(HEADS):
            high = ahead
            if h + 1 < HEADS:
                ahead = score(h + 1)
            old = top[h : h + 1, :]
            new = jnp.maximum(old, high)
            shrink = jnp.exp2((old - new) * EXPO)
            top[h : h + 1, :] = new
            added = None
            for b in range(NEAR_BLOCKS):
                weights = jnp.exp2((sbuf[h % 2, b * BLK : (b + 1) * BLK, :] - new) * EXPO)
                pbuf[h % 2, b * BLK : (b + 1) * BLK, :] = weights.astype(jnp.bfloat16)
                part = eighths(weights, jnp.add)
                added = part if added is None else added + part
            tot[h : h + 1, :] = tot[h : h + 1, :] * shrink + jnp.sum(added, axis=0, keepdims=True)
            values = jnp.concatenate(
                [vt_ref[step * NEAR_BLOCKS + b, lanes(h), :] for b in range(NEAR_BLOCKS)], axis=1
            )
            acc[h] = acc[h] * shrink + jnp.dot(
                values, pbuf[h % 2], preferred_element_type=jnp.float32
            )
        return carry

    lax.fori_loop(0, NBLK // NEAR_BLOCKS, chunk, 0)
    for h in range(HEADS):
        total = tot[h : h + 1, :]
        part = acc[h] * (1.0 / total)
        level = top[h : h + 1, :] * EXPO + jnp.log2(total)
        for s in range(MB):
            o_out[s, :, lanes(h)] = part[:, s * BLK : (s + 1) * BLK].astype(jnp.bfloat16)
            s_out[s : s + 1, lanes(h)] = level[:, s * BLK : (s + 1) * BLK]


def near(q, keys, values):
    rows = MB * BLK
    vmem = pl.BlockSpec(memory_space=pltpu.VMEM)
    return pl.pallas_call(
        near_kernel,
        in_specs=[vmem] * 3,
        out_specs=[vmem] * 2,
        scratch_shapes=[
            pltpu.VMEM((HEADS, HD, rows), jnp.float32),
            pltpu.VMEM((8, rows), jnp.float32),
            pltpu.VMEM((8, rows), jnp.float32),
            pltpu.VMEM((2, NEAR_ROWS, rows), jnp.float32),
            pltpu.VMEM((2, NEAR_ROWS, rows), jnp.bfloat16),
        ],
        out_shape=[
            jax.ShapeDtypeStruct((MB, HD, WIDE), jnp.bfloat16),
            jax.ShapeDtypeStruct((8, WIDE), jnp.float32),
        ],
        compiler_params=params(),
        cost_estimate=pl.CostEstimate(
            flops=4 * rows * NBLK * BLK * WIDE * 4, bytes_accessed=1_000_000, transcendentals=4_600_000
        ),
        name="near",
    )(q, keys, values)


def put_stats(stat, index, h, level):
    high = level.astype(jnp.bfloat16).astype(jnp.float32)
    rest = level - high
    mid = rest.astype(jnp.bfloat16).astype(jnp.float32)
    row = lax.broadcasted_iota(jnp.int32, (STAT, HD), 0) - index
    tile = stat[:, lanes(h)]
    for place, piece in ((0, high), (SIDE, mid), (2 * SIDE, rest - mid)):
        tile = jnp.where(row == place, piece, tile)
    stat[:, lanes(h)] = tile


def frame_at(me, item, slot, shift):
    z, x = me // SIDE, me % SIDE
    if slot == 0:
        z, x = (z + shift) % SIDE, (x + item) % SIDE
    else:
        z, x = (z + item) % SIDE, (x + shift) % SIDE
    return z * SIDE + x


def far_kernel(groups, table, *refs):
    n_groups = len(groups)
    queries, (keys, values) = refs[:n_groups], refs[n_groups : n_groups + 2]
    outs, stats = refs[n_groups + 2 : 2 * n_groups + 2], refs[2 * n_groups + 2 :]
    me = table[ME]
    for (slot, shift, skip), q_ref, out, stat in zip(groups, queries, outs, stats):
        stat[...] = jnp.zeros_like(stat)

        def step(i, carry):
            frame = frame_at(me, i + skip, slot, shift)
            count = table[RADIAL + jnp.maximum(jnp.abs(frame - me) - 1, 0)]
            start = table[frame * MB + slot] - lax.shift_right_logical(count, 1)
            start = jnp.where(start < 0, start + NBLK, start)
            spots = [start + j for j in range(CMAX)]
            spots = [jnp.where(spot >= NBLK, spot - NBLK, spot) for spot in spots]
            count = jnp.where(table[COUNTS + frame] > slot, count, 0)
            rows = pl.ds(pl.multiple_of((i + skip) * BLK, BLK), BLK)
            for n in range(1, CMAX + 1):

                @pl.when(count == n)
                def _():
                    def score(h):
                        return [
                            lax.dot_general(
                                keys[pl.ds(pl.multiple_of(spots[j] * BLK, BLK), BLK), lanes(h)],
                                q_ref[rows, lanes(h)],
                                (((1,), (1,)), ((), ())),
                                preferred_element_type=jnp.float32,
                            )
                            for j in range(n)
                        ]

                    scores = [score(h) for h in range(HEADS)]
                    tops, totals, probs = [], [], []
                    for h in range(HEADS):
                        peaks = [eighths(x, jnp.maximum) for x in scores[h]]
                        top = jnp.max(functools.reduce(jnp.maximum, peaks), axis=0, keepdims=True)
                        weights = [jnp.exp2((x - top) * EXPO) for x in scores[h]]
                        sums = [eighths(x, jnp.add) for x in weights]
                        totals.append(jnp.sum(functools.reduce(jnp.add, sums), axis=0, keepdims=True))
                        tops.append(top)
                        probs.append(jnp.concatenate([x.astype(jnp.bfloat16) for x in weights], axis=0))
                    parts = [
                        jnp.dot(
                            jnp.concatenate([values[spots[j], lanes(h), :] for j in range(n)], axis=1),
                            probs[h],
                            preferred_element_type=jnp.float32,
                        )
                        for h in range(HEADS)
                    ]
                    for h in range(HEADS):
                        out[rows, lanes(h)] = (parts[h] * (1.0 / totals[h])).astype(jnp.bfloat16)
                        put_stats(stat, i + skip, h, tops[h] * EXPO + jnp.log2(totals[h]))

            return carry

        lax.fori_loop(0, SIDE - skip, step, 0)
        out[SIDE * BLK :, :] = stat[...].astype(jnp.bfloat16)


def far(table, queries, keys, values, groups):
    items = sum(SIDE - skip for _, _, skip in groups)
    smem = pl.BlockSpec(memory_space=pltpu.SMEM)
    vmem = pl.BlockSpec(memory_space=pltpu.VMEM)
    return pl.pallas_call(
        functools.partial(far_kernel, groups),
        in_specs=[smem] + [vmem] * (len(groups) + 2),
        out_specs=[vmem] * len(groups),
        scratch_shapes=[pltpu.VMEM((STAT, WIDE), jnp.float32)] * len(groups),
        out_shape=[jax.ShapeDtypeStruct((PAY, WIDE), jnp.bfloat16)] * len(groups),
        compiler_params=params(),
        cost_estimate=pl.CostEstimate(
            flops=4 * items * BLK * CMAX * BLK * WIDE * 4,
            bytes_accessed=items * 4 * CMAX * BLK * WIDE,
            transcendentals=items * BLK * CMAX * BLK * HEADS,
        ),
        name="far",
    )(table, *queries, keys, values)


def read_level(ref, base, index):
    tile = ref[base : base + STAT, :].astype(jnp.float32)
    return (
        tile[index : index + 1]
        + tile[SIDE + index : SIDE + index + 1]
        + tile[2 * SIDE + index : 2 * SIDE + index + 1]
    )


def merge(levels, parts):
    top = functools.reduce(jnp.maximum, levels)
    shares = [jnp.exp2(level - top) for level in levels]
    total = functools.reduce(jnp.add, shares)
    scale = 1.0 / total
    out = None
    for share, part in zip(shares, parts):
        term = part() * (share * scale)
        out = term if out is None else out + term
    return out, top + jnp.log2(total)


def first_merge_kernel(slot, near_ref, near_stat, local, one, two, three, *outs):
    *outs, stat = outs
    for d in range(SIDE):
        sources = [one, two, three]
        levels = [read_level(r, SIDE * BLK, d) for r in sources]
        parts = [
            functools.partial(lambda r: r[d * BLK : (d + 1) * BLK, :].astype(jnp.float32), r)
            for r in sources
        ]
        if d == 0:
            levels.append(near_stat[slot : slot + 1, :])
            parts.append(lambda: near_ref[slot].astype(jnp.float32))
        else:
            levels.append(read_level(local, SIDE * BLK, d))
            parts.append(lambda: local[d * BLK : (d + 1) * BLK, :].astype(jnp.float32))
        value, level = merge(levels, parts)
        outs[d][:BLK, :] = value.astype(jnp.bfloat16)
        stat[...] = jnp.zeros_like(stat)
        for h in range(HEADS):
            put_stats(stat, 0, h, level[:, lanes(h)])
        outs[d][BLK:, :] = stat[...].astype(jnp.bfloat16)


def first_merge(slot, near_part, near_stat, local, received):
    return pl.pallas_call(
        functools.partial(first_merge_kernel, slot),
        out_shape=[jax.ShapeDtypeStruct((BLK + STAT, WIDE), jnp.bfloat16)] * SIDE,
        scratch_shapes=[pltpu.VMEM((STAT, WIDE), jnp.float32)],
        compiler_params=params(),
        cost_estimate=pl.CostEstimate(flops=8_000_000, bytes_accessed=3_500_000, transcendentals=0),
        name="first_merge",
    )(near_part, near_stat, local, *received)


def last_merge_kernel(table, *refs):
    *refs, out = refs
    for slot in range(MB):
        sources = refs[slot * SIDE : (slot + 1) * SIDE]
        live = table[COUNTS + table[ME]] > slot

        @pl.when(live)
        def _():
            levels = [read_level(r, BLK, 0) for r in sources]
            parts = [
                functools.partial(lambda r: r[:BLK, :].astype(jnp.float32), r) for r in sources
            ]
            value, _ = merge(levels, parts)
            for h in range(HEADS):
                out[slot * BLK : (slot + 1) * BLK, lanes(h)] = value[:, lanes(h)].T.astype(jnp.bfloat16)

        @pl.when(jnp.logical_not(live))
        def _():
            out[slot * BLK : (slot + 1) * BLK, :] = jnp.zeros((BLK, WIDE), jnp.bfloat16)


def last_merge(table, parts):
    vmem = pl.BlockSpec(memory_space=pltpu.VMEM)
    return pl.pallas_call(
        last_merge_kernel,
        in_specs=[pl.BlockSpec(memory_space=pltpu.SMEM)] + [vmem] * len(parts),
        out_specs=vmem,
        out_shape=jax.ShapeDtypeStruct((MB * BLK, WIDE), jnp.bfloat16),
        compiler_params=params(),
        name="last_merge",
    )(table, *parts)


def shift_to(x, dz, dx):
    pairs = [
        (z * SIDE + c, ((z + dz) % SIDE) * SIDE + (c + dx) % SIDE)
        for z in range(SIDE)
        for c in range(SIDE)
    ]
    return lax.ppermute(x, "frame", pairs)


def fetch(x, slot, k, step):
    along_x = (slot == 0) == (step == 1)
    return shift_to(x, 0, -k) if along_x else shift_to(x, -k, 0)


def give(x, slot, k, step):
    along_x = (slot == 0) == (step == 1)
    return shift_to(x, 0, k) if along_x else shift_to(x, k, 0)


ORDER = (1, 3, 2)


def body(
    fresh_queries,
    fresh_keys,
    fresh_values,
    key_cache,
    value_cache,
    masked_blocks,
    masked_count,
    radial_counts,
):
    me = lax.axis_index("frame").astype(jnp.int32)
    table = jnp.concatenate([masked_blocks.reshape(-1), masked_count, radial_counts, me[None]])
    q_split = split_heads(fresh_queries[0])
    q = lax.all_to_all(q_split, "head", 0, 0, tiled=True).reshape(MB * BLK, WIDE)
    halves = [q[:BLK], q[BLK:]]
    ring = [[halves[slot]] + [None] * (SIDE - 1) for slot in range(MB)]
    for k in ORDER:
        for slot in range(MB):
            ring[slot][k] = fetch(halves[slot], slot, k, 1)
    fresh = split_heads(fresh_keys[0], fresh_values[0])
    fresh = lax.all_to_all(fresh, "head", 0, 0, tiled=True)
    full = [stack(*ring[slot]) for slot in range(MB)]
    queries = [[None] * SIDE for _ in range(MB)]
    for k in ORDER:
        for slot in range(MB):
            queries[slot][k] = fetch(full[slot], slot, k, 2)
    keys, values = stage(table, fresh, key_cache[0], value_cache[0])
    late, queries[1][2] = lax.optimization_barrier((q, queries[1][2]))
    near_part, near_stat = near(late, keys, values)
    local = far(table, full, keys, values, ((0, 0, 1), (1, 0, 1)))
    back = [[] for _ in range(MB)]
    for k in ORDER:
        for slot in range(MB):
            (part,) = far(table, [queries[slot][k]], keys, values, ((slot, k, 0),))
            back[slot].append(give(part, slot, k, 2))
    final = []
    for slot in range(MB):
        merged = first_merge(slot, near_part, near_stat, local[slot], back[slot])
        final.append(merged[0])
        for k in ORDER:
            final.append(give(merged[k], slot, k, 1))
    edited = last_merge(table, final).reshape(8, MB * BLK // 8, WIDE)
    edited = lax.all_to_all(edited, "head", 0, 0, tiled=True)
    return join_heads(edited)[None]


def solution(mesh):
    placed = (
        P("frame", "head", None),
        P("frame", "head", None),
        P("frame", "head", None),
        P("frame", None, "head"),
        P("frame", None, "head"),
        P(),
        P(),
        P(),
    )
    return jax.shard_map(
        body, mesh=mesh, in_specs=placed, out_specs=P("frame", "head", None), check_vma=False
    )
```

```python
import functools
import math

import jax
import jax.numpy as jnp
from jax import lax
from jax.experimental import pallas as pl
from jax.experimental.pallas import tpu as pltpu
from jax.sharding import PartitionSpec as P

HD = 128
BLK = 128
NBLK = 28
MB = 2
CMAX = 3
HEADS = 5
WIDE = HEADS * HD
SIDE = 4
STAT = 16
PAY = SIDE * BLK + STAT
EXPO = math.log2(math.e) / math.sqrt(HD)
LOW = -1e30
FRAMES = SIDE * SIDE
COUNTS = FRAMES * MB
RADIAL = COUNTS + FRAMES
ME = RADIAL + FRAMES - 1
VMEM_LIMIT = 16 * 1024 * 1024
STAGE_LIMIT = 42 * 1024 * 1024


def lanes(h):
    return slice(h * HD, (h + 1) * HD)


def params(**kw):
    return pltpu.CompilerParams(vmem_limit_bytes=VMEM_LIMIT, **kw)


def split_kernel(*refs):
    *sources, dst = refs
    for i, src in enumerate(sources):
        rows = src.shape[0]
        for j in range(8):
            dst[j, i * rows : (i + 1) * rows, :] = src[:, j * WIDE : (j + 1) * WIDE]


def split_heads(*arrays):
    rows = sum(a.shape[0] for a in arrays)
    return pl.pallas_call(
        split_kernel,
        out_shape=jax.ShapeDtypeStruct((8, rows, WIDE), jnp.bfloat16),
        compiler_params=params(),
        name="split_heads",
    )(*arrays)


def stack_kernel(*refs):
    *sources, dst = refs
    for i, src in enumerate(sources):
        dst[i * BLK : (i + 1) * BLK, :] = src[...]


def stack(*arrays):
    return pl.pallas_call(
        stack_kernel,
        out_shape=jax.ShapeDtypeStruct((len(arrays) * BLK, WIDE), jnp.bfloat16),
        compiler_params=params(),
        name="stack",
    )(*arrays)


def join_kernel(src, dst):
    for j in range(8):
        dst[:, j * WIDE : (j + 1) * WIDE] = src[j]


def join_heads(x):
    return pl.pallas_call(
        join_kernel,
        out_shape=jax.ShapeDtypeStruct((x.shape[1], 8 * WIDE), jnp.bfloat16),
        compiler_params=params(),
        name="join_heads",
    )(x)


def fold(x, op, groups):
    rows = x.shape[0] // groups
    out = x[:rows]
    for g in range(1, groups):
        out = op(out, x[g * rows : (g + 1) * rows])
    return out


def col_max(x, groups=8):
    return jnp.max(fold(x, jnp.maximum, groups), axis=0, keepdims=True)


def col_sum(x, groups=8):
    return jnp.sum(fold(x, jnp.add, groups), axis=0, keepdims=True)


NEAR_BLOCKS = 7
NEAR_ROWS = NEAR_BLOCKS * BLK


def eighths(x, op):
    out = x[:8]
    for g in range(1, x.shape[0] // 8):
        out = op(out, x[g * 8 : (g + 1) * 8])
    return out


def stage_kernel(table, fresh_ref, kc_ref, vc_ref, k_out, vt_out, vbuf, k_sems, v_sems):
    pieces = NBLK // NEAR_BLOCKS
    part_rows = fresh_ref.shape[1] // 2
    parts = BLK // part_rows
    me = table[ME]

    def rows_of(p):
        return pl.ds(p * NEAR_ROWS, NEAR_ROWS)

    v_copies = [
        pltpu.make_async_copy(vc_ref.at[rows_of(p), :], vbuf.at[rows_of(p), :], v_sems.at[p])
        for p in range(pieces)
    ]
    k_copies = [
        pltpu.make_async_copy(kc_ref.at[rows_of(p), :], k_out.at[rows_of(p), :], k_sems.at[p])
        for p in range(pieces)
    ]
    for copy in v_copies + k_copies:
        copy.start()
    for p in range(pieces):
        v_copies[p].wait()

        def turn(b, carry):
            span = pl.ds(pl.multiple_of(b * BLK, BLK), BLK)
            for h in range(HEADS):
                vt_out[b, lanes(h), :] = vbuf[span, lanes(h)].T
            return carry

        lax.fori_loop(p * NEAR_BLOCKS, (p + 1) * NEAR_BLOCKS, turn, 0)
    for copy in k_copies:
        copy.wait()
    for s in range(MB):
        spot = table[me * MB + s]

        @pl.when(table[COUNTS + me] > s)
        def _():
            for i in range(parts):
                rows = pl.ds(pl.multiple_of(spot * BLK + i * part_rows, part_rows), part_rows)
                k_out[rows, :] = fresh_ref[s * parts + i, :part_rows, :]
            for h in range(HEADS):
                tile = jnp.concatenate(
                    [fresh_ref[s * parts + i, part_rows:, lanes(h)] for i in range(parts)], axis=0
                )
                vt_out[spot, lanes(h), :] = tile.T


def stage(table, fresh, key_cache, value_cache):
    vmem = pl.BlockSpec(memory_space=pltpu.VMEM)
    hbm = pl.BlockSpec(memory_space=pltpu.HBM)
    pieces = NBLK // NEAR_BLOCKS
    return pl.pallas_call(
        stage_kernel,
        in_specs=[pl.BlockSpec(memory_space=pltpu.SMEM), vmem, hbm, hbm],
        out_specs=[vmem] * 2,
        scratch_shapes=[
            pltpu.VMEM((NBLK * BLK, WIDE), jnp.bfloat16),
            pltpu.SemaphoreType.DMA((pieces,)),
            pltpu.SemaphoreType.DMA((pieces,)),
        ],
        out_shape=[
            jax.ShapeDtypeStruct((NBLK * BLK, WIDE), jnp.bfloat16),
            jax.ShapeDtypeStruct((NBLK, WIDE, BLK), jnp.bfloat16),
        ],
        compiler_params=pltpu.CompilerParams(vmem_limit_bytes=STAGE_LIMIT),
        cost_estimate=pl.CostEstimate(flops=0, bytes_accessed=15_000_000, transcendentals=0),
        name="stage",
    )(table, fresh, key_cache, value_cache)


def near_kernel(q_ref, k_ref, vt_ref, o_out, s_out, acc, top, tot, sbuf, pbuf):
    acc[...] = jnp.zeros_like(acc)
    top[...] = jnp.full_like(top, LOW)
    tot[...] = jnp.zeros_like(tot)

    def chunk(step, carry):
        def score(h):
            high = None
            for b in range(NEAR_BLOCKS):
                part = lax.dot_general(
                    k_ref[pl.ds(pl.multiple_of((step * NEAR_BLOCKS + b) * BLK, BLK), BLK), lanes(h)],
                    q_ref[:, lanes(h)],
                    (((1,), (1,)), ((), ())),
                    preferred_element_type=jnp.float32,
                )
                sbuf[h % 2, b * BLK : (b + 1) * BLK, :] = part
                peak = eighths(part, jnp.maximum)
                high = peak if high is None else jnp.maximum(high, peak)
            return jnp.max(high, axis=0, keepdims=True)

        ahead = score(0)
        for h in range(HEADS):
            high = ahead
            if h + 1 < HEADS:
                ahead = score(h + 1)
            old = top[h : h + 1, :]
            new = jnp.maximum(old, high)
            shrink = jnp.exp2((old - new) * EXPO)
            top[h : h + 1, :] = new
            added = None
            for b in range(NEAR_BLOCKS):
                weights = jnp.exp2((sbuf[h % 2, b * BLK : (b + 1) * BLK, :] - new) * EXPO)
                pbuf[h % 2, b * BLK : (b + 1) * BLK, :] = weights.astype(jnp.bfloat16)
                part = eighths(weights, jnp.add)
                added = part if added is None else added + part
            tot[h : h + 1, :] = tot[h : h + 1, :] * shrink + jnp.sum(added, axis=0, keepdims=True)
            values = jnp.concatenate(
                [vt_ref[step * NEAR_BLOCKS + b, lanes(h), :] for b in range(NEAR_BLOCKS)], axis=1
            )
            acc[h] = acc[h] * shrink + jnp.dot(
                values, pbuf[h % 2], preferred_element_type=jnp.float32
            )
        return carry

    lax.fori_loop(0, NBLK // NEAR_BLOCKS, chunk, 0)
    for h in range(HEADS):
        total = tot[h : h + 1, :]
        part = acc[h] * (1.0 / total)
        level = top[h : h + 1, :] * EXPO + jnp.log2(total)
        for s in range(MB):
            o_out[s, :, lanes(h)] = part[:, s * BLK : (s + 1) * BLK].astype(jnp.bfloat16)
            s_out[s : s + 1, lanes(h)] = level[:, s * BLK : (s + 1) * BLK]


def near(q, keys, values):
    rows = MB * BLK
    vmem = pl.BlockSpec(memory_space=pltpu.VMEM)
    return pl.pallas_call(
        near_kernel,
        in_specs=[vmem] * 3,
        out_specs=[vmem] * 2,
        scratch_shapes=[
            pltpu.VMEM((HEADS, HD, rows), jnp.float32),
            pltpu.VMEM((8, rows), jnp.float32),
            pltpu.VMEM((8, rows), jnp.float32),
            pltpu.VMEM((2, NEAR_ROWS, rows), jnp.float32),
            pltpu.VMEM((2, NEAR_ROWS, rows), jnp.bfloat16),
        ],
        out_shape=[
            jax.ShapeDtypeStruct((MB, HD, WIDE), jnp.bfloat16),
            jax.ShapeDtypeStruct((8, WIDE), jnp.float32),
        ],
        compiler_params=params(),
        cost_estimate=pl.CostEstimate(
            flops=4 * rows * NBLK * BLK * WIDE * 4, bytes_accessed=1_000_000, transcendentals=4_600_000
        ),
        name="near",
    )(q, keys, values)


def put_stats(stat, index, h, level):
    high = level.astype(jnp.bfloat16).astype(jnp.float32)
    rest = level - high
    mid = rest.astype(jnp.bfloat16).astype(jnp.float32)
    row = lax.broadcasted_iota(jnp.int32, (STAT, HD), 0) - index
    tile = stat[:, lanes(h)]
    for place, piece in ((0, high), (SIDE, mid), (2 * SIDE, rest - mid)):
        tile = jnp.where(row == place, piece, tile)
    stat[:, lanes(h)] = tile


def frame_at(me, item, slot, shift):
    z, x = me // SIDE, me % SIDE
    if slot == 0:
        z, x = (z + shift) % SIDE, (x + item) % SIDE
    else:
        z, x = (z + item) % SIDE, (x + shift) % SIDE
    return z * SIDE + x


def far_kernel(groups, table, *refs):
    n_groups = len(groups)
    queries, (keys, values) = refs[:n_groups], refs[n_groups : n_groups + 2]
    outs, stats = refs[n_groups + 2 : 2 * n_groups + 2], refs[2 * n_groups + 2 :]
    me = table[ME]
    for (slot, shift, skip), q_ref, out, stat in zip(groups, queries, outs, stats):
        stat[...] = jnp.zeros_like(stat)

        def step(i, carry):
            frame = frame_at(me, i + skip, slot, shift)
            count = table[RADIAL + jnp.maximum(jnp.abs(frame - me) - 1, 0)]
            start = table[frame * MB + slot] - lax.shift_right_logical(count, 1)
            start = jnp.where(start < 0, start + NBLK, start)
            spots = [start + j for j in range(CMAX)]
            spots = [jnp.where(spot >= NBLK, spot - NBLK, spot) for spot in spots]
            count = jnp.where(table[COUNTS + frame] > slot, count, 0)
            rows = pl.ds(pl.multiple_of((i + skip) * BLK, BLK), BLK)
            for n in range(1, CMAX + 1):

                @pl.when(count == n)
                def _():
                    def score(h):
                        return [
                            lax.dot_general(
                                keys[pl.ds(pl.multiple_of(spots[j] * BLK, BLK), BLK), lanes(h)],
                                q_ref[rows, lanes(h)],
                                (((1,), (1,)), ((), ())),
                                preferred_element_type=jnp.float32,
                            )
                            for j in range(n)
                        ]

                    scores = [score(h) for h in range(HEADS)]
                    tops, totals, probs = [], [], []
                    for h in range(HEADS):
                        peaks = [eighths(x, jnp.maximum) for x in scores[h]]
                        top = jnp.max(functools.reduce(jnp.maximum, peaks), axis=0, keepdims=True)
                        weights = [jnp.exp2((x - top) * EXPO) for x in scores[h]]
                        sums = [eighths(x, jnp.add) for x in weights]
                        totals.append(jnp.sum(functools.reduce(jnp.add, sums), axis=0, keepdims=True))
                        tops.append(top)
                        probs.append(jnp.concatenate([x.astype(jnp.bfloat16) for x in weights], axis=0))
                    parts = [
                        jnp.dot(
                            jnp.concatenate([values[spots[j], lanes(h), :] for j in range(n)], axis=1),
                            probs[h],
                            preferred_element_type=jnp.float32,
                        )
                        for h in range(HEADS)
                    ]
                    for h in range(HEADS):
                        out[rows, lanes(h)] = (parts[h] * (1.0 / totals[h])).astype(jnp.bfloat16)
                        put_stats(stat, i + skip, h, tops[h] * EXPO + jnp.log2(totals[h]))

            return carry

        lax.fori_loop(0, SIDE - skip, step, 0)
        out[SIDE * BLK :, :] = stat[...].astype(jnp.bfloat16)


def far(table, queries, keys, values, groups):
    items = sum(SIDE - skip for _, _, skip in groups)
    smem = pl.BlockSpec(memory_space=pltpu.SMEM)
    vmem = pl.BlockSpec(memory_space=pltpu.VMEM)
    return pl.pallas_call(
        functools.partial(far_kernel, groups),
        in_specs=[smem] + [vmem] * (len(groups) + 2),
        out_specs=[vmem] * len(groups),
        scratch_shapes=[pltpu.VMEM((STAT, WIDE), jnp.float32)] * len(groups),
        out_shape=[jax.ShapeDtypeStruct((PAY, WIDE), jnp.bfloat16)] * len(groups),
        compiler_params=params(),
        cost_estimate=pl.CostEstimate(
            flops=4 * items * BLK * CMAX * BLK * WIDE * 4,
            bytes_accessed=items * 4 * CMAX * BLK * WIDE,
            transcendentals=items * BLK * CMAX * BLK * HEADS,
        ),
        name="far",
    )(table, *queries, keys, values)


def read_level(ref, base, index):
    tile = ref[base : base + STAT, :].astype(jnp.float32)
    return (
        tile[index : index + 1]
        + tile[SIDE + index : SIDE + index + 1]
        + tile[2 * SIDE + index : 2 * SIDE + index + 1]
    )


def merge(levels, parts):
    top = functools.reduce(jnp.maximum, levels)
    shares = [jnp.exp2(level - top) for level in levels]
    total = functools.reduce(jnp.add, shares)
    scale = 1.0 / total
    out = None
    for share, part in zip(shares, parts):
        term = part() * (share * scale)
        out = term if out is None else out + term
    return out, top + jnp.log2(total)


def first_merge_kernel(slot, near_ref, near_stat, local, one, two, three, *outs):
    *outs, stat = outs
    for d in range(SIDE):
        sources = [one, two, three]
        levels = [read_level(r, SIDE * BLK, d) for r in sources]
        parts = [
            functools.partial(lambda r: r[d * BLK : (d + 1) * BLK, :].astype(jnp.float32), r)
            for r in sources
        ]
        if d == 0:
            levels.append(near_stat[slot : slot + 1, :])
            parts.append(lambda: near_ref[slot].astype(jnp.float32))
        else:
            levels.append(read_level(local, SIDE * BLK, d))
            parts.append(lambda: local[d * BLK : (d + 1) * BLK, :].astype(jnp.float32))
        value, level = merge(levels, parts)
        outs[d][:BLK, :] = value.astype(jnp.bfloat16)
        stat[...] = jnp.zeros_like(stat)
        for h in range(HEADS):
            put_stats(stat, 0, h, level[:, lanes(h)])
        outs[d][BLK:, :] = stat[...].astype(jnp.bfloat16)


def first_merge(slot, near_part, near_stat, local, received):
    return pl.pallas_call(
        functools.partial(first_merge_kernel, slot),
        out_shape=[jax.ShapeDtypeStruct((BLK + STAT, WIDE), jnp.bfloat16)] * SIDE,
        scratch_shapes=[pltpu.VMEM((STAT, WIDE), jnp.float32)],
        compiler_params=params(),
        cost_estimate=pl.CostEstimate(flops=8_000_000, bytes_accessed=3_500_000, transcendentals=0),
        name="first_merge",
    )(near_part, near_stat, local, *received)


def last_merge_kernel(table, *refs):
    *refs, out = refs
    for slot in range(MB):
        sources = refs[slot * SIDE : (slot + 1) * SIDE]
        live = table[COUNTS + table[ME]] > slot

        @pl.when(live)
        def _():
            levels = [read_level(r, BLK, 0) for r in sources]
            parts = [
                functools.partial(lambda r: r[:BLK, :].astype(jnp.float32), r) for r in sources
            ]
            value, _ = merge(levels, parts)
            for h in range(HEADS):
                out[slot * BLK : (slot + 1) * BLK, lanes(h)] = value[:, lanes(h)].T.astype(jnp.bfloat16)

        @pl.when(jnp.logical_not(live))
        def _():
            out[slot * BLK : (slot + 1) * BLK, :] = jnp.zeros((BLK, WIDE), jnp.bfloat16)


def last_merge(table, parts):
    vmem = pl.BlockSpec(memory_space=pltpu.VMEM)
    return pl.pallas_call(
        last_merge_kernel,
        in_specs=[pl.BlockSpec(memory_space=pltpu.SMEM)] + [vmem] * len(parts),
        out_specs=vmem,
        out_shape=jax.ShapeDtypeStruct((MB * BLK, WIDE), jnp.bfloat16),
        compiler_params=params(),
        name="last_merge",
    )(table, *parts)


def shift_to(x, dz, dx):
    pairs = [
        (z * SIDE + c, ((z + dz) % SIDE) * SIDE + (c + dx) % SIDE)
        for z in range(SIDE)
        for c in range(SIDE)
    ]
    return lax.ppermute(x, "frame", pairs)


def fetch(x, slot, k, step):
    along_x = (slot == 0) == (step == 1)
    return shift_to(x, 0, -k) if along_x else shift_to(x, -k, 0)


def give(x, slot, k, step):
    along_x = (slot == 0) == (step == 1)
    return shift_to(x, 0, k) if along_x else shift_to(x, k, 0)


ORDER = (1, 3, 2)


def body(
    fresh_queries,
    fresh_keys,
    fresh_values,
    key_cache,
    value_cache,
    masked_blocks,
    masked_count,
    radial_counts,
):
    me = lax.axis_index("frame").astype(jnp.int32)
    table = jnp.concatenate([masked_blocks.reshape(-1), masked_count, radial_counts, me[None]])
    q_split = split_heads(fresh_queries[0])
    q = lax.all_to_all(q_split, "head", 0, 0, tiled=True).reshape(MB * BLK, WIDE)
    halves = [q[:BLK], q[BLK:]]
    ring = [[halves[slot]] + [None] * (SIDE - 1) for slot in range(MB)]
    for k in ORDER:
        for slot in range(MB):
            ring[slot][k] = fetch(halves[slot], slot, k, 1)
    fresh = split_heads(fresh_keys[0], fresh_values[0])
    fresh = lax.all_to_all(fresh, "head", 0, 0, tiled=True)
    arrived = lax.optimization_barrier(tuple(ring[0] + ring[1]))
    full = [stack(*arrived[slot * SIDE : (slot + 1) * SIDE]) for slot in range(MB)]
    queries = [[None] * SIDE for _ in range(MB)]
    for k in ORDER:
        for slot in range(MB):
            queries[slot][k] = fetch(full[slot], slot, k, 2)
    keys, values = stage(table, fresh, key_cache[0], value_cache[0])
    late, queries[1][2] = lax.optimization_barrier((q, queries[1][2]))
    near_part, near_stat = near(late, keys, values)
    local = far(table, full, keys, values, ((0, 0, 1), (1, 0, 1)))
    back = [[] for _ in range(MB)]
    for k in ORDER:
        for slot in range(MB):
            (part,) = far(table, [queries[slot][k]], keys, values, ((slot, k, 0),))
            back[slot].append(give(part, slot, k, 2))
    final = []
    for slot in range(MB):
        merged = first_merge(slot, near_part, near_stat, local[slot], back[slot])
        final.append(merged[0])
        for k in ORDER:
            final.append(give(merged[k], slot, k, 1))
    edited = last_merge(table, final).reshape(8, MB * BLK // 8, WIDE)
    edited = lax.all_to_all(edited, "head", 0, 0, tiled=True)
    return join_heads(edited)[None]


def solution(mesh):
    placed = (
        P("frame", "head", None),
        P("frame", "head", None),
        P("frame", "head", None),
        P("frame", None, "head"),
        P("frame", None, "head"),
        P(),
        P(),
        P(),
    )
    return jax.shard_map(
        body, mesh=mesh, in_specs=placed, out_specs=P("frame", "head", None), check_vma=False
    )
```

```python
import functools
import math

import jax
import jax.numpy as jnp
from jax import lax
from jax.experimental import pallas as pl
from jax.experimental.pallas import tpu as pltpu
from jax.sharding import PartitionSpec as P

HD = 128
BLK = 128
NBLK = 28
MB = 2
CMAX = 3
HEADS = 5
WIDE = HEADS * HD
SIDE = 4
STAT = 16
PAY = SIDE * BLK + STAT
EXPO = math.log2(math.e) / math.sqrt(HD)
LOW = -1e30
FRAMES = SIDE * SIDE
COUNTS = FRAMES * MB
RADIAL = COUNTS + FRAMES
ME = RADIAL + FRAMES - 1
VMEM_LIMIT = 16 * 1024 * 1024
STAGE_LIMIT = 42 * 1024 * 1024


def lanes(h):
    return slice(h * HD, (h + 1) * HD)


def params(**kw):
    return pltpu.CompilerParams(vmem_limit_bytes=VMEM_LIMIT, **kw)


def split_kernel(*refs):
    *sources, dst = refs
    for i, src in enumerate(sources):
        rows = src.shape[0]
        for j in range(8):
            dst[j, i * rows : (i + 1) * rows, :] = src[:, j * WIDE : (j + 1) * WIDE]


def split_heads(*arrays):
    rows = sum(a.shape[0] for a in arrays)
    return pl.pallas_call(
        split_kernel,
        out_shape=jax.ShapeDtypeStruct((8, rows, WIDE), jnp.bfloat16),
        compiler_params=params(),
        name="split_heads",
    )(*arrays)


def stack_kernel(*refs):
    *sources, dst = refs
    for i, src in enumerate(sources):
        dst[i * BLK : (i + 1) * BLK, :] = src[...]


def stack(*arrays):
    return pl.pallas_call(
        stack_kernel,
        out_shape=jax.ShapeDtypeStruct((len(arrays) * BLK, WIDE), jnp.bfloat16),
        compiler_params=params(),
        name="stack",
    )(*arrays)


def join_kernel(src, dst):
    for j in range(8):
        dst[:, j * WIDE : (j + 1) * WIDE] = src[j]


def join_heads(x):
    return pl.pallas_call(
        join_kernel,
        out_shape=jax.ShapeDtypeStruct((x.shape[1], 8 * WIDE), jnp.bfloat16),
        compiler_params=params(),
        name="join_heads",
    )(x)


def fold(x, op, groups):
    rows = x.shape[0] // groups
    out = x[:rows]
    for g in range(1, groups):
        out = op(out, x[g * rows : (g + 1) * rows])
    return out


def col_max(x, groups=8):
    return jnp.max(fold(x, jnp.maximum, groups), axis=0, keepdims=True)


def col_sum(x, groups=8):
    return jnp.sum(fold(x, jnp.add, groups), axis=0, keepdims=True)


NEAR_BLOCKS = 7
NEAR_ROWS = NEAR_BLOCKS * BLK


def eighths(x, op):
    out = x[:8]
    for g in range(1, x.shape[0] // 8):
        out = op(out, x[g * 8 : (g + 1) * 8])
    return out


def stage_kernel(table, fresh_ref, kc_ref, vc_ref, k_out, vt_out, vbuf, k_sems, v_sems):
    pieces = NBLK // NEAR_BLOCKS
    part_rows = fresh_ref.shape[1] // 2
    parts = BLK // part_rows
    me = table[ME]

    def rows_of(p):
        return pl.ds(p * NEAR_ROWS, NEAR_ROWS)

    v_copies = [
        pltpu.make_async_copy(vc_ref.at[rows_of(p), :], vbuf.at[rows_of(p), :], v_sems.at[p])
        for p in range(pieces)
    ]
    k_copies = [
        pltpu.make_async_copy(kc_ref.at[rows_of(p), :], k_out.at[rows_of(p), :], k_sems.at[p])
        for p in range(pieces)
    ]
    for copy in v_copies + k_copies:
        copy.start()
    for p in range(pieces):
        v_copies[p].wait()

        def turn(b, carry):
            span = pl.ds(pl.multiple_of(b * BLK, BLK), BLK)
            for h in range(HEADS):
                vt_out[b, lanes(h), :] = vbuf[span, lanes(h)].T
            return carry

        lax.fori_loop(p * NEAR_BLOCKS, (p + 1) * NEAR_BLOCKS, turn, 0)
    for copy in k_copies:
        copy.wait()
    for s in range(MB):
        spot = table[me * MB + s]

        @pl.when(table[COUNTS + me] > s)
        def _():
            for i in range(parts):
                rows = pl.ds(pl.multiple_of(spot * BLK + i * part_rows, part_rows), part_rows)
                k_out[rows, :] = fresh_ref[s * parts + i, :part_rows, :]
            for h in range(HEADS):
                tile = jnp.concatenate(
                    [fresh_ref[s * parts + i, part_rows:, lanes(h)] for i in range(parts)], axis=0
                )
                vt_out[spot, lanes(h), :] = tile.T


def stage(table, fresh, key_cache, value_cache):
    vmem = pl.BlockSpec(memory_space=pltpu.VMEM)
    hbm = pl.BlockSpec(memory_space=pltpu.HBM)
    pieces = NBLK // NEAR_BLOCKS
    return pl.pallas_call(
        stage_kernel,
        in_specs=[pl.BlockSpec(memory_space=pltpu.SMEM), vmem, hbm, hbm],
        out_specs=[vmem] * 2,
        scratch_shapes=[
            pltpu.VMEM((NBLK * BLK, WIDE), jnp.bfloat16),
            pltpu.SemaphoreType.DMA((pieces,)),
            pltpu.SemaphoreType.DMA((pieces,)),
        ],
        out_shape=[
            jax.ShapeDtypeStruct((NBLK * BLK, WIDE), jnp.bfloat16),
            jax.ShapeDtypeStruct((NBLK, WIDE, BLK), jnp.bfloat16),
        ],
        compiler_params=pltpu.CompilerParams(vmem_limit_bytes=STAGE_LIMIT),
        cost_estimate=pl.CostEstimate(flops=0, bytes_accessed=15_000_000, transcendentals=0),
        name="stage",
    )(table, fresh, key_cache, value_cache)


def near_kernel(q_ref, k_ref, vt_ref, o_out, s_out, acc, top, tot, sbuf, pbuf):
    acc[...] = jnp.zeros_like(acc)
    top[...] = jnp.full_like(top, LOW)
    tot[...] = jnp.zeros_like(tot)

    def chunk(step, carry):
        def score(h):
            high = None
            for b in range(NEAR_BLOCKS):
                part = lax.dot_general(
                    k_ref[pl.ds(pl.multiple_of((step * NEAR_BLOCKS + b) * BLK, BLK), BLK), lanes(h)],
                    q_ref[:, lanes(h)],
                    (((1,), (1,)), ((), ())),
                    preferred_element_type=jnp.float32,
                )
                sbuf[h % 2, b * BLK : (b + 1) * BLK, :] = part
                peak = eighths(part, jnp.maximum)
                high = peak if high is None else jnp.maximum(high, peak)
            return jnp.max(high, axis=0, keepdims=True)

        ahead = score(0)
        for h in range(HEADS):
            high = ahead
            if h + 1 < HEADS:
                ahead = score(h + 1)
            old = top[h : h + 1, :]
            new = jnp.maximum(old, high)
            shrink = jnp.exp2((old - new) * EXPO)
            top[h : h + 1, :] = new
            added = None
            for b in range(NEAR_BLOCKS):
                weights = jnp.exp2((sbuf[h % 2, b * BLK : (b + 1) * BLK, :] - new) * EXPO)
                pbuf[h % 2, b * BLK : (b + 1) * BLK, :] = weights.astype(jnp.bfloat16)
                part = eighths(weights, jnp.add)
                added = part if added is None else added + part
            tot[h : h + 1, :] = tot[h : h + 1, :] * shrink + jnp.sum(added, axis=0, keepdims=True)
            values = jnp.concatenate(
                [vt_ref[step * NEAR_BLOCKS + b, lanes(h), :] for b in range(NEAR_BLOCKS)], axis=1
            )
            acc[h] = acc[h] * shrink + jnp.dot(
                values, pbuf[h % 2], preferred_element_type=jnp.float32
            )
        return carry

    lax.fori_loop(0, NBLK // NEAR_BLOCKS, chunk, 0)
    for h in range(HEADS):
        total = tot[h : h + 1, :]
        part = acc[h] * (1.0 / total)
        level = top[h : h + 1, :] * EXPO + jnp.log2(total)
        for s in range(MB):
            o_out[s, :, lanes(h)] = part[:, s * BLK : (s + 1) * BLK].astype(jnp.bfloat16)
            s_out[s : s + 1, lanes(h)] = level[:, s * BLK : (s + 1) * BLK]


def near(q, keys, values):
    rows = MB * BLK
    vmem = pl.BlockSpec(memory_space=pltpu.VMEM)
    return pl.pallas_call(
        near_kernel,
        in_specs=[vmem] * 3,
        out_specs=[vmem] * 2,
        scratch_shapes=[
            pltpu.VMEM((HEADS, HD, rows), jnp.float32),
            pltpu.VMEM((8, rows), jnp.float32),
            pltpu.VMEM((8, rows), jnp.float32),
            pltpu.VMEM((2, NEAR_ROWS, rows), jnp.float32),
            pltpu.VMEM((2, NEAR_ROWS, rows), jnp.bfloat16),
        ],
        out_shape=[
            jax.ShapeDtypeStruct((MB, HD, WIDE), jnp.bfloat16),
            jax.ShapeDtypeStruct((8, WIDE), jnp.float32),
        ],
        compiler_params=params(),
        cost_estimate=pl.CostEstimate(
            flops=4 * rows * NBLK * BLK * WIDE * 4, bytes_accessed=1_000_000, transcendentals=4_600_000
        ),
        name="near",
    )(q, keys, values)


def put_stats(stat, index, h, level):
    high = level.astype(jnp.bfloat16).astype(jnp.float32)
    rest = level - high
    mid = rest.astype(jnp.bfloat16).astype(jnp.float32)
    row = lax.broadcasted_iota(jnp.int32, (STAT, HD), 0) - index
    tile = stat[:, lanes(h)]
    for place, piece in ((0, high), (SIDE, mid), (2 * SIDE, rest - mid)):
        tile = jnp.where(row == place, piece, tile)
    stat[:, lanes(h)] = tile


def frame_at(me, item, slot, shift):
    z, x = me // SIDE, me % SIDE
    if slot == 0:
        z, x = (z + shift) % SIDE, (x + item) % SIDE
    else:
        z, x = (z + item) % SIDE, (x + shift) % SIDE
    return z * SIDE + x


def far_kernel(groups, table, *refs):
    n_groups = len(groups)
    queries, (keys, values) = refs[:n_groups], refs[n_groups : n_groups + 2]
    outs, stats = refs[n_groups + 2 : 2 * n_groups + 2], refs[2 * n_groups + 2 :]
    me = table[ME]
    for (slot, shift, skip), q_ref, out, stat in zip(groups, queries, outs, stats):
        stat[...] = jnp.zeros_like(stat)

        def step(i, carry):
            frame = frame_at(me, i + skip, slot, shift)
            count = table[RADIAL + jnp.maximum(jnp.abs(frame - me) - 1, 0)]
            start = table[frame * MB + slot] - lax.shift_right_logical(count, 1)
            start = jnp.where(start < 0, start + NBLK, start)
            spots = [start + j for j in range(CMAX)]
            spots = [jnp.where(spot >= NBLK, spot - NBLK, spot) for spot in spots]
            count = jnp.where(table[COUNTS + frame] > slot, count, 0)
            rows = pl.ds(pl.multiple_of((i + skip) * BLK, BLK), BLK)
            for n in range(1, CMAX + 1):

                @pl.when(count == n)
                def _():
                    def score(h):
                        return [
                            lax.dot_general(
                                keys[pl.ds(pl.multiple_of(spots[j] * BLK, BLK), BLK), lanes(h)],
                                q_ref[rows, lanes(h)],
                                (((1,), (1,)), ((), ())),
                                preferred_element_type=jnp.float32,
                            )
                            for j in range(n)
                        ]

                    scores = [score(h) for h in range(HEADS)]
                    tops, totals, probs = [], [], []
                    for h in range(HEADS):
                        peaks = [eighths(x, jnp.maximum) for x in scores[h]]
                        top = jnp.max(functools.reduce(jnp.maximum, peaks), axis=0, keepdims=True)
                        weights = [jnp.exp2((x - top) * EXPO) for x in scores[h]]
                        sums = [eighths(x, jnp.add) for x in weights]
                        totals.append(jnp.sum(functools.reduce(jnp.add, sums), axis=0, keepdims=True))
                        tops.append(top)
                        probs.append(jnp.concatenate([x.astype(jnp.bfloat16) for x in weights], axis=0))
                    parts = [
                        jnp.dot(
                            jnp.concatenate([values[spots[j], lanes(h), :] for j in range(n)], axis=1),
                            probs[h],
                            preferred_element_type=jnp.float32,
                        )
                        for h in range(HEADS)
                    ]
                    for h in range(HEADS):
                        out[rows, lanes(h)] = (parts[h] * (1.0 / totals[h])).astype(jnp.bfloat16)
                        put_stats(stat, i + skip, h, tops[h] * EXPO + jnp.log2(totals[h]))

            return carry

        lax.fori_loop(0, SIDE - skip, step, 0)
        out[SIDE * BLK :, :] = stat[...].astype(jnp.bfloat16)


def far(table, queries, keys, values, groups):
    items = sum(SIDE - skip for _, _, skip in groups)
    smem = pl.BlockSpec(memory_space=pltpu.SMEM)
    vmem = pl.BlockSpec(memory_space=pltpu.VMEM)
    return pl.pallas_call(
        functools.partial(far_kernel, groups),
        in_specs=[smem] + [vmem] * (len(groups) + 2),
        out_specs=[vmem] * len(groups),
        scratch_shapes=[pltpu.VMEM((STAT, WIDE), jnp.float32)] * len(groups),
        out_shape=[jax.ShapeDtypeStruct((PAY, WIDE), jnp.bfloat16)] * len(groups),
        compiler_params=params(),
        cost_estimate=pl.CostEstimate(
            flops=4 * items * BLK * CMAX * BLK * WIDE * 4,
            bytes_accessed=items * 4 * CMAX * BLK * WIDE,
            transcendentals=items * BLK * CMAX * BLK * HEADS,
        ),
        name="far",
    )(table, *queries, keys, values)


def read_level(ref, base, index):
    tile = ref[base : base + STAT, :].astype(jnp.float32)
    return (
        tile[index : index + 1]
        + tile[SIDE + index : SIDE + index + 1]
        + tile[2 * SIDE + index : 2 * SIDE + index + 1]
    )


def merge(levels, parts):
    top = functools.reduce(jnp.maximum, levels)
    shares = [jnp.exp2(level - top) for level in levels]
    total = functools.reduce(jnp.add, shares)
    scale = 1.0 / total
    out = None
    for share, part in zip(shares, parts):
        term = part() * (share * scale)
        out = term if out is None else out + term
    return out, top + jnp.log2(total)


def first_merge_kernel(slot, near_ref, near_stat, local, one, two, three, *outs):
    *outs, stat = outs
    for d in range(SIDE):
        sources = [one, two, three]
        levels = [read_level(r, SIDE * BLK, d) for r in sources]
        parts = [
            functools.partial(lambda r: r[d * BLK : (d + 1) * BLK, :].astype(jnp.float32), r)
            for r in sources
        ]
        if d == 0:
            levels.append(near_stat[slot : slot + 1, :])
            parts.append(lambda: near_ref[slot].astype(jnp.float32))
        else:
            levels.append(read_level(local, SIDE * BLK, d))
            parts.append(lambda: local[d * BLK : (d + 1) * BLK, :].astype(jnp.float32))
        value, level = merge(levels, parts)
        outs[d][:BLK, :] = value.astype(jnp.bfloat16)
        stat[...] = jnp.zeros_like(stat)
        for h in range(HEADS):
            put_stats(stat, 0, h, level[:, lanes(h)])
        outs[d][BLK:, :] = stat[...].astype(jnp.bfloat16)


def first_merge(slot, near_part, near_stat, local, received):
    return pl.pallas_call(
        functools.partial(first_merge_kernel, slot),
        out_shape=[jax.ShapeDtypeStruct((BLK + STAT, WIDE), jnp.bfloat16)] * SIDE,
        scratch_shapes=[pltpu.VMEM((STAT, WIDE), jnp.float32)],
        compiler_params=params(),
        cost_estimate=pl.CostEstimate(flops=8_000_000, bytes_accessed=3_500_000, transcendentals=0),
        name="first_merge",
    )(near_part, near_stat, local, *received)


def last_merge_kernel(table, *refs):
    *refs, out = refs
    for slot in range(MB):
        sources = refs[slot * SIDE : (slot + 1) * SIDE]
        live = table[COUNTS + table[ME]] > slot

        @pl.when(live)
        def _():
            levels = [read_level(r, BLK, 0) for r in sources]
            parts = [
                functools.partial(lambda r: r[:BLK, :].astype(jnp.float32), r) for r in sources
            ]
            value, _ = merge(levels, parts)
            for h in range(HEADS):
                out[slot * BLK : (slot + 1) * BLK, lanes(h)] = value[:, lanes(h)].T.astype(jnp.bfloat16)

        @pl.when(jnp.logical_not(live))
        def _():
            out[slot * BLK : (slot + 1) * BLK, :] = jnp.zeros((BLK, WIDE), jnp.bfloat16)


def last_merge(table, parts):
    vmem = pl.BlockSpec(memory_space=pltpu.VMEM)
    return pl.pallas_call(
        last_merge_kernel,
        in_specs=[pl.BlockSpec(memory_space=pltpu.SMEM)] + [vmem] * len(parts),
        out_specs=vmem,
        out_shape=jax.ShapeDtypeStruct((MB * BLK, WIDE), jnp.bfloat16),
        compiler_params=params(),
        name="last_merge",
    )(table, *parts)


def shift_to(x, dz, dx):
    pairs = [
        (z * SIDE + c, ((z + dz) % SIDE) * SIDE + (c + dx) % SIDE)
        for z in range(SIDE)
        for c in range(SIDE)
    ]
    return lax.ppermute(x, "frame", pairs)


def fetch(x, slot, k, step):
    along_x = (slot == 0) == (step == 1)
    return shift_to(x, 0, -k) if along_x else shift_to(x, -k, 0)


def give(x, slot, k, step):
    along_x = (slot == 0) == (step == 1)
    return shift_to(x, 0, k) if along_x else shift_to(x, k, 0)


ORDER = (1, 3, 2)


def body(
    fresh_queries,
    fresh_keys,
    fresh_values,
    key_cache,
    value_cache,
    masked_blocks,
    masked_count,
    radial_counts,
):
    me = lax.axis_index("frame").astype(jnp.int32)
    table = jnp.concatenate([masked_blocks.reshape(-1), masked_count, radial_counts, me[None]])
    q_split = split_heads(fresh_queries[0])
    q = lax.all_to_all(q_split, "head", 0, 0, tiled=True).reshape(MB * BLK, WIDE)
    halves = [q[:BLK], q[BLK:]]
    ring = [[halves[slot]] + [None] * (SIDE - 1) for slot in range(MB)]
    for k in ORDER:
        for slot in range(MB):
            ring[slot][k] = fetch(halves[slot], slot, k, 1)
    arrived = lax.optimization_barrier(tuple(ring[0] + ring[1]))
    full = [stack(*arrived[slot * SIDE : (slot + 1) * SIDE]) for slot in range(MB)]
    queries = [[None] * SIDE for _ in range(MB)]
    for k in ORDER[:2]:
        for slot in range(MB):
            queries[slot][k] = fetch(full[slot], slot, k, 2)
    fresh, *_ = lax.optimization_barrier(
        (split_heads(fresh_keys[0], fresh_values[0]), *full)
    )
    fresh = lax.all_to_all(fresh, "head", 0, 0, tiled=True)
    keys, values = stage(table, fresh, key_cache[0], value_cache[0])
    local = far(table, full, keys, values, ((0, 0, 1), (1, 0, 1)))
    *late, _ = lax.optimization_barrier((*full, local[0]))
    for slot in range(MB):
        queries[slot][2] = fetch(late[slot], slot, 2, 2)
    back = [[] for _ in range(MB)]
    last = None
    for k in ORDER:
        for slot in range(MB):
            query = queries[slot][k]
            if last is not None:
                query, _ = lax.optimization_barrier((query, last))
            (last,) = far(table, [query], keys, values, ((slot, k, 0),))
            back[slot].append(give(last, slot, k, 2))
    late, _ = lax.optimization_barrier((q, last))
    near_part, near_stat = near(late, keys, values)
    final = []
    for slot in range(MB):
        merged = first_merge(slot, near_part, near_stat, local[slot], back[slot])
        final.append(merged[0])
        for k in ORDER:
            final.append(give(merged[k], slot, k, 1))
    edited = last_merge(table, final).reshape(8, MB * BLK // 8, WIDE)
    edited = lax.all_to_all(edited, "head", 0, 0, tiled=True)
    return join_heads(edited)[None]


def solution(mesh):
    placed = (
        P("frame", "head", None),
        P("frame", "head", None),
        P("frame", "head", None),
        P("frame", None, "head"),
        P("frame", None, "head"),
        P(),
        P(),
        P(),
    )
    return jax.shard_map(
        body, mesh=mesh, in_specs=placed, out_specs=P("frame", "head", None), check_vma=False
    )
```

```python
import functools
import math

import jax
import jax.numpy as jnp
from jax import lax
from jax.experimental import pallas as pl
from jax.experimental.pallas import tpu as pltpu
from jax.sharding import PartitionSpec as P

HD = 128
BLK = 128
NBLK = 28
MB = 2
CMAX = 3
HEADS = 5
WIDE = HEADS * HD
SIDE = 4
ROWS = MB * BLK
ITEMS = SIDE * MB
STAT = 32
PAY = SIDE * ROWS + STAT
ONE = 16
EXPO = math.log2(math.e) / math.sqrt(HD)
LOW = -1e30
FRAMES = SIDE * SIDE
COUNTS = FRAMES * MB
RADIAL = COUNTS + FRAMES
ME = RADIAL + FRAMES - 1
CORE = ME + 1
VMEM_LIMIT = 16 * 1024 * 1024
STAGE_LIMIT = 42 * 1024 * 1024


def lanes(h):
    return slice(h * HD, (h + 1) * HD)


def params(**kw):
    return pltpu.CompilerParams(vmem_limit_bytes=VMEM_LIMIT, **kw)


def split_kernel(*refs):
    *sources, dst = refs
    for i, src in enumerate(sources):
        rows = src.shape[0]
        for j in range(8):
            dst[j, i * rows : (i + 1) * rows, :] = src[:, j * WIDE : (j + 1) * WIDE]


def split_heads(*arrays):
    rows = sum(a.shape[0] for a in arrays)
    return pl.pallas_call(
        split_kernel,
        out_shape=jax.ShapeDtypeStruct((8, rows, WIDE), jnp.bfloat16),
        compiler_params=params(),
        name="split_heads",
    )(*arrays)


def stack_kernel(*refs):
    *sources, dst = refs
    for i, src in enumerate(sources):
        dst[i * ROWS : (i + 1) * ROWS, :] = src[...]


def stack(*arrays):
    return pl.pallas_call(
        stack_kernel,
        out_shape=jax.ShapeDtypeStruct((len(arrays) * ROWS, WIDE), jnp.bfloat16),
        compiler_params=params(),
        name="stack",
    )(*arrays)


def join_kernel(src, dst):
    for j in range(8):
        dst[:, j * WIDE : (j + 1) * WIDE] = src[j]


def join_heads(x):
    return pl.pallas_call(
        join_kernel,
        out_shape=jax.ShapeDtypeStruct((x.shape[1], 8 * WIDE), jnp.bfloat16),
        compiler_params=params(),
        name="join_heads",
    )(x)


def fold(x, op, groups):
    rows = x.shape[0] // groups
    out = x[:rows]
    for g in range(1, groups):
        out = op(out, x[g * rows : (g + 1) * rows])
    return out


def col_max(x, groups=8):
    return jnp.max(fold(x, jnp.maximum, groups), axis=0, keepdims=True)


def col_sum(x, groups=8):
    return jnp.sum(fold(x, jnp.add, groups), axis=0, keepdims=True)


NEAR_BLOCKS = 7
NEAR_ROWS = NEAR_BLOCKS * BLK


def eighths(x, op):
    out = x[:8]
    for g in range(1, x.shape[0] // 8):
        out = op(out, x[g * 8 : (g + 1) * 8])
    return out


def stage_kernel(table, fresh_ref, kc_ref, vc_ref, k_out, vt_out, vbuf, k_sems, v_sems):
    pieces = NBLK // NEAR_BLOCKS
    part_rows = fresh_ref.shape[1] // 2
    parts = BLK // part_rows
    me = table[ME]

    def rows_of(p):
        return pl.ds(p * NEAR_ROWS, NEAR_ROWS)

    v_copies = [
        pltpu.make_async_copy(vc_ref.at[rows_of(p), :], vbuf.at[rows_of(p), :], v_sems.at[p])
        for p in range(pieces)
    ]
    k_copies = [
        pltpu.make_async_copy(kc_ref.at[rows_of(p), :], k_out.at[rows_of(p), :], k_sems.at[p])
        for p in range(pieces)
    ]
    for copy in v_copies + k_copies:
        copy.start()
    for p in range(pieces):
        v_copies[p].wait()

        def turn(b, carry):
            span = pl.ds(pl.multiple_of(b * BLK, BLK), BLK)
            for h in range(HEADS):
                vt_out[b, lanes(h), :] = vbuf[span, lanes(h)].T
            return carry

        lax.fori_loop(p * NEAR_BLOCKS, (p + 1) * NEAR_BLOCKS, turn, 0)
    for copy in k_copies:
        copy.wait()
    for s in range(MB):
        spot = table[me * MB + s]

        @pl.when(table[COUNTS + me] > s)
        def _():
            for i in range(parts):
                rows = pl.ds(pl.multiple_of(spot * BLK + i * part_rows, part_rows), part_rows)
                k_out[rows, :] = fresh_ref[s * parts + i, :part_rows, :]
            for h in range(HEADS):
                tile = jnp.concatenate(
                    [fresh_ref[s * parts + i, part_rows:, lanes(h)] for i in range(parts)], axis=0
                )
                vt_out[spot, lanes(h), :] = tile.T


def stage(table, fresh, key_cache, value_cache):
    vmem = pl.BlockSpec(memory_space=pltpu.VMEM)
    hbm = pl.BlockSpec(memory_space=pltpu.HBM)
    pieces = NBLK // NEAR_BLOCKS
    return pl.pallas_call(
        stage_kernel,
        in_specs=[pl.BlockSpec(memory_space=pltpu.SMEM), vmem, hbm, hbm],
        out_specs=[vmem] * 2,
        scratch_shapes=[
            pltpu.VMEM((NBLK * BLK, WIDE), jnp.bfloat16),
            pltpu.SemaphoreType.DMA((pieces,)),
            pltpu.SemaphoreType.DMA((pieces,)),
        ],
        out_shape=[
            jax.ShapeDtypeStruct((NBLK * BLK, WIDE), jnp.bfloat16),
            jax.ShapeDtypeStruct((NBLK, WIDE, BLK), jnp.bfloat16),
        ],
        compiler_params=pltpu.CompilerParams(vmem_limit_bytes=STAGE_LIMIT),
        cost_estimate=pl.CostEstimate(flops=0, bytes_accessed=15_000_000, transcendentals=0),
        name="stage",
    )(table, fresh, key_cache, value_cache)


def near_kernel(q_ref, k_ref, vt_ref, o_out, s_out, acc, top, tot, sbuf, pbuf):
    acc[...] = jnp.zeros_like(acc)
    top[...] = jnp.full_like(top, LOW)
    tot[...] = jnp.zeros_like(tot)

    def chunk(step, carry):
        def score(h):
            high = None
            for b in range(NEAR_BLOCKS):
                part = lax.dot_general(
                    k_ref[pl.ds(pl.multiple_of((step * NEAR_BLOCKS + b) * BLK, BLK), BLK), lanes(h)],
                    q_ref[:, lanes(h)],
                    (((1,), (1,)), ((), ())),
                    preferred_element_type=jnp.float32,
                )
                sbuf[h % 2, b * BLK : (b + 1) * BLK, :] = part
                peak = eighths(part, jnp.maximum)
                high = peak if high is None else jnp.maximum(high, peak)
            return jnp.max(high, axis=0, keepdims=True)

        ahead = score(0)
        for h in range(HEADS):
            high = ahead
            if h + 1 < HEADS:
                ahead = score(h + 1)
            old = top[h : h + 1, :]
            new = jnp.maximum(old, high)
            shrink = jnp.exp2((old - new) * EXPO)
            top[h : h + 1, :] = new
            added = None
            for b in range(NEAR_BLOCKS):
                weights = jnp.exp2((sbuf[h % 2, b * BLK : (b + 1) * BLK, :] - new) * EXPO)
                pbuf[h % 2, b * BLK : (b + 1) * BLK, :] = weights.astype(jnp.bfloat16)
                part = eighths(weights, jnp.add)
                added = part if added is None else added + part
            tot[h : h + 1, :] = tot[h : h + 1, :] * shrink + jnp.sum(added, axis=0, keepdims=True)
            values = jnp.concatenate(
                [vt_ref[step * NEAR_BLOCKS + b, lanes(h), :] for b in range(NEAR_BLOCKS)], axis=1
            )
            acc[h] = acc[h] * shrink + jnp.dot(
                values, pbuf[h % 2], preferred_element_type=jnp.float32
            )
        return carry

    lax.fori_loop(0, NBLK // NEAR_BLOCKS, chunk, 0)
    for h in range(HEADS):
        total = tot[h : h + 1, :]
        part = acc[h] * (1.0 / total)
        level = top[h : h + 1, :] * EXPO + jnp.log2(total)
        for s in range(MB):
            o_out[s, :, lanes(h)] = part[:, s * BLK : (s + 1) * BLK].astype(jnp.bfloat16)
            s_out[s : s + 1, lanes(h)] = level[:, s * BLK : (s + 1) * BLK]


def near(q, keys, values):
    rows = MB * BLK
    vmem = pl.BlockSpec(memory_space=pltpu.VMEM)
    return pl.pallas_call(
        near_kernel,
        in_specs=[vmem] * 3,
        out_specs=[vmem] * 2,
        scratch_shapes=[
            pltpu.VMEM((HEADS, HD, rows), jnp.float32),
            pltpu.VMEM((8, rows), jnp.float32),
            pltpu.VMEM((8, rows), jnp.float32),
            pltpu.VMEM((2, NEAR_ROWS, rows), jnp.float32),
            pltpu.VMEM((2, NEAR_ROWS, rows), jnp.bfloat16),
        ],
        out_shape=[
            jax.ShapeDtypeStruct((MB, HD, WIDE), jnp.bfloat16),
            jax.ShapeDtypeStruct((8, WIDE), jnp.float32),
        ],
        compiler_params=params(),
        cost_estimate=pl.CostEstimate(
            flops=100_000_000, bytes_accessed=400_000, transcendentals=0
        ),
        name="near",
    )(q, keys, values)


def put_stats(stat, index, apart, h, level):
    high = level.astype(jnp.bfloat16).astype(jnp.float32)
    rest = level - high
    mid = rest.astype(jnp.bfloat16).astype(jnp.float32)
    row = lax.broadcasted_iota(jnp.int32, (stat.shape[0], HD), 0) - index
    tile = stat[:, lanes(h)]
    for place, piece in ((0, high), (apart, mid), (2 * apart, rest - mid)):
        tile = jnp.where(row == place, piece, tile)
    stat[:, lanes(h)] = tile


def frame_at(table, item, shift):
    me = table[ME]
    odd = table[CORE] == 1
    z = lax.shift_right_logical(me, 2) + jnp.where(odd, item, shift)
    x = (me & (SIDE - 1)) + jnp.where(odd, shift, item)
    return (z & (SIDE - 1)) * SIDE + (x & (SIDE - 1))


def far_kernel(shift, skip, table, q_ref, keys, values, out, stat):
    stat[...] = jnp.zeros_like(stat)
    me = table[ME]

    def step(i, carry):
        slot = i & (MB - 1)
        frame = frame_at(table, lax.shift_right_logical(i, 1), shift)
        count = table[RADIAL + jnp.maximum(jnp.abs(frame - me) - 1, 0)]
        start = table[frame * MB + slot] - lax.shift_right_logical(count, 1)
        start = jnp.where(start < 0, start + NBLK, start)
        spots = [start + j for j in range(CMAX)]
        spots = [jnp.where(spot >= NBLK, spot - NBLK, spot) for spot in spots]
        count = jnp.where(table[COUNTS + frame] > slot, count, 0)
        rows = pl.ds(pl.multiple_of(i * BLK, BLK), BLK)
        for n in range(1, CMAX + 1):

            @pl.when(count == n)
            def _():
                def score(h):
                    return [
                        lax.dot_general(
                            keys[pl.ds(pl.multiple_of(spots[j] * BLK, BLK), BLK), lanes(h)],
                            q_ref[rows, lanes(h)],
                            (((1,), (1,)), ((), ())),
                            preferred_element_type=jnp.float32,
                        )
                        for j in range(n)
                    ]

                scores = [score(h) for h in range(HEADS)]
                tops, totals, probs = [], [], []
                for h in range(HEADS):
                    peaks = [eighths(x, jnp.maximum) for x in scores[h]]
                    top = jnp.max(functools.reduce(jnp.maximum, peaks), axis=0, keepdims=True)
                    weights = [jnp.exp2((x - top) * EXPO) for x in scores[h]]
                    sums = [eighths(x, jnp.add) for x in weights]
                    totals.append(jnp.sum(functools.reduce(jnp.add, sums), axis=0, keepdims=True))
                    tops.append(top)
                    probs.append(jnp.concatenate([x.astype(jnp.bfloat16) for x in weights], axis=0))
                parts = [
                    jnp.dot(
                        jnp.concatenate([values[spots[j], lanes(h), :] for j in range(n)], axis=1),
                        probs[h],
                        preferred_element_type=jnp.float32,
                    )
                    for h in range(HEADS)
                ]
                for h in range(HEADS):
                    out[rows, lanes(h)] = (parts[h] * (1.0 / totals[h])).astype(jnp.bfloat16)
                    put_stats(stat, i, ITEMS, h, tops[h] * EXPO + jnp.log2(totals[h]))

        return carry

    lax.fori_loop(skip * MB, ITEMS, step, 0)
    out[SIDE * ROWS :, :] = stat[...].astype(jnp.bfloat16)


def far(table, queries, keys, values, shift, skip):
    smem = pl.BlockSpec(memory_space=pltpu.SMEM)
    vmem = pl.BlockSpec(memory_space=pltpu.VMEM)
    return pl.pallas_call(
        functools.partial(far_kernel, shift, skip),
        in_specs=[smem] + [vmem] * 3,
        out_specs=vmem,
        scratch_shapes=[pltpu.VMEM((STAT, WIDE), jnp.float32)],
        out_shape=jax.ShapeDtypeStruct((PAY, WIDE), jnp.bfloat16),
        compiler_params=params(),
        cost_estimate=pl.CostEstimate(
            flops=100_000_000, bytes_accessed=400_000, transcendentals=0
        ),
        name="far",
    )(table, queries, keys, values)


def read_level(ref, base, index, apart):
    tile = ref[base:, :].astype(jnp.float32)
    return (
        tile[index : index + 1]
        + tile[apart + index : apart + index + 1]
        + tile[2 * apart + index : 2 * apart + index + 1]
    )


def read_part(ref, index):
    return ref[index * BLK : (index + 1) * BLK, :].astype(jnp.float32)


def merge(levels, parts):
    top = functools.reduce(jnp.maximum, levels)
    shares = [jnp.exp2(level - top) for level in levels]
    total = functools.reduce(jnp.add, shares)
    scale = 1.0 / total
    out = None
    for share, part in zip(shares, parts):
        term = part() * (share * scale)
        out = term if out is None else out + term
    return out, top + jnp.log2(total)


def first_merge_kernel(near_ref, near_stat, local, one, two, three, *outs):
    *outs, stat = outs
    for d in range(SIDE):
        stat[...] = jnp.zeros_like(stat)
        for slot in range(MB):
            index = d * MB + slot
            sources = [one, two, three] + ([local] if d else [])
            levels = [read_level(r, SIDE * ROWS, index, ITEMS) for r in sources]
            parts = [functools.partial(read_part, r, index) for r in sources]
            if d == 0:
                levels.append(near_stat[slot : slot + 1, :])
                parts.append(lambda: near_ref[slot].astype(jnp.float32))
            value, level = merge(levels, parts)
            outs[d][slot * BLK : (slot + 1) * BLK, :] = value.astype(jnp.bfloat16)
            for h in range(HEADS):
                put_stats(stat, slot, MB, h, level[:, lanes(h)])
        outs[d][ROWS:, :] = stat[...].astype(jnp.bfloat16)


def first_merge(near_part, near_stat, local, received):
    return pl.pallas_call(
        first_merge_kernel,
        out_shape=[jax.ShapeDtypeStruct((ROWS + ONE, WIDE), jnp.bfloat16)] * SIDE,
        scratch_shapes=[pltpu.VMEM((ONE, WIDE), jnp.float32)],
        compiler_params=params(),
        cost_estimate=pl.CostEstimate(flops=16_000_000, bytes_accessed=7_000_000, transcendentals=0),
        name="first_merge",
    )(near_part, near_stat, local, *received)


def last_merge_kernel(table, *refs):
    *sources, out = refs
    for slot in range(MB):
        live = table[COUNTS + table[ME]] > slot

        @pl.when(live)
        def _():
            levels = [read_level(r, ROWS, slot, MB) for r in sources]
            parts = [functools.partial(read_part, r, slot) for r in sources]
            value, _ = merge(levels, parts)
            for h in range(HEADS):
                out[slot * BLK : (slot + 1) * BLK, lanes(h)] = value[:, lanes(h)].T.astype(jnp.bfloat16)

        @pl.when(jnp.logical_not(live))
        def _():
            out[slot * BLK : (slot + 1) * BLK, :] = jnp.zeros((BLK, WIDE), jnp.bfloat16)


def last_merge(table, parts):
    vmem = pl.BlockSpec(memory_space=pltpu.VMEM)
    return pl.pallas_call(
        last_merge_kernel,
        in_specs=[pl.BlockSpec(memory_space=pltpu.SMEM)] + [vmem] * len(parts),
        out_specs=vmem,
        out_shape=jax.ShapeDtypeStruct((ROWS, WIDE), jnp.bfloat16),
        compiler_params=params(),
        name="last_merge",
    )(table, *parts)


HEAD_SHARDS = 8


def give(x, k, step):
    pairs = []
    for z in range(SIDE):
        for c in range(SIDE):
            for head in range(HEAD_SHARDS):
                along_x = (head % 2 == 0) == (step == 1)
                to = (z, (c + k) % SIDE) if along_x else ((z + k) % SIDE, c)
                pairs.append(
                    ((z * SIDE + c) * HEAD_SHARDS + head, (to[0] * SIDE + to[1]) * HEAD_SHARDS + head)
                )
    return lax.ppermute(x, ("frame", "head"), pairs)


def fetch(x, k, step):
    return give(x, SIDE - k, step)


ORDER = (1, 3, 2)


def body(
    fresh_queries,
    fresh_keys,
    fresh_values,
    key_cache,
    value_cache,
    masked_blocks,
    masked_count,
    radial_counts,
):
    me = lax.axis_index("frame").astype(jnp.int32)
    core = lax.axis_index("head").astype(jnp.int32) % 2
    table = jnp.concatenate(
        [masked_blocks.reshape(-1), masked_count, radial_counts, me[None], core[None]]
    )
    q = lax.all_to_all(split_heads(fresh_queries[0]), "head", 0, 0, tiled=True).reshape(ROWS, WIDE)
    fresh = lax.all_to_all(
        split_heads(fresh_keys[0], fresh_values[0]), "head", 0, 0, tiled=True
    )
    ring = [q] + [fetch(q, k, 1) for k in range(1, SIDE)]
    full = stack(*ring)
    queries = {k: fetch(full, k, 2) for k in ORDER}
    keys, values = stage(table, fresh, key_cache[0], value_cache[0])
    local = far(table, full, keys, values, 0, 1)
    back = []
    for k in ORDER:
        last = far(table, queries[k], keys, values, k, 0)
        back.append(give(last, k, 2))
    late, _ = lax.optimization_barrier((q, last))
    near_part, near_stat = near(late, keys, values)
    merged = first_merge(near_part, near_stat, local, back)
    final = [merged[0]] + [give(merged[k], k, 1) for k in range(1, SIDE)]
    edited = last_merge(table, final).reshape(8, MB * BLK // 8, WIDE)
    edited = lax.all_to_all(edited, "head", 0, 0, tiled=True)
    return join_heads(edited)[None]


def solution(mesh):
    placed = (
        P("frame", "head", None),
        P("frame", "head", None),
        P("frame", "head", None),
        P("frame", None, "head"),
        P("frame", None, "head"),
        P(),
        P(),
        P(),
    )
    return jax.shard_map(
        body, mesh=mesh, in_specs=placed, out_specs=P("frame", "head", None), check_vma=False
    )
```

```python
import functools
import math

import jax
import jax.numpy as jnp
from jax import lax
from jax.experimental import pallas as pl
from jax.experimental.pallas import tpu as pltpu
from jax.sharding import PartitionSpec as P

HD = 128
BLK = 128
NBLK = 28
MB = 2
CMAX = 3
HEADS = 5
WIDE = HEADS * HD
SIDE = 4
ROWS = MB * BLK
ITEMS = SIDE * MB
STAT = 32
PAY = SIDE * ROWS + STAT
ONE = 16
EXPO = math.log2(math.e) / math.sqrt(HD)
LOW = -1e30
FRAMES = SIDE * SIDE
COUNTS = FRAMES * MB
RADIAL = COUNTS + FRAMES
ME = RADIAL + FRAMES - 1
CORE = ME + 1
VMEM_LIMIT = 16 * 1024 * 1024
STAGE_LIMIT = 42 * 1024 * 1024


def lanes(h):
    return slice(h * HD, (h + 1) * HD)


def params(**kw):
    return pltpu.CompilerParams(vmem_limit_bytes=VMEM_LIMIT, **kw)


def split_kernel(*refs):
    *sources, dst = refs
    for i, src in enumerate(sources):
        rows = src.shape[0]
        for j in range(8):
            dst[j, i * rows : (i + 1) * rows, :] = src[:, j * WIDE : (j + 1) * WIDE]


def split_heads(*arrays):
    rows = sum(a.shape[0] for a in arrays)
    return pl.pallas_call(
        split_kernel,
        out_shape=jax.ShapeDtypeStruct((8, rows, WIDE), jnp.bfloat16),
        compiler_params=params(),
        name="split_heads",
    )(*arrays)


def take_kernel(src, dst):
    rows = dst.shape[0] // src.shape[0]
    for i in range(src.shape[0]):
        dst[i * rows : (i + 1) * rows, :] = src[i, :rows, :]


def take_queries(fresh):
    return pl.pallas_call(
        take_kernel,
        out_shape=jax.ShapeDtypeStruct((ROWS, WIDE), jnp.bfloat16),
        compiler_params=params(),
        name="take_queries",
    )(fresh)


def stack_kernel(count, *refs):
    sources, dst = refs[:count], refs[-1]
    for i, src in enumerate(sources):
        dst[i * ROWS : (i + 1) * ROWS, :] = src[...]


def stack(*arrays, held=()):
    return pl.pallas_call(
        functools.partial(stack_kernel, len(arrays)),
        out_shape=jax.ShapeDtypeStruct((len(arrays) * ROWS, WIDE), jnp.bfloat16),
        compiler_params=params(),
        name="stack",
    )(*arrays, *held)


def join_kernel(src, dst):
    for j in range(8):
        dst[:, j * WIDE : (j + 1) * WIDE] = src[j]


def join_heads(x):
    return pl.pallas_call(
        join_kernel,
        out_shape=jax.ShapeDtypeStruct((x.shape[1], 8 * WIDE), jnp.bfloat16),
        compiler_params=params(),
        name="join_heads",
    )(x)


def fold(x, op, groups):
    rows = x.shape[0] // groups
    out = x[:rows]
    for g in range(1, groups):
        out = op(out, x[g * rows : (g + 1) * rows])
    return out


def col_max(x, groups=8):
    return jnp.max(fold(x, jnp.maximum, groups), axis=0, keepdims=True)


def col_sum(x, groups=8):
    return jnp.sum(fold(x, jnp.add, groups), axis=0, keepdims=True)


NEAR_BLOCKS = 7
NEAR_ROWS = NEAR_BLOCKS * BLK


def eighths(x, op):
    out = x[:8]
    for g in range(1, x.shape[0] // 8):
        out = op(out, x[g * 8 : (g + 1) * 8])
    return out


def stage_kernel(table, fresh_ref, kc_ref, vc_ref, k_out, vt_out, done, vbuf, k_sems, v_sems):
    pieces = NBLK // NEAR_BLOCKS
    part_rows = fresh_ref.shape[1] // 3
    parts = BLK // part_rows
    me = table[ME]

    def rows_of(p):
        return pl.ds(p * NEAR_ROWS, NEAR_ROWS)

    v_copies = [
        pltpu.make_async_copy(vc_ref.at[rows_of(p), :], vbuf.at[rows_of(p), :], v_sems.at[p])
        for p in range(pieces)
    ]
    k_copies = [
        pltpu.make_async_copy(kc_ref.at[rows_of(p), :], k_out.at[rows_of(p), :], k_sems.at[p])
        for p in range(pieces)
    ]
    for copy in v_copies + k_copies:
        copy.start()
    for p in range(pieces):
        v_copies[p].wait()

        def turn(b, carry):
            span = pl.ds(pl.multiple_of(b * BLK, BLK), BLK)
            for h in range(HEADS):
                vt_out[b, lanes(h), :] = vbuf[span, lanes(h)].T
            return carry

        lax.fori_loop(p * NEAR_BLOCKS, (p + 1) * NEAR_BLOCKS, turn, 0)
    for copy in k_copies:
        copy.wait()
    for s in range(MB):
        spot = table[me * MB + s]

        @pl.when(table[COUNTS + me] > s)
        def _():
            for i in range(parts):
                rows = pl.ds(pl.multiple_of(spot * BLK + i * part_rows, part_rows), part_rows)
                k_out[rows, :] = fresh_ref[s * parts + i, part_rows : 2 * part_rows, :]
            for h in range(HEADS):
                tile = jnp.concatenate(
                    [fresh_ref[s * parts + i, 2 * part_rows :, lanes(h)] for i in range(parts)], axis=0
                )
                vt_out[spot, lanes(h), :] = tile.T

    done[...] = jnp.zeros_like(done)


def stage(table, fresh, key_cache, value_cache):
    vmem = pl.BlockSpec(memory_space=pltpu.VMEM)
    hbm = pl.BlockSpec(memory_space=pltpu.HBM)
    pieces = NBLK // NEAR_BLOCKS
    return pl.pallas_call(
        stage_kernel,
        in_specs=[pl.BlockSpec(memory_space=pltpu.SMEM), vmem, hbm, hbm],
        out_specs=[vmem] * 3,
        scratch_shapes=[
            pltpu.VMEM((NBLK * BLK, WIDE), jnp.bfloat16),
            pltpu.SemaphoreType.DMA((pieces,)),
            pltpu.SemaphoreType.DMA((pieces,)),
        ],
        out_shape=[
            jax.ShapeDtypeStruct((NBLK * BLK, WIDE), jnp.bfloat16),
            jax.ShapeDtypeStruct((NBLK, WIDE, BLK), jnp.bfloat16),
            jax.ShapeDtypeStruct((8, BLK), jnp.float32),
        ],
        compiler_params=pltpu.CompilerParams(vmem_limit_bytes=STAGE_LIMIT),
        cost_estimate=pl.CostEstimate(flops=0, bytes_accessed=15_000_000, transcendentals=0),
        name="stage",
    )(table, fresh, key_cache, value_cache)


def near_kernel(q_ref, k_ref, vt_ref, o_out, s_out, acc, top, tot, sbuf, pbuf):
    acc[...] = jnp.zeros_like(acc)
    top[...] = jnp.full_like(top, LOW)
    tot[...] = jnp.zeros_like(tot)

    def chunk(step, carry):
        def score(h):
            high = None
            for b in range(NEAR_BLOCKS):
                part = lax.dot_general(
                    k_ref[pl.ds(pl.multiple_of((step * NEAR_BLOCKS + b) * BLK, BLK), BLK), lanes(h)],
                    q_ref[:, lanes(h)],
                    (((1,), (1,)), ((), ())),
                    preferred_element_type=jnp.float32,
                )
                sbuf[h % 2, b * BLK : (b + 1) * BLK, :] = part
                peak = eighths(part, jnp.maximum)
                high = peak if high is None else jnp.maximum(high, peak)
            return jnp.max(high, axis=0, keepdims=True)

        ahead = score(0)
        for h in range(HEADS):
            high = ahead
            if h + 1 < HEADS:
                ahead = score(h + 1)
            old = top[h : h + 1, :]
            new = jnp.maximum(old, high)
            shrink = jnp.exp2((old - new) * EXPO)
            top[h : h + 1, :] = new
            added = None
            for b in range(NEAR_BLOCKS):
                weights = jnp.exp2((sbuf[h % 2, b * BLK : (b + 1) * BLK, :] - new) * EXPO)
                pbuf[h % 2, b * BLK : (b + 1) * BLK, :] = weights.astype(jnp.bfloat16)
                part = eighths(weights, jnp.add)
                added = part if added is None else added + part
            tot[h : h + 1, :] = tot[h : h + 1, :] * shrink + jnp.sum(added, axis=0, keepdims=True)
            values = jnp.concatenate(
                [vt_ref[step * NEAR_BLOCKS + b, lanes(h), :] for b in range(NEAR_BLOCKS)], axis=1
            )
            acc[h] = acc[h] * shrink + jnp.dot(
                values, pbuf[h % 2], preferred_element_type=jnp.float32
            )
        return carry

    lax.fori_loop(0, NBLK // NEAR_BLOCKS, chunk, 0)
    for h in range(HEADS):
        total = tot[h : h + 1, :]
        part = acc[h] * (1.0 / total)
        level = top[h : h + 1, :] * EXPO + jnp.log2(total)
        for s in range(MB):
            o_out[s, :, lanes(h)] = part[:, s * BLK : (s + 1) * BLK].astype(jnp.bfloat16)
            s_out[s : s + 1, lanes(h)] = level[:, s * BLK : (s + 1) * BLK]


def near(q, keys, values):
    rows = MB * BLK
    vmem = pl.BlockSpec(memory_space=pltpu.VMEM)
    return pl.pallas_call(
        near_kernel,
        in_specs=[vmem] * 3,
        out_specs=[vmem] * 2,
        scratch_shapes=[
            pltpu.VMEM((HEADS, HD, rows), jnp.float32),
            pltpu.VMEM((8, rows), jnp.float32),
            pltpu.VMEM((8, rows), jnp.float32),
            pltpu.VMEM((2, NEAR_ROWS, rows), jnp.float32),
            pltpu.VMEM((2, NEAR_ROWS, rows), jnp.bfloat16),
        ],
        out_shape=[
            jax.ShapeDtypeStruct((MB, HD, WIDE), jnp.bfloat16),
            jax.ShapeDtypeStruct((8, WIDE), jnp.float32),
        ],
        compiler_params=params(),
        cost_estimate=pl.CostEstimate(
            flops=100_000_000, bytes_accessed=400_000, transcendentals=0
        ),
        name="near",
    )(q, keys, values)


def put_stats(stat, index, apart, h, level):
    high = level.astype(jnp.bfloat16).astype(jnp.float32)
    rest = level - high
    mid = rest.astype(jnp.bfloat16).astype(jnp.float32)
    row = lax.broadcasted_iota(jnp.int32, (stat.shape[0], HD), 0) - index
    tile = stat[:, lanes(h)]
    for place, piece in ((0, high), (apart, mid), (2 * apart, rest - mid)):
        tile = jnp.where(row == place, piece, tile)
    stat[:, lanes(h)] = tile


def frame_at(table, item, shift):
    me = table[ME]
    odd = table[CORE] == 1
    z = lax.shift_right_logical(me, 2) + jnp.where(odd, item, shift)
    x = (me & (SIDE - 1)) + jnp.where(odd, shift, item)
    return (z & (SIDE - 1)) * SIDE + (x & (SIDE - 1))


def far_kernel(shift, skip, table, q_ref, keys, values, out, stat):
    stat[...] = jnp.zeros_like(stat)
    me = table[ME]

    def step(i, carry):
        slot = i & (MB - 1)
        frame = frame_at(table, lax.shift_right_logical(i, 1), shift)
        count = table[RADIAL + jnp.maximum(jnp.abs(frame - me) - 1, 0)]
        start = table[frame * MB + slot] - lax.shift_right_logical(count, 1)
        start = jnp.where(start < 0, start + NBLK, start)
        spots = [start + j for j in range(CMAX)]
        spots = [jnp.where(spot >= NBLK, spot - NBLK, spot) for spot in spots]
        count = jnp.where(table[COUNTS + frame] > slot, count, 0)
        rows = pl.ds(pl.multiple_of(i * BLK, BLK), BLK)
        for n in range(1, CMAX + 1):

            @pl.when(count == n)
            def _():
                def score(h):
                    return [
                        lax.dot_general(
                            keys[pl.ds(pl.multiple_of(spots[j] * BLK, BLK), BLK), lanes(h)],
                            q_ref[rows, lanes(h)],
                            (((1,), (1,)), ((), ())),
                            preferred_element_type=jnp.float32,
                        )
                        for j in range(n)
                    ]

                scores = [score(h) for h in range(HEADS)]
                tops, totals, probs = [], [], []
                for h in range(HEADS):
                    peaks = [eighths(x, jnp.maximum) for x in scores[h]]
                    top = jnp.max(functools.reduce(jnp.maximum, peaks), axis=0, keepdims=True)
                    weights = [jnp.exp2((x - top) * EXPO) for x in scores[h]]
                    sums = [eighths(x, jnp.add) for x in weights]
                    totals.append(jnp.sum(functools.reduce(jnp.add, sums), axis=0, keepdims=True))
                    tops.append(top)
                    probs.append(jnp.concatenate([x.astype(jnp.bfloat16) for x in weights], axis=0))
                parts = [
                    jnp.dot(
                        jnp.concatenate([values[spots[j], lanes(h), :] for j in range(n)], axis=1),
                        probs[h],
                        preferred_element_type=jnp.float32,
                    )
                    for h in range(HEADS)
                ]
                for h in range(HEADS):
                    out[rows, lanes(h)] = (parts[h] * (1.0 / totals[h])).astype(jnp.bfloat16)
                    put_stats(stat, i, ITEMS, h, tops[h] * EXPO + jnp.log2(totals[h]))

        return carry

    lax.fori_loop(skip * MB, ITEMS, step, 0)
    out[SIDE * ROWS :, :] = stat[...].astype(jnp.bfloat16)


def far(table, queries, keys, values, shift, skip):
    smem = pl.BlockSpec(memory_space=pltpu.SMEM)
    vmem = pl.BlockSpec(memory_space=pltpu.VMEM)
    return pl.pallas_call(
        functools.partial(far_kernel, shift, skip),
        in_specs=[smem] + [vmem] * 3,
        out_specs=vmem,
        scratch_shapes=[pltpu.VMEM((STAT, WIDE), jnp.float32)],
        out_shape=jax.ShapeDtypeStruct((PAY, WIDE), jnp.bfloat16),
        compiler_params=params(),
        cost_estimate=pl.CostEstimate(
            flops=100_000_000, bytes_accessed=400_000, transcendentals=0
        ),
        name="far",
    )(table, queries, keys, values)


def read_level(ref, base, index, apart):
    tile = ref[base:, :].astype(jnp.float32)
    return (
        tile[index : index + 1]
        + tile[apart + index : apart + index + 1]
        + tile[2 * apart + index : 2 * apart + index + 1]
    )


def read_part(ref, index):
    return ref[index * BLK : (index + 1) * BLK, :].astype(jnp.float32)


def merge(levels, parts):
    top = functools.reduce(jnp.maximum, levels)
    shares = [jnp.exp2(level - top) for level in levels]
    total = functools.reduce(jnp.add, shares)
    scale = 1.0 / total
    out = None
    for share, part in zip(shares, parts):
        term = part() * (share * scale)
        out = term if out is None else out + term
    return out, top + jnp.log2(total)


def first_merge_kernel(near_ref, near_stat, local, one, two, three, *outs):
    *outs, stat = outs
    for d in range(SIDE):
        stat[...] = jnp.zeros_like(stat)
        for slot in range(MB):
            index = d * MB + slot
            sources = [one, two, three] + ([local] if d else [])
            levels = [read_level(r, SIDE * ROWS, index, ITEMS) for r in sources]
            parts = [functools.partial(read_part, r, index) for r in sources]
            if d == 0:
                levels.append(near_stat[slot : slot + 1, :])
                parts.append(lambda: near_ref[slot].astype(jnp.float32))
            value, level = merge(levels, parts)
            outs[d][slot * BLK : (slot + 1) * BLK, :] = value.astype(jnp.bfloat16)
            for h in range(HEADS):
                put_stats(stat, slot, MB, h, level[:, lanes(h)])
        outs[d][ROWS:, :] = stat[...].astype(jnp.bfloat16)


def first_merge(near_part, near_stat, local, received):
    return pl.pallas_call(
        first_merge_kernel,
        out_shape=[jax.ShapeDtypeStruct((ROWS + ONE, WIDE), jnp.bfloat16)] * SIDE,
        scratch_shapes=[pltpu.VMEM((ONE, WIDE), jnp.float32)],
        compiler_params=params(),
        cost_estimate=pl.CostEstimate(flops=16_000_000, bytes_accessed=7_000_000, transcendentals=0),
        name="first_merge",
    )(near_part, near_stat, local, *received)


def last_merge_kernel(table, *refs):
    *sources, out = refs
    for slot in range(MB):
        live = table[COUNTS + table[ME]] > slot

        @pl.when(live)
        def _():
            levels = [read_level(r, ROWS, slot, MB) for r in sources]
            parts = [functools.partial(read_part, r, slot) for r in sources]
            value, _ = merge(levels, parts)
            for h in range(HEADS):
                out[slot * BLK : (slot + 1) * BLK, lanes(h)] = value[:, lanes(h)].T.astype(jnp.bfloat16)

        @pl.when(jnp.logical_not(live))
        def _():
            out[slot * BLK : (slot + 1) * BLK, :] = jnp.zeros((BLK, WIDE), jnp.bfloat16)


def last_merge(table, parts):
    vmem = pl.BlockSpec(memory_space=pltpu.VMEM)
    return pl.pallas_call(
        last_merge_kernel,
        in_specs=[pl.BlockSpec(memory_space=pltpu.SMEM)] + [vmem] * len(parts),
        out_specs=vmem,
        out_shape=jax.ShapeDtypeStruct((ROWS, WIDE), jnp.bfloat16),
        compiler_params=params(),
        name="last_merge",
    )(table, *parts)


HEAD_SHARDS = 8


def give(x, k, step):
    pairs = []
    for z in range(SIDE):
        for c in range(SIDE):
            for head in range(HEAD_SHARDS):
                along_x = (head % 2 == 0) == (step == 1)
                to = (z, (c + k) % SIDE) if along_x else ((z + k) % SIDE, c)
                pairs.append(
                    ((z * SIDE + c) * HEAD_SHARDS + head, (to[0] * SIDE + to[1]) * HEAD_SHARDS + head)
                )
    return lax.ppermute(x, ("frame", "head"), pairs)


def fetch(x, k, step):
    return give(x, SIDE - k, step)


ORDER = (1, 3, 2)


def body(
    fresh_queries,
    fresh_keys,
    fresh_values,
    key_cache,
    value_cache,
    masked_blocks,
    masked_count,
    radial_counts,
):
    me = lax.axis_index("frame").astype(jnp.int32)
    core = lax.axis_index("head").astype(jnp.int32) % 2
    table = jnp.concatenate(
        [masked_blocks.reshape(-1), masked_count, radial_counts, me[None], core[None]]
    )
    fresh = lax.all_to_all(
        split_heads(fresh_queries[0], fresh_keys[0], fresh_values[0]), "head", 0, 0, tiled=True
    )
    q = take_queries(fresh)
    ring = [q] + [fetch(q, k, 1) for k in range(1, SIDE)]
    keys, values, staged = stage(table, fresh, key_cache[0], value_cache[0])
    full = stack(*ring, held=(staged,))
    queries = {k: fetch(full, k, 2) for k in ORDER[:2]}
    local = far(table, full, keys, values, 0, 1)
    late, queries[1], local = lax.optimization_barrier((full, queries[1], local))
    queries[2] = fetch(late, 2, 2)
    back = []
    for k in ORDER:
        last = far(table, queries[k], keys, values, k, 0)
        if k == ORDER[-1]:
            late, last = lax.optimization_barrier((q, last))
        back.append(give(last, k, 2))
    near_part, near_stat = near(late, keys, values)
    merged = first_merge(near_part, near_stat, local, back)
    final = [merged[0]] + [give(merged[k], k, 1) for k in range(1, SIDE)]
    edited = last_merge(table, final).reshape(8, MB * BLK // 8, WIDE)
    edited = lax.all_to_all(edited, "head", 0, 0, tiled=True)
    return join_heads(edited)[None]


def solution(mesh):
    placed = (
        P("frame", "head", None),
        P("frame", "head", None),
        P("frame", "head", None),
        P("frame", None, "head"),
        P("frame", None, "head"),
        P(),
        P(),
        P(),
    )
    return jax.shard_map(
        body, mesh=mesh, in_specs=placed, out_specs=P("frame", "head", None), check_vma=False
    )
```

```python
import functools
import math

import jax
import jax.numpy as jnp
from jax import lax
from jax.experimental import pallas as pl
from jax.experimental.pallas import tpu as pltpu
from jax.sharding import PartitionSpec as P

HD = 128
BLK = 128
NBLK = 28
MB = 2
CMAX = 3
HEADS = 5
WIDE = HEADS * HD
SIDE = 4
ROWS = MB * BLK
ITEMS = SIDE * MB
STAT = 32
PAY = SIDE * ROWS + STAT
ONE = 16
EXPO = math.log2(math.e) / math.sqrt(HD)
LOW = -1e30
FRAMES = SIDE * SIDE
COUNTS = FRAMES * MB
RADIAL = COUNTS + FRAMES
ME = RADIAL + FRAMES - 1
CORE = ME + 1
VMEM_LIMIT = 16 * 1024 * 1024
STAGE_LIMIT = 42 * 1024 * 1024


def lanes(h):
    return slice(h * HD, (h + 1) * HD)


def params(**kw):
    return pltpu.CompilerParams(vmem_limit_bytes=VMEM_LIMIT, **kw)


def split_kernel(*refs):
    *sources, dst = refs
    for i, src in enumerate(sources):
        rows = src.shape[0]
        for j in range(8):
            dst[j, i * rows : (i + 1) * rows, :] = src[:, j * WIDE : (j + 1) * WIDE]


def split_heads(*arrays):
    rows = sum(a.shape[0] for a in arrays)
    return pl.pallas_call(
        split_kernel,
        out_shape=jax.ShapeDtypeStruct((8, rows, WIDE), jnp.bfloat16),
        compiler_params=params(),
        name="split_heads",
    )(*arrays)


def take_kernel(src, dst):
    rows = dst.shape[0] // src.shape[0]
    for i in range(src.shape[0]):
        dst[i * rows : (i + 1) * rows, :] = src[i, :rows, :]


def take_queries(fresh):
    return pl.pallas_call(
        take_kernel,
        out_shape=jax.ShapeDtypeStruct((ROWS, WIDE), jnp.bfloat16),
        compiler_params=params(),
        name="take_queries",
    )(fresh)


def stack_kernel(count, *refs):
    sources, dst = refs[:count], refs[-1]
    for i, src in enumerate(sources):
        dst[i * ROWS : (i + 1) * ROWS, :] = src[...]


def stack(*arrays, held=()):
    return pl.pallas_call(
        functools.partial(stack_kernel, len(arrays)),
        out_shape=jax.ShapeDtypeStruct((len(arrays) * ROWS, WIDE), jnp.bfloat16),
        compiler_params=params(),
        name="stack",
    )(*arrays, *held)


def join_kernel(src, dst):
    for j in range(8):
        dst[:, j * WIDE : (j + 1) * WIDE] = src[j]


def join_heads(x):
    return pl.pallas_call(
        join_kernel,
        out_shape=jax.ShapeDtypeStruct((x.shape[1], 8 * WIDE), jnp.bfloat16),
        compiler_params=params(),
        name="join_heads",
    )(x)


def fold(x, op, groups):
    rows = x.shape[0] // groups
    out = x[:rows]
    for g in range(1, groups):
        out = op(out, x[g * rows : (g + 1) * rows])
    return out


def col_max(x, groups=8):
    return jnp.max(fold(x, jnp.maximum, groups), axis=0, keepdims=True)


def col_sum(x, groups=8):
    return jnp.sum(fold(x, jnp.add, groups), axis=0, keepdims=True)


NEAR_BLOCKS = 7
NEAR_ROWS = NEAR_BLOCKS * BLK


def eighths(x, op):
    out = x[:8]
    for g in range(1, x.shape[0] // 8):
        out = op(out, x[g * 8 : (g + 1) * 8])
    return out


def stage_kernel(table, fresh_ref, kc_ref, vc_ref, k_out, vt_out, done, vbuf, k_sems, v_sems):
    pieces = NBLK // NEAR_BLOCKS
    part_rows = fresh_ref.shape[1] // 3
    parts = BLK // part_rows
    me = table[ME]

    def rows_of(p):
        return pl.ds(p * NEAR_ROWS, NEAR_ROWS)

    v_copies = [
        pltpu.make_async_copy(vc_ref.at[rows_of(p), :], vbuf.at[rows_of(p), :], v_sems.at[p])
        for p in range(pieces)
    ]
    k_copies = [
        pltpu.make_async_copy(kc_ref.at[rows_of(p), :], k_out.at[rows_of(p), :], k_sems.at[p])
        for p in range(pieces)
    ]
    for copy in v_copies + k_copies:
        copy.start()
    for p in range(pieces):
        v_copies[p].wait()

        def turn(b, carry):
            span = pl.ds(pl.multiple_of(b * BLK, BLK), BLK)
            for h in range(HEADS):
                vt_out[b, lanes(h), :] = vbuf[span, lanes(h)].T
            return carry

        lax.fori_loop(p * NEAR_BLOCKS, (p + 1) * NEAR_BLOCKS, turn, 0)
    for copy in k_copies:
        copy.wait()
    for s in range(MB):
        spot = table[me * MB + s]

        @pl.when(table[COUNTS + me] > s)
        def _():
            for i in range(parts):
                rows = pl.ds(pl.multiple_of(spot * BLK + i * part_rows, part_rows), part_rows)
                k_out[rows, :] = fresh_ref[s * parts + i, part_rows : 2 * part_rows, :]
            for h in range(HEADS):
                tile = jnp.concatenate(
                    [fresh_ref[s * parts + i, 2 * part_rows :, lanes(h)] for i in range(parts)], axis=0
                )
                vt_out[spot, lanes(h), :] = tile.T

    done[...] = jnp.zeros_like(done)


def stage(table, fresh, key_cache, value_cache):
    vmem = pl.BlockSpec(memory_space=pltpu.VMEM)
    hbm = pl.BlockSpec(memory_space=pltpu.HBM)
    pieces = NBLK // NEAR_BLOCKS
    return pl.pallas_call(
        stage_kernel,
        in_specs=[pl.BlockSpec(memory_space=pltpu.SMEM), vmem, hbm, hbm],
        out_specs=[vmem] * 3,
        scratch_shapes=[
            pltpu.VMEM((NBLK * BLK, WIDE), jnp.bfloat16),
            pltpu.SemaphoreType.DMA((pieces,)),
            pltpu.SemaphoreType.DMA((pieces,)),
        ],
        out_shape=[
            jax.ShapeDtypeStruct((NBLK * BLK, WIDE), jnp.bfloat16),
            jax.ShapeDtypeStruct((NBLK, WIDE, BLK), jnp.bfloat16),
            jax.ShapeDtypeStruct((8, BLK), jnp.float32),
        ],
        compiler_params=pltpu.CompilerParams(vmem_limit_bytes=STAGE_LIMIT),
        cost_estimate=pl.CostEstimate(flops=0, bytes_accessed=15_000_000, transcendentals=0),
        name="stage",
    )(table, fresh, key_cache, value_cache)


def near_kernel(q_ref, k_ref, vt_ref, o_out, s_out, acc, top, tot, sbuf, pbuf):
    acc[...] = jnp.zeros_like(acc)
    top[...] = jnp.full_like(top, LOW)
    tot[...] = jnp.zeros_like(tot)

    def chunk(step, carry):
        def score(h):
            high = None
            for b in range(NEAR_BLOCKS):
                part = lax.dot_general(
                    k_ref[pl.ds(pl.multiple_of((step * NEAR_BLOCKS + b) * BLK, BLK), BLK), lanes(h)],
                    q_ref[:, lanes(h)],
                    (((1,), (1,)), ((), ())),
                    preferred_element_type=jnp.float32,
                )
                sbuf[h % 2, b * BLK : (b + 1) * BLK, :] = part
                peak = eighths(part, jnp.maximum)
                high = peak if high is None else jnp.maximum(high, peak)
            return jnp.max(high, axis=0, keepdims=True)

        ahead = score(0)
        for h in range(HEADS):
            high = ahead
            if h + 1 < HEADS:
                ahead = score(h + 1)
            old = top[h : h + 1, :]
            new = jnp.maximum(old, high)
            shrink = jnp.exp2((old - new) * EXPO)
            top[h : h + 1, :] = new
            added = None
            for b in range(NEAR_BLOCKS):
                weights = jnp.exp2((sbuf[h % 2, b * BLK : (b + 1) * BLK, :] - new) * EXPO)
                pbuf[h % 2, b * BLK : (b + 1) * BLK, :] = weights.astype(jnp.bfloat16)
                part = eighths(weights, jnp.add)
                added = part if added is None else added + part
            tot[h : h + 1, :] = tot[h : h + 1, :] * shrink + jnp.sum(added, axis=0, keepdims=True)
            values = jnp.concatenate(
                [vt_ref[step * NEAR_BLOCKS + b, lanes(h), :] for b in range(NEAR_BLOCKS)], axis=1
            )
            acc[h] = acc[h] * shrink + jnp.dot(
                values, pbuf[h % 2], preferred_element_type=jnp.float32
            )
        return carry

    lax.fori_loop(0, NBLK // NEAR_BLOCKS, chunk, 0)
    for h in range(HEADS):
        total = tot[h : h + 1, :]
        part = acc[h] * (1.0 / total)
        level = top[h : h + 1, :] * EXPO + jnp.log2(total)
        for s in range(MB):
            o_out[s, :, lanes(h)] = part[:, s * BLK : (s + 1) * BLK].astype(jnp.bfloat16)
            s_out[s : s + 1, lanes(h)] = level[:, s * BLK : (s + 1) * BLK]


def near(q, keys, values):
    rows = MB * BLK
    vmem = pl.BlockSpec(memory_space=pltpu.VMEM)
    return pl.pallas_call(
        near_kernel,
        in_specs=[vmem] * 3,
        out_specs=[vmem] * 2,
        scratch_shapes=[
            pltpu.VMEM((HEADS, HD, rows), jnp.float32),
            pltpu.VMEM((8, rows), jnp.float32),
            pltpu.VMEM((8, rows), jnp.float32),
            pltpu.VMEM((2, NEAR_ROWS, rows), jnp.float32),
            pltpu.VMEM((2, NEAR_ROWS, rows), jnp.bfloat16),
        ],
        out_shape=[
            jax.ShapeDtypeStruct((MB, HD, WIDE), jnp.bfloat16),
            jax.ShapeDtypeStruct((8, WIDE), jnp.float32),
        ],
        compiler_params=params(),
        cost_estimate=pl.CostEstimate(
            flops=100_000_000, bytes_accessed=400_000, transcendentals=0
        ),
        name="near",
    )(q, keys, values)


def put_stats(stat, index, apart, h, level):
    high = level.astype(jnp.bfloat16).astype(jnp.float32)
    rest = level - high
    mid = rest.astype(jnp.bfloat16).astype(jnp.float32)
    row = lax.broadcasted_iota(jnp.int32, (stat.shape[0], HD), 0) - index
    tile = stat[:, lanes(h)]
    for place, piece in ((0, high), (apart, mid), (2 * apart, rest - mid)):
        tile = jnp.where(row == place, piece, tile)
    stat[:, lanes(h)] = tile


def frame_at(table, item, shift):
    me = table[ME]
    odd = table[CORE] == 1
    z = lax.shift_right_logical(me, 2) + jnp.where(odd, item, shift)
    x = (me & (SIDE - 1)) + jnp.where(odd, shift, item)
    return (z & (SIDE - 1)) * SIDE + (x & (SIDE - 1))


def far_kernel(shift, skip, table, q_ref, keys, values, out, stat):
    stat[...] = jnp.zeros_like(stat)
    me = table[ME]

    def step(i, carry):
        slot = i & (MB - 1)
        frame = frame_at(table, lax.shift_right_logical(i, 1), shift)
        count = table[RADIAL + jnp.maximum(jnp.abs(frame - me) - 1, 0)]
        start = table[frame * MB + slot] - lax.shift_right_logical(count, 1)
        start = jnp.where(start < 0, start + NBLK, start)
        spots = [start + j for j in range(CMAX)]
        spots = [jnp.where(spot >= NBLK, spot - NBLK, spot) for spot in spots]
        count = jnp.where(table[COUNTS + frame] > slot, count, 0)
        rows = pl.ds(pl.multiple_of(i * BLK, BLK), BLK)
        for n in range(1, CMAX + 1):

            @pl.when(count == n)
            def _():
                def score(h):
                    return [
                        lax.dot_general(
                            keys[pl.ds(pl.multiple_of(spots[j] * BLK, BLK), BLK), lanes(h)],
                            q_ref[rows, lanes(h)],
                            (((1,), (1,)), ((), ())),
                            preferred_element_type=jnp.float32,
                        )
                        for j in range(n)
                    ]

                scores = [score(h) for h in range(HEADS)]
                tops, totals, probs = [], [], []
                for h in range(HEADS):
                    peaks = [eighths(x, jnp.maximum) for x in scores[h]]
                    top = jnp.max(functools.reduce(jnp.maximum, peaks), axis=0, keepdims=True)
                    weights = [jnp.exp2((x - top) * EXPO) for x in scores[h]]
                    sums = [eighths(x, jnp.add) for x in weights]
                    totals.append(jnp.sum(functools.reduce(jnp.add, sums), axis=0, keepdims=True))
                    tops.append(top)
                    probs.append(jnp.concatenate([x.astype(jnp.bfloat16) for x in weights], axis=0))
                parts = [
                    jnp.dot(
                        jnp.concatenate([values[spots[j], lanes(h), :] for j in range(n)], axis=1),
                        probs[h],
                        preferred_element_type=jnp.float32,
                    )
                    for h in range(HEADS)
                ]
                for h in range(HEADS):
                    out[rows, lanes(h)] = (parts[h] * (1.0 / totals[h])).astype(jnp.bfloat16)
                    put_stats(stat, i, ITEMS, h, tops[h] * EXPO + jnp.log2(totals[h]))

        return carry

    lax.fori_loop(skip * MB, ITEMS, step, 0)
    out[SIDE * ROWS :, :] = stat[...].astype(jnp.bfloat16)


def far(table, queries, keys, values, shift, skip):
    smem = pl.BlockSpec(memory_space=pltpu.SMEM)
    vmem = pl.BlockSpec(memory_space=pltpu.VMEM)
    return pl.pallas_call(
        functools.partial(far_kernel, shift, skip),
        in_specs=[smem] + [vmem] * 3,
        out_specs=vmem,
        scratch_shapes=[pltpu.VMEM((STAT, WIDE), jnp.float32)],
        out_shape=jax.ShapeDtypeStruct((PAY, WIDE), jnp.bfloat16),
        compiler_params=params(),
        cost_estimate=pl.CostEstimate(
            flops=100_000_000, bytes_accessed=400_000, transcendentals=0
        ),
        name="far",
    )(table, queries, keys, values)


def read_level(ref, base, index, apart):
    tile = ref[base:, :].astype(jnp.float32)
    return (
        tile[index : index + 1]
        + tile[apart + index : apart + index + 1]
        + tile[2 * apart + index : 2 * apart + index + 1]
    )


def read_part(ref, index):
    return ref[index * BLK : (index + 1) * BLK, :].astype(jnp.float32)


def merge(levels, parts):
    top = functools.reduce(jnp.maximum, levels)
    shares = [jnp.exp2(level - top) for level in levels]
    total = functools.reduce(jnp.add, shares)
    scale = 1.0 / total
    out = None
    for share, part in zip(shares, parts):
        term = part() * (share * scale)
        out = term if out is None else out + term
    return out, top + jnp.log2(total)


def first_merge_kernel(near_ref, near_stat, local, one, two, three, *outs):
    *outs, stat = outs
    for d in range(SIDE):
        stat[...] = jnp.zeros_like(stat)
        for slot in range(MB):
            index = d * MB + slot
            sources = [one, two, three] + ([local] if d else [])
            levels = [read_level(r, SIDE * ROWS, index, ITEMS) for r in sources]
            parts = [functools.partial(read_part, r, index) for r in sources]
            if d == 0:
                levels.append(near_stat[slot : slot + 1, :])
                parts.append(lambda: near_ref[slot].astype(jnp.float32))
            value, level = merge(levels, parts)
            outs[d][slot * BLK : (slot + 1) * BLK, :] = value.astype(jnp.bfloat16)
            for h in range(HEADS):
                put_stats(stat, slot, MB, h, level[:, lanes(h)])
        outs[d][ROWS:, :] = stat[...].astype(jnp.bfloat16)


def first_merge(near_part, near_stat, local, received):
    return pl.pallas_call(
        first_merge_kernel,
        out_shape=[jax.ShapeDtypeStruct((ROWS + ONE, WIDE), jnp.bfloat16)] * SIDE,
        scratch_shapes=[pltpu.VMEM((ONE, WIDE), jnp.float32)],
        compiler_params=params(),
        cost_estimate=pl.CostEstimate(flops=16_000_000, bytes_accessed=7_000_000, transcendentals=0),
        name="first_merge",
    )(near_part, near_stat, local, *received)


def last_merge_kernel(table, *refs):
    *sources, out = refs
    for slot in range(MB):
        live = table[COUNTS + table[ME]] > slot

        @pl.when(live)
        def _():
            levels = [read_level(r, ROWS, slot, MB) for r in sources]
            parts = [functools.partial(read_part, r, slot) for r in sources]
            value, _ = merge(levels, parts)
            for h in range(HEADS):
                out[slot * BLK : (slot + 1) * BLK, lanes(h)] = value[:, lanes(h)].T.astype(jnp.bfloat16)

        @pl.when(jnp.logical_not(live))
        def _():
            out[slot * BLK : (slot + 1) * BLK, :] = jnp.zeros((BLK, WIDE), jnp.bfloat16)


def last_merge(table, parts):
    vmem = pl.BlockSpec(memory_space=pltpu.VMEM)
    return pl.pallas_call(
        last_merge_kernel,
        in_specs=[pl.BlockSpec(memory_space=pltpu.SMEM)] + [vmem] * len(parts),
        out_specs=vmem,
        out_shape=jax.ShapeDtypeStruct((ROWS, WIDE), jnp.bfloat16),
        compiler_params=params(),
        name="last_merge",
    )(table, *parts)


HEAD_SHARDS = 8


def give(x, k, step):
    pairs = []
    for z in range(SIDE):
        for c in range(SIDE):
            for head in range(HEAD_SHARDS):
                along_x = (head % 2 == 0) == (step == 1)
                to = (z, (c + k) % SIDE) if along_x else ((z + k) % SIDE, c)
                pairs.append(
                    ((z * SIDE + c) * HEAD_SHARDS + head, (to[0] * SIDE + to[1]) * HEAD_SHARDS + head)
                )
    return lax.ppermute(x, ("frame", "head"), pairs)


def fetch(x, k, step):
    return give(x, SIDE - k, step)


ORDER = (2, 1, 3)


def body(
    fresh_queries,
    fresh_keys,
    fresh_values,
    key_cache,
    value_cache,
    masked_blocks,
    masked_count,
    radial_counts,
):
    me = lax.axis_index("frame").astype(jnp.int32)
    core = lax.axis_index("head").astype(jnp.int32) % 2
    table = jnp.concatenate(
        [masked_blocks.reshape(-1), masked_count, radial_counts, me[None], core[None]]
    )
    fresh = lax.all_to_all(
        split_heads(fresh_queries[0], fresh_keys[0], fresh_values[0]), "head", 0, 0, tiled=True
    )
    q = take_queries(fresh)
    ring = [q] + [fetch(q, k, 1) for k in range(1, SIDE)]
    keys, values, staged = stage(table, fresh, key_cache[0], value_cache[0])
    full = stack(*ring, held=(staged,))
    queries = {k: fetch(full, k, 2) for k in (2, 1, 3)}
    near_part, near_stat = near(q, keys, values)
    local = far(table, full, keys, values, 0, 1)
    queries[2], near_stat, local = lax.optimization_barrier((queries[2], near_stat, local))
    back = []
    for k in ORDER:
        back.append(give(far(table, queries[k], keys, values, k, 0), k, 2))
    merged = first_merge(near_part, near_stat, local, back)
    final = [merged[0]] + [give(merged[k], k, 1) for k in range(1, SIDE)]
    edited = last_merge(table, final).reshape(8, MB * BLK // 8, WIDE)
    edited = lax.all_to_all(edited, "head", 0, 0, tiled=True)
    return join_heads(edited)[None]


def solution(mesh):
    placed = (
        P("frame", "head", None),
        P("frame", "head", None),
        P("frame", "head", None),
        P("frame", None, "head"),
        P("frame", None, "head"),
        P(),
        P(),
        P(),
    )
    return jax.shard_map(
        body, mesh=mesh, in_specs=placed, out_specs=P("frame", "head", None), check_vma=False
    )
```

```python
import functools
import math

import jax
import jax.numpy as jnp
from jax import lax
from jax.experimental import pallas as pl
from jax.experimental.pallas import tpu as pltpu
from jax.sharding import PartitionSpec as P

HD = 128
BLK = 128
NBLK = 28
MB = 2
CMAX = 3
HEADS = 5
WIDE = HEADS * HD
SIDE = 4
ROWS = MB * BLK
ITEMS = SIDE * MB
STAT = 32
PAY = SIDE * ROWS + STAT
ONE = 16
EXPO = math.log2(math.e) / math.sqrt(HD)
LOW = -1e30
FRAMES = SIDE * SIDE
COUNTS = FRAMES * MB
RADIAL = COUNTS + FRAMES
ME = RADIAL + FRAMES - 1
CORE = ME + 1
VMEM_LIMIT = 16 * 1024 * 1024
STAGE_LIMIT = 42 * 1024 * 1024


def lanes(h):
    return slice(h * HD, (h + 1) * HD)


def params(**kw):
    return pltpu.CompilerParams(vmem_limit_bytes=VMEM_LIMIT, **kw)


def split_kernel(*refs):
    *sources, dst = refs
    for i, src in enumerate(sources):
        rows = src.shape[0]
        for j in range(8):
            dst[j, i * rows : (i + 1) * rows, :] = src[:, j * WIDE : (j + 1) * WIDE]


def split_heads(*arrays):
    rows = sum(a.shape[0] for a in arrays)
    return pl.pallas_call(
        split_kernel,
        out_shape=jax.ShapeDtypeStruct((8, rows, WIDE), jnp.bfloat16),
        compiler_params=params(),
        name="split_heads",
    )(*arrays)


def stack_kernel(*refs):
    *sources, dst = refs
    for i, src in enumerate(sources):
        dst[i * ROWS : (i + 1) * ROWS, :] = src[...]


def stack(*arrays):
    return pl.pallas_call(
        stack_kernel,
        out_shape=jax.ShapeDtypeStruct((len(arrays) * ROWS, WIDE), jnp.bfloat16),
        compiler_params=params(),
        name="stack",
    )(*arrays)


def join_kernel(src, dst):
    for j in range(8):
        dst[:, j * WIDE : (j + 1) * WIDE] = src[j]


def join_heads(x):
    return pl.pallas_call(
        join_kernel,
        out_shape=jax.ShapeDtypeStruct((x.shape[1], 8 * WIDE), jnp.bfloat16),
        compiler_params=params(),
        name="join_heads",
    )(x)


def fold(x, op, groups):
    rows = x.shape[0] // groups
    out = x[:rows]
    for g in range(1, groups):
        out = op(out, x[g * rows : (g + 1) * rows])
    return out


def col_max(x, groups=8):
    return jnp.max(fold(x, jnp.maximum, groups), axis=0, keepdims=True)


def col_sum(x, groups=8):
    return jnp.sum(fold(x, jnp.add, groups), axis=0, keepdims=True)


NEAR_BLOCKS = 7
NEAR_ROWS = NEAR_BLOCKS * BLK


def eighths(x, op):
    out = x[:8]
    for g in range(1, x.shape[0] // 8):
        out = op(out, x[g * 8 : (g + 1) * 8])
    return out


def stage_kernel(table, fresh_ref, kc_ref, vc_ref, k_out, vt_out, vbuf, k_sems, v_sems):
    pieces = NBLK // NEAR_BLOCKS
    part_rows = fresh_ref.shape[1] // 2
    parts = BLK // part_rows
    me = table[ME]

    def rows_of(p):
        return pl.ds(p * NEAR_ROWS, NEAR_ROWS)

    v_copies = [
        pltpu.make_async_copy(vc_ref.at[rows_of(p), :], vbuf.at[rows_of(p), :], v_sems.at[p])
        for p in range(pieces)
    ]
    k_copies = [
        pltpu.make_async_copy(kc_ref.at[rows_of(p), :], k_out.at[rows_of(p), :], k_sems.at[p])
        for p in range(pieces)
    ]
    for copy in v_copies + k_copies:
        copy.start()
    for p in range(pieces):
        v_copies[p].wait()

        def turn(b, carry):
            span = pl.ds(pl.multiple_of(b * BLK, BLK), BLK)
            for h in range(HEADS):
                vt_out[b, lanes(h), :] = vbuf[span, lanes(h)].T
            return carry

        lax.fori_loop(p * NEAR_BLOCKS, (p + 1) * NEAR_BLOCKS, turn, 0)
    for copy in k_copies:
        copy.wait()
    for s in range(MB):
        spot = table[me * MB + s]

        @pl.when(table[COUNTS + me] > s)
        def _():
            for i in range(parts):
                rows = pl.ds(pl.multiple_of(spot * BLK + i * part_rows, part_rows), part_rows)
                k_out[rows, :] = fresh_ref[s * parts + i, :part_rows, :]
            for h in range(HEADS):
                tile = jnp.concatenate(
                    [fresh_ref[s * parts + i, part_rows:, lanes(h)] for i in range(parts)], axis=0
                )
                vt_out[spot, lanes(h), :] = tile.T


def stage(table, fresh, key_cache, value_cache):
    vmem = pl.BlockSpec(memory_space=pltpu.VMEM)
    hbm = pl.BlockSpec(memory_space=pltpu.HBM)
    pieces = NBLK // NEAR_BLOCKS
    return pl.pallas_call(
        stage_kernel,
        in_specs=[pl.BlockSpec(memory_space=pltpu.SMEM), vmem, hbm, hbm],
        out_specs=[vmem] * 2,
        scratch_shapes=[
            pltpu.VMEM((NBLK * BLK, WIDE), jnp.bfloat16),
            pltpu.SemaphoreType.DMA((pieces,)),
            pltpu.SemaphoreType.DMA((pieces,)),
        ],
        out_shape=[
            jax.ShapeDtypeStruct((NBLK * BLK, WIDE), jnp.bfloat16),
            jax.ShapeDtypeStruct((NBLK, WIDE, BLK), jnp.bfloat16),
        ],
        compiler_params=pltpu.CompilerParams(vmem_limit_bytes=STAGE_LIMIT),
        cost_estimate=pl.CostEstimate(flops=0, bytes_accessed=15_000_000, transcendentals=0),
        name="stage",
    )(table, fresh, key_cache, value_cache)


def near_kernel(q_ref, k_ref, vt_ref, o_out, s_out, acc, top, tot, sbuf, pbuf):
    acc[...] = jnp.zeros_like(acc)
    top[...] = jnp.full_like(top, LOW)
    tot[...] = jnp.zeros_like(tot)

    def chunk(step, carry):
        def score(h):
            high = None
            for b in range(NEAR_BLOCKS):
                part = lax.dot_general(
                    k_ref[pl.ds(pl.multiple_of((step * NEAR_BLOCKS + b) * BLK, BLK), BLK), lanes(h)],
                    q_ref[:, lanes(h)],
                    (((1,), (1,)), ((), ())),
                    preferred_element_type=jnp.float32,
                )
                sbuf[h % 2, b * BLK : (b + 1) * BLK, :] = part
                peak = eighths(part, jnp.maximum)
                high = peak if high is None else jnp.maximum(high, peak)
            return jnp.max(high, axis=0, keepdims=True)

        ahead = score(0)
        for h in range(HEADS):
            high = ahead
            if h + 1 < HEADS:
                ahead = score(h + 1)
            old = top[h : h + 1, :]
            new = jnp.maximum(old, high)
            shrink = jnp.exp2((old - new) * EXPO)
            top[h : h + 1, :] = new
            added = None
            for b in range(NEAR_BLOCKS):
                weights = jnp.exp2((sbuf[h % 2, b * BLK : (b + 1) * BLK, :] - new) * EXPO)
                pbuf[h % 2, b * BLK : (b + 1) * BLK, :] = weights.astype(jnp.bfloat16)
                part = eighths(weights, jnp.add)
                added = part if added is None else added + part
            tot[h : h + 1, :] = tot[h : h + 1, :] * shrink + jnp.sum(added, axis=0, keepdims=True)
            values = jnp.concatenate(
                [vt_ref[step * NEAR_BLOCKS + b, lanes(h), :] for b in range(NEAR_BLOCKS)], axis=1
            )
            acc[h] = acc[h] * shrink + jnp.dot(
                values, pbuf[h % 2], preferred_element_type=jnp.float32
            )
        return carry

    lax.fori_loop(0, NBLK // NEAR_BLOCKS, chunk, 0)
    for h in range(HEADS):
        total = tot[h : h + 1, :]
        part = acc[h] * (1.0 / total)
        level = top[h : h + 1, :] * EXPO + jnp.log2(total)
        for s in range(MB):
            o_out[s, :, lanes(h)] = part[:, s * BLK : (s + 1) * BLK].astype(jnp.bfloat16)
            s_out[s : s + 1, lanes(h)] = level[:, s * BLK : (s + 1) * BLK]


def near(q, keys, values):
    rows = MB * BLK
    vmem = pl.BlockSpec(memory_space=pltpu.VMEM)
    return pl.pallas_call(
        near_kernel,
        in_specs=[vmem] * 3,
        out_specs=[vmem] * 2,
        scratch_shapes=[
            pltpu.VMEM((HEADS, HD, rows), jnp.float32),
            pltpu.VMEM((8, rows), jnp.float32),
            pltpu.VMEM((8, rows), jnp.float32),
            pltpu.VMEM((2, NEAR_ROWS, rows), jnp.float32),
            pltpu.VMEM((2, NEAR_ROWS, rows), jnp.bfloat16),
        ],
        out_shape=[
            jax.ShapeDtypeStruct((MB, HD, WIDE), jnp.bfloat16),
            jax.ShapeDtypeStruct((8, WIDE), jnp.float32),
        ],
        compiler_params=params(),
        cost_estimate=pl.CostEstimate(
            flops=100_000_000, bytes_accessed=400_000, transcendentals=0
        ),
        name="near",
    )(q, keys, values)


def put_stats(stat, index, apart, h, level):
    high = level.astype(jnp.bfloat16).astype(jnp.float32)
    rest = level - high
    mid = rest.astype(jnp.bfloat16).astype(jnp.float32)
    row = lax.broadcasted_iota(jnp.int32, (stat.shape[0], HD), 0) - index
    tile = stat[:, lanes(h)]
    for place, piece in ((0, high), (apart, mid), (2 * apart, rest - mid)):
        tile = jnp.where(row == place, piece, tile)
    stat[:, lanes(h)] = tile


def frame_at(table, item, shift):
    me = table[ME]
    odd = table[CORE] == 1
    z = lax.shift_right_logical(me, 2) + jnp.where(odd, item, shift)
    x = (me & (SIDE - 1)) + jnp.where(odd, shift, item)
    return (z & (SIDE - 1)) * SIDE + (x & (SIDE - 1))


def far_kernel(shift, skip, table, q_ref, keys, values, *refs):
    out, done, stat = refs[-3:]
    done[...] = jnp.zeros_like(done)
    stat[...] = jnp.zeros_like(stat)
    me = table[ME]

    def step(i, carry):
        slot = i & (MB - 1)
        frame = frame_at(table, lax.shift_right_logical(i, 1), shift)
        count = table[RADIAL + jnp.maximum(jnp.abs(frame - me) - 1, 0)]
        start = table[frame * MB + slot] - lax.shift_right_logical(count, 1)
        start = jnp.where(start < 0, start + NBLK, start)
        spots = [start + j for j in range(CMAX)]
        spots = [jnp.where(spot >= NBLK, spot - NBLK, spot) for spot in spots]
        count = jnp.where(table[COUNTS + frame] > slot, count, 0)
        rows = pl.ds(pl.multiple_of(i * BLK, BLK), BLK)
        for n in range(1, CMAX + 1):

            @pl.when(count == n)
            def _():
                def score(h):
                    return [
                        lax.dot_general(
                            keys[pl.ds(pl.multiple_of(spots[j] * BLK, BLK), BLK), lanes(h)],
                            q_ref[rows, lanes(h)],
                            (((1,), (1,)), ((), ())),
                            preferred_element_type=jnp.float32,
                        )
                        for j in range(n)
                    ]

                scores = [score(h) for h in range(HEADS)]
                tops, totals, probs = [], [], []
                for h in range(HEADS):
                    peaks = [eighths(x, jnp.maximum) for x in scores[h]]
                    top = jnp.max(functools.reduce(jnp.maximum, peaks), axis=0, keepdims=True)
                    weights = [jnp.exp2((x - top) * EXPO) for x in scores[h]]
                    sums = [eighths(x, jnp.add) for x in weights]
                    totals.append(jnp.sum(functools.reduce(jnp.add, sums), axis=0, keepdims=True))
                    tops.append(top)
                    probs.append(jnp.concatenate([x.astype(jnp.bfloat16) for x in weights], axis=0))
                parts = [
                    jnp.dot(
                        jnp.concatenate([values[spots[j], lanes(h), :] for j in range(n)], axis=1),
                        probs[h],
                        preferred_element_type=jnp.float32,
                    )
                    for h in range(HEADS)
                ]
                for h in range(HEADS):
                    out[rows, lanes(h)] = (parts[h] * (1.0 / totals[h])).astype(jnp.bfloat16)
                    put_stats(stat, i, ITEMS, h, tops[h] * EXPO + jnp.log2(totals[h]))

        return carry

    lax.fori_loop(skip * MB, ITEMS, step, 0)
    out[SIDE * ROWS :, :] = stat[...].astype(jnp.bfloat16)


def far(table, queries, keys, values, shift, skip, after=()):
    smem = pl.BlockSpec(memory_space=pltpu.SMEM)
    vmem = pl.BlockSpec(memory_space=pltpu.VMEM)
    return pl.pallas_call(
        functools.partial(far_kernel, shift, skip),
        in_specs=[smem] + [vmem] * (3 + len(after)),
        out_specs=[vmem] * 2,
        scratch_shapes=[pltpu.VMEM((STAT, WIDE), jnp.float32)],
        out_shape=[
            jax.ShapeDtypeStruct((PAY, WIDE), jnp.bfloat16),
            jax.ShapeDtypeStruct((8, BLK), jnp.float32),
        ],
        compiler_params=params(),
        cost_estimate=pl.CostEstimate(
            flops=100_000_000, bytes_accessed=400_000, transcendentals=0
        ),
        name="far",
    )(table, queries, keys, values, *after)


def read_level(ref, base, index, apart):
    tile = ref[base:, :].astype(jnp.float32)
    return (
        tile[index : index + 1]
        + tile[apart + index : apart + index + 1]
        + tile[2 * apart + index : 2 * apart + index + 1]
    )


def read_part(ref, index):
    return ref[index * BLK : (index + 1) * BLK, :].astype(jnp.float32)


def merge(levels, parts):
    top = functools.reduce(jnp.maximum, levels)
    shares = [jnp.exp2(level - top) for level in levels]
    total = functools.reduce(jnp.add, shares)
    scale = 1.0 / total
    out = None
    for share, part in zip(shares, parts):
        term = part() * (share * scale)
        out = term if out is None else out + term
    return out, top + jnp.log2(total)


def first_merge_kernel(near_ref, near_stat, local, one, two, three, *outs):
    *outs, stat = outs
    for d in range(SIDE):
        stat[...] = jnp.zeros_like(stat)
        for slot in range(MB):
            index = d * MB + slot
            sources = [one, two, three] + ([local] if d else [])
            levels = [read_level(r, SIDE * ROWS, index, ITEMS) for r in sources]
            parts = [functools.partial(read_part, r, index) for r in sources]
            if d == 0:
                levels.append(near_stat[slot : slot + 1, :])
                parts.append(lambda: near_ref[slot].astype(jnp.float32))
            value, level = merge(levels, parts)
            outs[d][slot * BLK : (slot + 1) * BLK, :] = value.astype(jnp.bfloat16)
            for h in range(HEADS):
                put_stats(stat, slot, MB, h, level[:, lanes(h)])
        outs[d][ROWS:, :] = stat[...].astype(jnp.bfloat16)


def first_merge(near_part, near_stat, local, received):
    return pl.pallas_call(
        first_merge_kernel,
        out_shape=[jax.ShapeDtypeStruct((ROWS + ONE, WIDE), jnp.bfloat16)] * SIDE,
        scratch_shapes=[pltpu.VMEM((ONE, WIDE), jnp.float32)],
        compiler_params=params(),
        cost_estimate=pl.CostEstimate(flops=16_000_000, bytes_accessed=7_000_000, transcendentals=0),
        name="first_merge",
    )(near_part, near_stat, local, *received)


def last_merge_kernel(table, *refs):
    *sources, out = refs
    for slot in range(MB):
        live = table[COUNTS + table[ME]] > slot

        @pl.when(live)
        def _():
            levels = [read_level(r, ROWS, slot, MB) for r in sources]
            parts = [functools.partial(read_part, r, slot) for r in sources]
            value, _ = merge(levels, parts)
            for h in range(HEADS):
                out[slot * BLK : (slot + 1) * BLK, lanes(h)] = value[:, lanes(h)].T.astype(jnp.bfloat16)

        @pl.when(jnp.logical_not(live))
        def _():
            out[slot * BLK : (slot + 1) * BLK, :] = jnp.zeros((BLK, WIDE), jnp.bfloat16)


def last_merge(table, parts):
    vmem = pl.BlockSpec(memory_space=pltpu.VMEM)
    return pl.pallas_call(
        last_merge_kernel,
        in_specs=[pl.BlockSpec(memory_space=pltpu.SMEM)] + [vmem] * len(parts),
        out_specs=vmem,
        out_shape=jax.ShapeDtypeStruct((ROWS, WIDE), jnp.bfloat16),
        compiler_params=params(),
        name="last_merge",
    )(table, *parts)


HEAD_SHARDS = 8


def give(x, k, step):
    pairs = []
    for z in range(SIDE):
        for c in range(SIDE):
            for head in range(HEAD_SHARDS):
                along_x = (head % 2 == 0) == (step == 1)
                to = (z, (c + k) % SIDE) if along_x else ((z + k) % SIDE, c)
                pairs.append(
                    ((z * SIDE + c) * HEAD_SHARDS + head, (to[0] * SIDE + to[1]) * HEAD_SHARDS + head)
                )
    return lax.ppermute(x, ("frame", "head"), pairs)


def fetch(x, k, step):
    return give(x, SIDE - k, step)


ORDER = (2, 1, 3)


def body(
    fresh_queries,
    fresh_keys,
    fresh_values,
    key_cache,
    value_cache,
    masked_blocks,
    masked_count,
    radial_counts,
):
    me = lax.axis_index("frame").astype(jnp.int32)
    core = lax.axis_index("head").astype(jnp.int32) % 2
    table = jnp.concatenate(
        [masked_blocks.reshape(-1), masked_count, radial_counts, me[None], core[None]]
    )
    q = lax.all_to_all(split_heads(fresh_queries[0]), "head", 0, 0, tiled=True).reshape(ROWS, WIDE)
    ring = [q] + [fetch(q, k, 1) for k in range(1, SIDE)]
    full = stack(*ring)
    queries = {k: fetch(full, k, 2) for k in ORDER}
    fresh = lax.all_to_all(
        split_heads(fresh_keys[0], fresh_values[0]), "head", 0, 0, tiled=True
    )
    keys, values = stage(table, fresh, key_cache[0], value_cache[0])
    part, done = far(table, queries[ORDER[0]], keys, values, ORDER[0], 0)
    back = [give(part, ORDER[0], 2)]
    for k in ORDER[1:]:
        part, _ = far(table, queries[k], keys, values, k, 0, (done,))
        back.append(give(part, k, 2))
    q, back[0] = lax.optimization_barrier((q, back[0]))
    local, _ = far(table, full, keys, values, 0, 1)
    near_part, near_stat = near(q, keys, values)
    merged = first_merge(near_part, near_stat, local, back)
    final = [merged[0]] + [give(merged[k], k, 1) for k in range(1, SIDE)]
    edited = last_merge(table, final).reshape(8, MB * BLK // 8, WIDE)
    edited = lax.all_to_all(edited, "head", 0, 0, tiled=True)
    return join_heads(edited)[None]


def solution(mesh):
    placed = (
        P("frame", "head", None),
        P("frame", "head", None),
        P("frame", "head", None),
        P("frame", None, "head"),
        P("frame", None, "head"),
        P(),
        P(),
        P(),
    )
    return jax.shard_map(
        body, mesh=mesh, in_specs=placed, out_specs=P("frame", "head", None), check_vma=False
    )
```

```python
import functools
import math

import jax
import jax.numpy as jnp
from jax import lax
from jax.experimental import pallas as pl
from jax.experimental.pallas import tpu as pltpu
from jax.sharding import PartitionSpec as P

HD = 128
BLK = 128
NBLK = 28
MB = 2
CMAX = 3
HEADS = 5
WIDE = HEADS * HD
SIDE = 4
ROWS = MB * BLK
ITEMS = SIDE * MB
STAT = 32
PAY = SIDE * ROWS + STAT
ONE = 16
EXPO = math.log2(math.e) / math.sqrt(HD)
LOW = -1e30
FRAMES = SIDE * SIDE
COUNTS = FRAMES * MB
RADIAL = COUNTS + FRAMES
ME = RADIAL + FRAMES - 1
CORE = ME + 1
VMEM_LIMIT = 16 * 1024 * 1024
STAGE_LIMIT = 42 * 1024 * 1024


def lanes(h):
    return slice(h * HD, (h + 1) * HD)


def params(**kw):
    return pltpu.CompilerParams(vmem_limit_bytes=VMEM_LIMIT, **kw)


def split_kernel(*refs):
    *sources, dst = refs
    for i, src in enumerate(sources):
        rows = src.shape[0]
        for j in range(8):
            dst[j, i * rows : (i + 1) * rows, :] = src[:, j * WIDE : (j + 1) * WIDE]


def split_heads(*arrays):
    rows = sum(a.shape[0] for a in arrays)
    return pl.pallas_call(
        split_kernel,
        out_shape=jax.ShapeDtypeStruct((8, rows, WIDE), jnp.bfloat16),
        compiler_params=params(),
        name="split_heads",
    )(*arrays)


def stack_kernel(*refs):
    *sources, dst = refs
    for i, src in enumerate(sources):
        dst[i * ROWS : (i + 1) * ROWS, :] = src[...]


def stack(*arrays):
    return pl.pallas_call(
        stack_kernel,
        out_shape=jax.ShapeDtypeStruct((len(arrays) * ROWS, WIDE), jnp.bfloat16),
        compiler_params=params(),
        name="stack",
    )(*arrays)


def join_kernel(src, dst):
    for j in range(8):
        dst[:, j * WIDE : (j + 1) * WIDE] = src[j]


def join_heads(x):
    return pl.pallas_call(
        join_kernel,
        out_shape=jax.ShapeDtypeStruct((x.shape[1], 8 * WIDE), jnp.bfloat16),
        compiler_params=params(),
        name="join_heads",
    )(x)


def fold(x, op, groups):
    rows = x.shape[0] // groups
    out = x[:rows]
    for g in range(1, groups):
        out = op(out, x[g * rows : (g + 1) * rows])
    return out


def col_max(x, groups=8):
    return jnp.max(fold(x, jnp.maximum, groups), axis=0, keepdims=True)


def col_sum(x, groups=8):
    return jnp.sum(fold(x, jnp.add, groups), axis=0, keepdims=True)


NEAR_BLOCKS = 7
NEAR_ROWS = NEAR_BLOCKS * BLK


def eighths(x, op):
    out = x[:8]
    for g in range(1, x.shape[0] // 8):
        out = op(out, x[g * 8 : (g + 1) * 8])
    return out


def stage_kernel(table, fresh_ref, kc_ref, vc_ref, k_out, vt_out, vbuf, k_sems, v_sems):
    pieces = NBLK // NEAR_BLOCKS
    part_rows = fresh_ref.shape[1] // 2
    parts = BLK // part_rows
    me = table[ME]

    def rows_of(p):
        return pl.ds(p * NEAR_ROWS, NEAR_ROWS)

    v_copies = [
        pltpu.make_async_copy(vc_ref.at[rows_of(p), :], vbuf.at[rows_of(p), :], v_sems.at[p])
        for p in range(pieces)
    ]
    k_copies = [
        pltpu.make_async_copy(kc_ref.at[rows_of(p), :], k_out.at[rows_of(p), :], k_sems.at[p])
        for p in range(pieces)
    ]
    for copy in v_copies + k_copies:
        copy.start()
    for p in range(pieces):
        v_copies[p].wait()

        def turn(b, carry):
            span = pl.ds(pl.multiple_of(b * BLK, BLK), BLK)
            for h in range(HEADS):
                vt_out[b, lanes(h), :] = vbuf[span, lanes(h)].T
            return carry

        lax.fori_loop(p * NEAR_BLOCKS, (p + 1) * NEAR_BLOCKS, turn, 0)
    for copy in k_copies:
        copy.wait()
    for s in range(MB):
        spot = table[me * MB + s]

        @pl.when(table[COUNTS + me] > s)
        def _():
            for i in range(parts):
                rows = pl.ds(pl.multiple_of(spot * BLK + i * part_rows, part_rows), part_rows)
                k_out[rows, :] = fresh_ref[s * parts + i, :part_rows, :]
            for h in range(HEADS):
                tile = jnp.concatenate(
                    [fresh_ref[s * parts + i, part_rows:, lanes(h)] for i in range(parts)], axis=0
                )
                vt_out[spot, lanes(h), :] = tile.T


def stage(table, fresh, key_cache, value_cache):
    vmem = pl.BlockSpec(memory_space=pltpu.VMEM)
    hbm = pl.BlockSpec(memory_space=pltpu.HBM)
    pieces = NBLK // NEAR_BLOCKS
    return pl.pallas_call(
        stage_kernel,
        in_specs=[pl.BlockSpec(memory_space=pltpu.SMEM), vmem, hbm, hbm],
        out_specs=[vmem] * 2,
        scratch_shapes=[
            pltpu.VMEM((NBLK * BLK, WIDE), jnp.bfloat16),
            pltpu.SemaphoreType.DMA((pieces,)),
            pltpu.SemaphoreType.DMA((pieces,)),
        ],
        out_shape=[
            jax.ShapeDtypeStruct((NBLK * BLK, WIDE), jnp.bfloat16),
            jax.ShapeDtypeStruct((NBLK, WIDE, BLK), jnp.bfloat16),
        ],
        compiler_params=pltpu.CompilerParams(vmem_limit_bytes=STAGE_LIMIT),
        cost_estimate=pl.CostEstimate(flops=0, bytes_accessed=15_000_000, transcendentals=0),
        name="stage",
    )(table, fresh, key_cache, value_cache)


def near_kernel(q_ref, k_ref, vt_ref, o_out, s_out, acc, top, tot, sbuf, pbuf):
    acc[...] = jnp.zeros_like(acc)
    top[...] = jnp.full_like(top, LOW)
    tot[...] = jnp.zeros_like(tot)

    def chunk(step, carry):
        def score(h):
            high = None
            for b in range(NEAR_BLOCKS):
                part = lax.dot_general(
                    k_ref[pl.ds(pl.multiple_of((step * NEAR_BLOCKS + b) * BLK, BLK), BLK), lanes(h)],
                    q_ref[:, lanes(h)],
                    (((1,), (1,)), ((), ())),
                    preferred_element_type=jnp.float32,
                )
                sbuf[h % 2, b * BLK : (b + 1) * BLK, :] = part
                peak = eighths(part, jnp.maximum)
                high = peak if high is None else jnp.maximum(high, peak)
            return jnp.max(high, axis=0, keepdims=True)

        ahead = score(0)
        for h in range(HEADS):
            high = ahead
            if h + 1 < HEADS:
                ahead = score(h + 1)
            old = top[h : h + 1, :]
            new = jnp.maximum(old, high)
            shrink = jnp.exp2((old - new) * EXPO)
            top[h : h + 1, :] = new
            added = None
            for b in range(NEAR_BLOCKS):
                weights = jnp.exp2((sbuf[h % 2, b * BLK : (b + 1) * BLK, :] - new) * EXPO)
                pbuf[h % 2, b * BLK : (b + 1) * BLK, :] = weights.astype(jnp.bfloat16)
                part = eighths(weights, jnp.add)
                added = part if added is None else added + part
            tot[h : h + 1, :] = tot[h : h + 1, :] * shrink + jnp.sum(added, axis=0, keepdims=True)
            values = jnp.concatenate(
                [vt_ref[step * NEAR_BLOCKS + b, lanes(h), :] for b in range(NEAR_BLOCKS)], axis=1
            )
            acc[h] = acc[h] * shrink + jnp.dot(
                values, pbuf[h % 2], preferred_element_type=jnp.float32
            )
        return carry

    lax.fori_loop(0, NBLK // NEAR_BLOCKS, chunk, 0)
    for h in range(HEADS):
        total = tot[h : h + 1, :]
        part = acc[h] * (1.0 / total)
        level = top[h : h + 1, :] * EXPO + jnp.log2(total)
        for s in range(MB):
            o_out[s, :, lanes(h)] = part[:, s * BLK : (s + 1) * BLK].astype(jnp.bfloat16)
            s_out[s : s + 1, lanes(h)] = level[:, s * BLK : (s + 1) * BLK]


def near(q, keys, values):
    rows = MB * BLK
    vmem = pl.BlockSpec(memory_space=pltpu.VMEM)
    return pl.pallas_call(
        near_kernel,
        in_specs=[vmem] * 3,
        out_specs=[vmem] * 2,
        scratch_shapes=[
            pltpu.VMEM((HEADS, HD, rows), jnp.float32),
            pltpu.VMEM((8, rows), jnp.float32),
            pltpu.VMEM((8, rows), jnp.float32),
            pltpu.VMEM((2, NEAR_ROWS, rows), jnp.float32),
            pltpu.VMEM((2, NEAR_ROWS, rows), jnp.bfloat16),
        ],
        out_shape=[
            jax.ShapeDtypeStruct((MB, HD, WIDE), jnp.bfloat16),
            jax.ShapeDtypeStruct((8, WIDE), jnp.float32),
        ],
        compiler_params=params(),
        cost_estimate=pl.CostEstimate(
            flops=100_000_000, bytes_accessed=400_000, transcendentals=0
        ),
        name="near",
    )(q, keys, values)


def put_stats(stat, index, apart, h, level):
    high = level.astype(jnp.bfloat16).astype(jnp.float32)
    rest = level - high
    mid = rest.astype(jnp.bfloat16).astype(jnp.float32)
    row = lax.broadcasted_iota(jnp.int32, (stat.shape[0], HD), 0) - index
    tile = stat[:, lanes(h)]
    for place, piece in ((0, high), (apart, mid), (2 * apart, rest - mid)):
        tile = jnp.where(row == place, piece, tile)
    stat[:, lanes(h)] = tile


def frame_at(table, item, shift):
    me = table[ME]
    odd = table[CORE] == 1
    z = lax.shift_right_logical(me, 2) + jnp.where(odd, item, shift)
    x = (me & (SIDE - 1)) + jnp.where(odd, shift, item)
    return (z & (SIDE - 1)) * SIDE + (x & (SIDE - 1))


def far_kernel(shift, skip, table, own_ref, rest_ref, keys, values, *refs):
    out, done, stat = refs[-3:]
    done[...] = jnp.zeros_like(done)
    stat[...] = jnp.zeros_like(stat)
    me = table[ME]

    def step(q_ref, offset, i, carry):
        slot = i & (MB - 1)
        frame = frame_at(table, lax.shift_right_logical(i, 1), shift)
        count = table[RADIAL + jnp.maximum(jnp.abs(frame - me) - 1, 0)]
        start = table[frame * MB + slot] - lax.shift_right_logical(count, 1)
        start = jnp.where(start < 0, start + NBLK, start)
        spots = [start + j for j in range(CMAX)]
        spots = [jnp.where(spot >= NBLK, spot - NBLK, spot) for spot in spots]
        count = jnp.where(table[COUNTS + frame] > slot, count, 0)
        rows = pl.ds(pl.multiple_of(i * BLK, BLK), BLK)
        source = pl.ds(pl.multiple_of((i - offset) * BLK, BLK), BLK)
        for n in range(1, CMAX + 1):

            @pl.when(count == n)
            def _():
                def score(h):
                    return [
                        lax.dot_general(
                            keys[pl.ds(pl.multiple_of(spots[j] * BLK, BLK), BLK), lanes(h)],
                            q_ref[source, lanes(h)],
                            (((1,), (1,)), ((), ())),
                            preferred_element_type=jnp.float32,
                        )
                        for j in range(n)
                    ]

                scores = [score(h) for h in range(HEADS)]
                tops, totals, probs = [], [], []
                for h in range(HEADS):
                    peaks = [eighths(x, jnp.maximum) for x in scores[h]]
                    top = jnp.max(functools.reduce(jnp.maximum, peaks), axis=0, keepdims=True)
                    weights = [jnp.exp2((x - top) * EXPO) for x in scores[h]]
                    sums = [eighths(x, jnp.add) for x in weights]
                    totals.append(jnp.sum(functools.reduce(jnp.add, sums), axis=0, keepdims=True))
                    tops.append(top)
                    probs.append(jnp.concatenate([x.astype(jnp.bfloat16) for x in weights], axis=0))
                parts = [
                    jnp.dot(
                        jnp.concatenate([values[spots[j], lanes(h), :] for j in range(n)], axis=1),
                        probs[h],
                        preferred_element_type=jnp.float32,
                    )
                    for h in range(HEADS)
                ]
                for h in range(HEADS):
                    out[rows, lanes(h)] = (parts[h] * (1.0 / totals[h])).astype(jnp.bfloat16)
                    put_stats(stat, i, ITEMS, h, tops[h] * EXPO + jnp.log2(totals[h]))

        return carry

    if not skip:
        lax.fori_loop(0, MB, functools.partial(step, own_ref, 0), 0)
    lax.fori_loop(MB, ITEMS, functools.partial(step, rest_ref, MB), 0)
    out[SIDE * ROWS :, :] = stat[...].astype(jnp.bfloat16)


def far(table, own, rest, keys, values, shift, skip, after=()):
    smem = pl.BlockSpec(memory_space=pltpu.SMEM)
    vmem = pl.BlockSpec(memory_space=pltpu.VMEM)
    return pl.pallas_call(
        functools.partial(far_kernel, shift, skip),
        in_specs=[smem] + [vmem] * (4 + len(after)),
        out_specs=[vmem] * 2,
        scratch_shapes=[pltpu.VMEM((STAT, WIDE), jnp.float32)],
        out_shape=[
            jax.ShapeDtypeStruct((PAY, WIDE), jnp.bfloat16),
            jax.ShapeDtypeStruct((8, BLK), jnp.float32),
        ],
        compiler_params=params(),
        cost_estimate=pl.CostEstimate(
            flops=100_000_000, bytes_accessed=400_000, transcendentals=0
        ),
        name="far",
    )(table, own, rest, keys, values, *after)


def read_level(ref, base, index, apart):
    tile = ref[base:, :].astype(jnp.float32)
    return (
        tile[index : index + 1]
        + tile[apart + index : apart + index + 1]
        + tile[2 * apart + index : 2 * apart + index + 1]
    )


def read_part(ref, index):
    return ref[index * BLK : (index + 1) * BLK, :].astype(jnp.float32)


def merge(levels, parts):
    top = functools.reduce(jnp.maximum, levels)
    shares = [jnp.exp2(level - top) for level in levels]
    total = functools.reduce(jnp.add, shares)
    scale = 1.0 / total
    out = None
    for share, part in zip(shares, parts):
        term = part() * (share * scale)
        out = term if out is None else out + term
    return out, top + jnp.log2(total)


def first_merge_kernel(near_ref, near_stat, local, one, two, three, *outs):
    *outs, stat = outs
    for d in range(SIDE):
        stat[...] = jnp.zeros_like(stat)
        for slot in range(MB):
            index = d * MB + slot
            sources = [one, two, three] + ([local] if d else [])
            levels = [read_level(r, SIDE * ROWS, index, ITEMS) for r in sources]
            parts = [functools.partial(read_part, r, index) for r in sources]
            if d == 0:
                levels.append(near_stat[slot : slot + 1, :])
                parts.append(lambda: near_ref[slot].astype(jnp.float32))
            value, level = merge(levels, parts)
            outs[d][slot * BLK : (slot + 1) * BLK, :] = value.astype(jnp.bfloat16)
            for h in range(HEADS):
                put_stats(stat, slot, MB, h, level[:, lanes(h)])
        outs[d][ROWS:, :] = stat[...].astype(jnp.bfloat16)


def first_merge(near_part, near_stat, local, received):
    return pl.pallas_call(
        first_merge_kernel,
        out_shape=[jax.ShapeDtypeStruct((ROWS + ONE, WIDE), jnp.bfloat16)] * SIDE,
        scratch_shapes=[pltpu.VMEM((ONE, WIDE), jnp.float32)],
        compiler_params=params(),
        cost_estimate=pl.CostEstimate(flops=16_000_000, bytes_accessed=7_000_000, transcendentals=0),
        name="first_merge",
    )(near_part, near_stat, local, *received)


def last_merge_kernel(table, *refs):
    *sources, out = refs
    for slot in range(MB):
        live = table[COUNTS + table[ME]] > slot

        @pl.when(live)
        def _():
            levels = [read_level(r, ROWS, slot, MB) for r in sources]
            parts = [functools.partial(read_part, r, slot) for r in sources]
            value, _ = merge(levels, parts)
            for h in range(HEADS):
                out[slot * BLK : (slot + 1) * BLK, lanes(h)] = value[:, lanes(h)].T.astype(jnp.bfloat16)

        @pl.when(jnp.logical_not(live))
        def _():
            out[slot * BLK : (slot + 1) * BLK, :] = jnp.zeros((BLK, WIDE), jnp.bfloat16)


def last_merge(table, parts):
    vmem = pl.BlockSpec(memory_space=pltpu.VMEM)
    return pl.pallas_call(
        last_merge_kernel,
        in_specs=[pl.BlockSpec(memory_space=pltpu.SMEM)] + [vmem] * len(parts),
        out_specs=vmem,
        out_shape=jax.ShapeDtypeStruct((ROWS, WIDE), jnp.bfloat16),
        compiler_params=params(),
        name="last_merge",
    )(table, *parts)


HEAD_SHARDS = 8


def give(x, k, step):
    pairs = []
    for z in range(SIDE):
        for c in range(SIDE):
            for head in range(HEAD_SHARDS):
                along_x = (head % 2 == 0) == (step == 1)
                to = (z, (c + k) % SIDE) if along_x else ((z + k) % SIDE, c)
                pairs.append(
                    ((z * SIDE + c) * HEAD_SHARDS + head, (to[0] * SIDE + to[1]) * HEAD_SHARDS + head)
                )
    return lax.ppermute(x, ("frame", "head"), pairs)


def fetch(x, k, step):
    return give(x, SIDE - k, step)


ORDER = (2, 1, 3)


def body(
    fresh_queries,
    fresh_keys,
    fresh_values,
    key_cache,
    value_cache,
    masked_blocks,
    masked_count,
    radial_counts,
):
    me = lax.axis_index("frame").astype(jnp.int32)
    core = lax.axis_index("head").astype(jnp.int32) % 2
    table = jnp.concatenate(
        [masked_blocks.reshape(-1), masked_count, radial_counts, me[None], core[None]]
    )
    q = lax.all_to_all(split_heads(fresh_queries[0]), "head", 0, 0, tiled=True).reshape(ROWS, WIDE)
    ring = [fetch(q, k, 1) for k in range(1, SIDE)]
    own = {k: fetch(q, k, 2) for k in ORDER}
    *ring, own[2], own[3] = lax.optimization_barrier((*ring, own[2], own[3]))
    full = stack(*ring)
    queries = {k: fetch(full, k, 2) for k in ORDER}
    fresh = lax.all_to_all(
        split_heads(fresh_keys[0], fresh_values[0]), "head", 0, 0, tiled=True
    )
    keys, values = stage(table, fresh, key_cache[0], value_cache[0])
    part, done = far(table, own[ORDER[0]], queries[ORDER[0]], keys, values, ORDER[0], 0)
    back = [give(part, ORDER[0], 2)]
    for k in ORDER[1:]:
        part, _ = far(table, own[k], queries[k], keys, values, k, 0, (done,))
        back.append(give(part, k, 2))
    q, back[0] = lax.optimization_barrier((q, back[0]))
    local, _ = far(table, q, full, keys, values, 0, 1)
    near_part, near_stat = near(q, keys, values)
    merged = first_merge(near_part, near_stat, local, back)
    final = [merged[0]] + [give(merged[k], k, 1) for k in range(1, SIDE)]
    edited = last_merge(table, final).reshape(8, MB * BLK // 8, WIDE)
    edited = lax.all_to_all(edited, "head", 0, 0, tiled=True)
    return join_heads(edited)[None]


def solution(mesh):
    placed = (
        P("frame", "head", None),
        P("frame", "head", None),
        P("frame", "head", None),
        P("frame", None, "head"),
        P("frame", None, "head"),
        P(),
        P(),
        P(),
    )
    return jax.shard_map(
        body, mesh=mesh, in_specs=placed, out_specs=P("frame", "head", None), check_vma=False
    )
```

```python
import functools
import math

import jax
import jax.numpy as jnp
from jax import lax
from jax.experimental import pallas as pl
from jax.experimental.pallas import tpu as pltpu
from jax.sharding import PartitionSpec as P

HD = 128
BLK = 128
NBLK = 28
MB = 2
CMAX = 3
HEADS = 5
WIDE = HEADS * HD
SIDE = 4
ROWS = MB * BLK
ITEMS = SIDE * MB
STAT = 32
PAY = SIDE * ROWS + STAT
ONE = 16
EXPO = math.log2(math.e) / math.sqrt(HD)
LOW = -1e30
FRAMES = SIDE * SIDE
COUNTS = FRAMES * MB
RADIAL = COUNTS + FRAMES
ME = RADIAL + FRAMES - 1
CORE = ME + 1
VMEM_LIMIT = 16 * 1024 * 1024
STAGE_LIMIT = 42 * 1024 * 1024


def lanes(h):
    return slice(h * HD, (h + 1) * HD)


def params(**kw):
    return pltpu.CompilerParams(vmem_limit_bytes=VMEM_LIMIT, **kw)


def split_kernel(*refs):
    *sources, dst = refs
    for i, src in enumerate(sources):
        rows = src.shape[0]
        for j in range(8):
            dst[j, i * rows : (i + 1) * rows, :] = src[:, j * WIDE : (j + 1) * WIDE]


def split_heads(*arrays):
    rows = sum(a.shape[0] for a in arrays)
    return pl.pallas_call(
        split_kernel,
        out_shape=jax.ShapeDtypeStruct((8, rows, WIDE), jnp.bfloat16),
        compiler_params=params(),
        name="split_heads",
    )(*arrays)


def stack_kernel(*refs):
    *sources, dst = refs
    for i, src in enumerate(sources):
        dst[i * ROWS : (i + 1) * ROWS, :] = src[...]


def stack(*arrays):
    return pl.pallas_call(
        stack_kernel,
        out_shape=jax.ShapeDtypeStruct((len(arrays) * ROWS, WIDE), jnp.bfloat16),
        compiler_params=params(),
        name="stack",
    )(*arrays)


def join_kernel(src, dst):
    for j in range(8):
        dst[:, j * WIDE : (j + 1) * WIDE] = src[j]


def join_heads(x):
    return pl.pallas_call(
        join_kernel,
        out_shape=jax.ShapeDtypeStruct((x.shape[1], 8 * WIDE), jnp.bfloat16),
        compiler_params=params(),
        name="join_heads",
    )(x)


def fold(x, op, groups):
    rows = x.shape[0] // groups
    out = x[:rows]
    for g in range(1, groups):
        out = op(out, x[g * rows : (g + 1) * rows])
    return out


def col_max(x, groups=8):
    return jnp.max(fold(x, jnp.maximum, groups), axis=0, keepdims=True)


def col_sum(x, groups=8):
    return jnp.sum(fold(x, jnp.add, groups), axis=0, keepdims=True)


NEAR_BLOCKS = 7
NEAR_ROWS = NEAR_BLOCKS * BLK


def eighths(x, op):
    out = x[:8]
    for g in range(1, x.shape[0] // 8):
        out = op(out, x[g * 8 : (g + 1) * 8])
    return out


def stage_kernel(table, fresh_ref, kc_ref, vc_ref, k_out, vt_out, vbuf, k_sems, v_sems):
    pieces = NBLK // NEAR_BLOCKS
    part_rows = fresh_ref.shape[1] // 2
    parts = BLK // part_rows
    me = table[ME]

    def rows_of(p):
        return pl.ds(p * NEAR_ROWS, NEAR_ROWS)

    v_copies = [
        pltpu.make_async_copy(vc_ref.at[rows_of(p), :], vbuf.at[rows_of(p), :], v_sems.at[p])
        for p in range(pieces)
    ]
    k_copies = [
        pltpu.make_async_copy(kc_ref.at[rows_of(p), :], k_out.at[rows_of(p), :], k_sems.at[p])
        for p in range(pieces)
    ]
    for copy in v_copies + k_copies:
        copy.start()
    for p in range(pieces):
        v_copies[p].wait()

        def turn(b, carry):
            span = pl.ds(pl.multiple_of(b * BLK, BLK), BLK)
            for h in range(HEADS):
                vt_out[b, lanes(h), :] = vbuf[span, lanes(h)].T
            return carry

        lax.fori_loop(p * NEAR_BLOCKS, (p + 1) * NEAR_BLOCKS, turn, 0)
    for copy in k_copies:
        copy.wait()
    for s in range(MB):
        spot = table[me * MB + s]

        @pl.when(table[COUNTS + me] > s)
        def _():
            for i in range(parts):
                rows = pl.ds(pl.multiple_of(spot * BLK + i * part_rows, part_rows), part_rows)
                k_out[rows, :] = fresh_ref[s * parts + i, :part_rows, :]
            for h in range(HEADS):
                tile = jnp.concatenate(
                    [fresh_ref[s * parts + i, part_rows:, lanes(h)] for i in range(parts)], axis=0
                )
                vt_out[spot, lanes(h), :] = tile.T


def stage(table, fresh, key_cache, value_cache):
    vmem = pl.BlockSpec(memory_space=pltpu.VMEM)
    hbm = pl.BlockSpec(memory_space=pltpu.HBM)
    pieces = NBLK // NEAR_BLOCKS
    return pl.pallas_call(
        stage_kernel,
        in_specs=[pl.BlockSpec(memory_space=pltpu.SMEM), vmem, hbm, hbm],
        out_specs=[vmem] * 2,
        scratch_shapes=[
            pltpu.VMEM((NBLK * BLK, WIDE), jnp.bfloat16),
            pltpu.SemaphoreType.DMA((pieces,)),
            pltpu.SemaphoreType.DMA((pieces,)),
        ],
        out_shape=[
            jax.ShapeDtypeStruct((NBLK * BLK, WIDE), jnp.bfloat16),
            jax.ShapeDtypeStruct((NBLK, WIDE, BLK), jnp.bfloat16),
        ],
        compiler_params=pltpu.CompilerParams(vmem_limit_bytes=STAGE_LIMIT),
        cost_estimate=pl.CostEstimate(flops=0, bytes_accessed=15_000_000, transcendentals=0),
        name="stage",
    )(table, fresh, key_cache, value_cache)


def near_kernel(q_ref, k_ref, vt_ref, o_out, s_out, acc, top, tot, sbuf, pbuf):
    acc[...] = jnp.zeros_like(acc)
    top[...] = jnp.full_like(top, LOW)
    tot[...] = jnp.zeros_like(tot)

    def chunk(step, carry):
        def score(h):
            high = None
            for b in range(NEAR_BLOCKS):
                part = lax.dot_general(
                    k_ref[pl.ds(pl.multiple_of((step * NEAR_BLOCKS + b) * BLK, BLK), BLK), lanes(h)],
                    q_ref[:, lanes(h)],
                    (((1,), (1,)), ((), ())),
                    preferred_element_type=jnp.float32,
                )
                sbuf[h % 2, b * BLK : (b + 1) * BLK, :] = part
                peak = eighths(part, jnp.maximum)
                high = peak if high is None else jnp.maximum(high, peak)
            return jnp.max(high, axis=0, keepdims=True)

        ahead = score(0)
        for h in range(HEADS):
            high = ahead
            if h + 1 < HEADS:
                ahead = score(h + 1)
            old = top[h : h + 1, :]
            new = jnp.maximum(old, high)
            shrink = jnp.exp2((old - new) * EXPO)
            top[h : h + 1, :] = new
            added = None
            for b in range(NEAR_BLOCKS):
                weights = jnp.exp2((sbuf[h % 2, b * BLK : (b + 1) * BLK, :] - new) * EXPO)
                pbuf[h % 2, b * BLK : (b + 1) * BLK, :] = weights.astype(jnp.bfloat16)
                part = eighths(weights, jnp.add)
                added = part if added is None else added + part
            tot[h : h + 1, :] = tot[h : h + 1, :] * shrink + jnp.sum(added, axis=0, keepdims=True)
            values = jnp.concatenate(
                [vt_ref[step * NEAR_BLOCKS + b, lanes(h), :] for b in range(NEAR_BLOCKS)], axis=1
            )
            acc[h] = acc[h] * shrink + jnp.dot(
                values, pbuf[h % 2], preferred_element_type=jnp.float32
            )
        return carry

    lax.fori_loop(0, NBLK // NEAR_BLOCKS, chunk, 0)
    for h in range(HEADS):
        total = tot[h : h + 1, :]
        part = acc[h] * (1.0 / total)
        level = top[h : h + 1, :] * EXPO + jnp.log2(total)
        for s in range(MB):
            o_out[s, :, lanes(h)] = part[:, s * BLK : (s + 1) * BLK].astype(jnp.bfloat16)
            s_out[s : s + 1, lanes(h)] = level[:, s * BLK : (s + 1) * BLK]


def near(q, keys, values):
    rows = MB * BLK
    vmem = pl.BlockSpec(memory_space=pltpu.VMEM)
    return pl.pallas_call(
        near_kernel,
        in_specs=[vmem] * 3,
        out_specs=[vmem] * 2,
        scratch_shapes=[
            pltpu.VMEM((HEADS, HD, rows), jnp.float32),
            pltpu.VMEM((8, rows), jnp.float32),
            pltpu.VMEM((8, rows), jnp.float32),
            pltpu.VMEM((2, NEAR_ROWS, rows), jnp.float32),
            pltpu.VMEM((2, NEAR_ROWS, rows), jnp.bfloat16),
        ],
        out_shape=[
            jax.ShapeDtypeStruct((MB, HD, WIDE), jnp.bfloat16),
            jax.ShapeDtypeStruct((8, WIDE), jnp.float32),
        ],
        compiler_params=params(),
        cost_estimate=pl.CostEstimate(
            flops=100_000_000, bytes_accessed=400_000, transcendentals=0
        ),
        name="near",
    )(q, keys, values)


def put_stats(stat, index, apart, h, level):
    high = level.astype(jnp.bfloat16).astype(jnp.float32)
    rest = level - high
    mid = rest.astype(jnp.bfloat16).astype(jnp.float32)
    row = lax.broadcasted_iota(jnp.int32, (stat.shape[0], HD), 0) - index
    tile = stat[:, lanes(h)]
    for place, piece in ((0, high), (apart, mid), (2 * apart, rest - mid)):
        tile = jnp.where(row == place, piece, tile)
    stat[:, lanes(h)] = tile


def frame_at(table, item, shift):
    me = table[ME]
    odd = table[CORE] == 1
    z = lax.shift_right_logical(me, 2) + jnp.where(odd, item, shift)
    x = (me & (SIDE - 1)) + jnp.where(odd, shift, item)
    return (z & (SIDE - 1)) * SIDE + (x & (SIDE - 1))


def far_kernel(shift, skip, table, q_ref, keys, values, *refs):
    out, done, stat = refs[-3:]
    done[...] = jnp.zeros_like(done)
    stat[...] = jnp.zeros_like(stat)
    me = table[ME]

    def step(i, carry):
        slot = i & (MB - 1)
        frame = frame_at(table, lax.shift_right_logical(i, 1), shift)
        count = table[RADIAL + jnp.maximum(jnp.abs(frame - me) - 1, 0)]
        start = table[frame * MB + slot] - lax.shift_right_logical(count, 1)
        start = jnp.where(start < 0, start + NBLK, start)
        spots = [start + j for j in range(CMAX)]
        spots = [jnp.where(spot >= NBLK, spot - NBLK, spot) for spot in spots]
        count = jnp.where(table[COUNTS + frame] > slot, count, 0)
        rows = pl.ds(pl.multiple_of(i * BLK, BLK), BLK)
        for n in range(1, CMAX + 1):

            @pl.when(count == n)
            def _():
                def score(h):
                    return [
                        lax.dot_general(
                            keys[pl.ds(pl.multiple_of(spots[j] * BLK, BLK), BLK), lanes(h)],
                            q_ref[rows, lanes(h)],
                            (((1,), (1,)), ((), ())),
                            preferred_element_type=jnp.float32,
                        )
                        for j in range(n)
                    ]

                scores = [score(h) for h in range(HEADS)]
                tops, totals, probs = [], [], []
                for h in range(HEADS):
                    peaks = [eighths(x, jnp.maximum) for x in scores[h]]
                    top = jnp.max(functools.reduce(jnp.maximum, peaks), axis=0, keepdims=True)
                    weights = [jnp.exp2((x - top) * EXPO) for x in scores[h]]
                    sums = [eighths(x, jnp.add) for x in weights]
                    totals.append(jnp.sum(functools.reduce(jnp.add, sums), axis=0, keepdims=True))
                    tops.append(top)
                    probs.append(jnp.concatenate([x.astype(jnp.bfloat16) for x in weights], axis=0))
                parts = [
                    jnp.dot(
                        jnp.concatenate([values[spots[j], lanes(h), :] for j in range(n)], axis=1),
                        probs[h],
                        preferred_element_type=jnp.float32,
                    )
                    for h in range(HEADS)
                ]
                for h in range(HEADS):
                    out[rows, lanes(h)] = (parts[h] * (1.0 / totals[h])).astype(jnp.bfloat16)
                    put_stats(stat, i, ITEMS, h, tops[h] * EXPO + jnp.log2(totals[h]))

        return carry

    lax.fori_loop(skip * MB, ITEMS, step, 0)
    out[SIDE * ROWS :, :] = stat[...].astype(jnp.bfloat16)


def far(table, queries, keys, values, shift, skip, after=()):
    smem = pl.BlockSpec(memory_space=pltpu.SMEM)
    vmem = pl.BlockSpec(memory_space=pltpu.VMEM)
    return pl.pallas_call(
        functools.partial(far_kernel, shift, skip),
        in_specs=[smem] + [vmem] * (3 + len(after)),
        out_specs=[vmem] * 2,
        scratch_shapes=[pltpu.VMEM((STAT, WIDE), jnp.float32)],
        out_shape=[
            jax.ShapeDtypeStruct((PAY, WIDE), jnp.bfloat16),
            jax.ShapeDtypeStruct((8, BLK), jnp.float32),
        ],
        compiler_params=params(),
        cost_estimate=pl.CostEstimate(
            flops=100_000_000, bytes_accessed=400_000, transcendentals=0
        ),
        name="far",
    )(table, queries, keys, values, *after)


def read_level(ref, base, index, apart):
    tile = ref[base:, :].astype(jnp.float32)
    return (
        tile[index : index + 1]
        + tile[apart + index : apart + index + 1]
        + tile[2 * apart + index : 2 * apart + index + 1]
    )


def read_part(ref, index):
    return ref[index * BLK : (index + 1) * BLK, :].astype(jnp.float32)


def merge(levels, parts):
    top = functools.reduce(jnp.maximum, levels)
    shares = [jnp.exp2(level - top) for level in levels]
    total = functools.reduce(jnp.add, shares)
    scale = 1.0 / total
    out = None
    for share, part in zip(shares, parts):
        term = part() * (share * scale)
        out = term if out is None else out + term
    return out, top + jnp.log2(total)


def first_merge_kernel(d, *refs):
    *sources, out, stat = refs
    if d == 0:
        near_ref, near_stat, *sources = sources
    stat[...] = jnp.zeros_like(stat)
    for slot in range(MB):
        index = d * MB + slot
        levels = [read_level(r, SIDE * ROWS, index, ITEMS) for r in sources]
        parts = [functools.partial(read_part, r, index) for r in sources]
        if d == 0:
            levels.append(near_stat[slot : slot + 1, :])
            parts.append(lambda: near_ref[slot].astype(jnp.float32))
        value, level = merge(levels, parts)
        out[slot * BLK : (slot + 1) * BLK, :] = value.astype(jnp.bfloat16)
        for h in range(HEADS):
            put_stats(stat, slot, MB, h, level[:, lanes(h)])
    out[ROWS:, :] = stat[...].astype(jnp.bfloat16)


def first_merge(d, near_part, near_stat, local, received):
    own = (near_part, near_stat) if d == 0 else (local,)
    return pl.pallas_call(
        functools.partial(first_merge_kernel, d),
        out_shape=jax.ShapeDtypeStruct((ROWS + ONE, WIDE), jnp.bfloat16),
        scratch_shapes=[pltpu.VMEM((ONE, WIDE), jnp.float32)],
        compiler_params=params(),
        cost_estimate=pl.CostEstimate(flops=4_000_000, bytes_accessed=400_000, transcendentals=0),
        name="first_merge",
    )(*own, *received)


def last_merge_kernel(table, *refs):
    *sources, out = refs
    for slot in range(MB):
        live = table[COUNTS + table[ME]] > slot

        @pl.when(live)
        def _():
            levels = [read_level(r, ROWS, slot, MB) for r in sources]
            parts = [functools.partial(read_part, r, slot) for r in sources]
            value, _ = merge(levels, parts)
            for h in range(HEADS):
                out[slot * BLK : (slot + 1) * BLK, lanes(h)] = value[:, lanes(h)].T.astype(jnp.bfloat16)

        @pl.when(jnp.logical_not(live))
        def _():
            out[slot * BLK : (slot + 1) * BLK, :] = jnp.zeros((BLK, WIDE), jnp.bfloat16)


def last_merge(table, parts):
    vmem = pl.BlockSpec(memory_space=pltpu.VMEM)
    return pl.pallas_call(
        last_merge_kernel,
        in_specs=[pl.BlockSpec(memory_space=pltpu.SMEM)] + [vmem] * len(parts),
        out_specs=vmem,
        out_shape=jax.ShapeDtypeStruct((ROWS, WIDE), jnp.bfloat16),
        compiler_params=params(),
        name="last_merge",
    )(table, *parts)


HEAD_SHARDS = 8


def give(x, k, step):
    pairs = []
    for z in range(SIDE):
        for c in range(SIDE):
            for head in range(HEAD_SHARDS):
                along_x = (head % 2 == 0) == (step == 1)
                to = (z, (c + k) % SIDE) if along_x else ((z + k) % SIDE, c)
                pairs.append(
                    ((z * SIDE + c) * HEAD_SHARDS + head, (to[0] * SIDE + to[1]) * HEAD_SHARDS + head)
                )
    return lax.ppermute(x, ("frame", "head"), pairs)


def fetch(x, k, step):
    return give(x, SIDE - k, step)


ORDER = (2, 1, 3)


def body(
    fresh_queries,
    fresh_keys,
    fresh_values,
    key_cache,
    value_cache,
    masked_blocks,
    masked_count,
    radial_counts,
):
    me = lax.axis_index("frame").astype(jnp.int32)
    core = lax.axis_index("head").astype(jnp.int32) % 2
    table = jnp.concatenate(
        [masked_blocks.reshape(-1), masked_count, radial_counts, me[None], core[None]]
    )
    q = lax.all_to_all(split_heads(fresh_queries[0]), "head", 0, 0, tiled=True).reshape(ROWS, WIDE)
    ring = [q] + [fetch(q, k, 1) for k in range(1, SIDE)]
    full = stack(*ring)
    queries = {k: fetch(full, k, 2) for k in ORDER}
    fresh = lax.all_to_all(
        split_heads(fresh_keys[0], fresh_values[0]), "head", 0, 0, tiled=True
    )
    keys, values = stage(table, fresh, key_cache[0], value_cache[0])
    part, done = far(table, queries[ORDER[0]], keys, values, ORDER[0], 0)
    back = [give(part, ORDER[0], 2)]
    for k in ORDER[1:]:
        part, _ = far(table, queries[k], keys, values, k, 0, (done,))
        back.append(give(part, k, 2))
    q, back[0] = lax.optimization_barrier((q, back[0]))
    local, _ = far(table, full, keys, values, 0, 1)
    near_part, near_stat = near(q, keys, values)
    near_stat, back[1], back[2] = lax.optimization_barrier((near_stat, back[1], back[2]))
    final = {k: give(first_merge(k, near_part, near_stat, local, back), k, 1) for k in ORDER}
    final[0] = first_merge(0, near_part, near_stat, local, back)
    final = [final[k] for k in range(SIDE)]
    edited = last_merge(table, final).reshape(8, MB * BLK // 8, WIDE)
    edited = lax.all_to_all(edited, "head", 0, 0, tiled=True)
    return join_heads(edited)[None]


def solution(mesh):
    placed = (
        P("frame", "head", None),
        P("frame", "head", None),
        P("frame", "head", None),
        P("frame", None, "head"),
        P("frame", None, "head"),
        P(),
        P(),
        P(),
    )
    return jax.shard_map(
        body, mesh=mesh, in_specs=placed, out_specs=P("frame", "head", None), check_vma=False
    )
```

```python
import functools
import math

import jax
import jax.numpy as jnp
from jax import lax
from jax.experimental import pallas as pl
from jax.experimental.pallas import tpu as pltpu
from jax.sharding import PartitionSpec as P

HD = 128
BLK = 128
NBLK = 28
MB = 2
CMAX = 3
HEADS = 5
WIDE = HEADS * HD
SIDE = 4
ROWS = MB * BLK
ITEMS = SIDE * MB
STAT = 32
PAY = SIDE * ROWS + STAT
ONE = 16
EXPO = math.log2(math.e) / math.sqrt(HD)
LOW = -1e30
FRAMES = SIDE * SIDE
COUNTS = FRAMES * MB
RADIAL = COUNTS + FRAMES
ME = RADIAL + FRAMES - 1
CORE = ME + 1
VMEM_LIMIT = 16 * 1024 * 1024
STAGE_LIMIT = 42 * 1024 * 1024


def lanes(h):
    return slice(h * HD, (h + 1) * HD)


def params(**kw):
    return pltpu.CompilerParams(vmem_limit_bytes=VMEM_LIMIT, **kw)


def split_kernel(*refs):
    *sources, dst = refs
    for i, src in enumerate(sources):
        rows = src.shape[0]
        for j in range(8):
            dst[j, i * rows : (i + 1) * rows, :] = src[:, j * WIDE : (j + 1) * WIDE]


def split_heads(*arrays):
    rows = sum(a.shape[0] for a in arrays)
    return pl.pallas_call(
        split_kernel,
        out_shape=jax.ShapeDtypeStruct((8, rows, WIDE), jnp.bfloat16),
        compiler_params=params(),
        name="split_heads",
    )(*arrays)


def stack_kernel(*refs):
    *sources, dst = refs
    for i, src in enumerate(sources):
        dst[i * ROWS : (i + 1) * ROWS, :] = src[...]


def stack(*arrays):
    return pl.pallas_call(
        stack_kernel,
        out_shape=jax.ShapeDtypeStruct((len(arrays) * ROWS, WIDE), jnp.bfloat16),
        compiler_params=params(),
        name="stack",
    )(*arrays)


def join_kernel(src, dst):
    for j in range(8):
        dst[:, j * WIDE : (j + 1) * WIDE] = src[j]


def join_heads(x):
    return pl.pallas_call(
        join_kernel,
        out_shape=jax.ShapeDtypeStruct((x.shape[1], 8 * WIDE), jnp.bfloat16),
        compiler_params=params(),
        name="join_heads",
    )(x)


def fold(x, op, groups):
    rows = x.shape[0] // groups
    out = x[:rows]
    for g in range(1, groups):
        out = op(out, x[g * rows : (g + 1) * rows])
    return out


def col_max(x, groups=8):
    return jnp.max(fold(x, jnp.maximum, groups), axis=0, keepdims=True)


def col_sum(x, groups=8):
    return jnp.sum(fold(x, jnp.add, groups), axis=0, keepdims=True)


NEAR_BLOCKS = 7
NEAR_ROWS = NEAR_BLOCKS * BLK


def eighths(x, op):
    out = x[:8]
    for g in range(1, x.shape[0] // 8):
        out = op(out, x[g * 8 : (g + 1) * 8])
    return out


def stage_kernel(table, fresh_ref, kc_ref, vc_ref, k_out, vt_out, vbuf, k_sems, v_sems):
    pieces = NBLK // NEAR_BLOCKS
    part_rows = fresh_ref.shape[1] // 2
    parts = BLK // part_rows
    me = table[ME]

    def rows_of(p):
        return pl.ds(p * NEAR_ROWS, NEAR_ROWS)

    v_copies = [
        pltpu.make_async_copy(vc_ref.at[rows_of(p), :], vbuf.at[rows_of(p), :], v_sems.at[p])
        for p in range(pieces)
    ]
    k_copies = [
        pltpu.make_async_copy(kc_ref.at[rows_of(p), :], k_out.at[rows_of(p), :], k_sems.at[p])
        for p in range(pieces)
    ]
    for copy in v_copies + k_copies:
        copy.start()
    for p in range(pieces):
        v_copies[p].wait()

        def turn(b, carry):
            span = pl.ds(pl.multiple_of(b * BLK, BLK), BLK)
            for h in range(HEADS):
                vt_out[b, lanes(h), :] = vbuf[span, lanes(h)].T
            return carry

        lax.fori_loop(p * NEAR_BLOCKS, (p + 1) * NEAR_BLOCKS, turn, 0)
    for copy in k_copies:
        copy.wait()
    for s in range(MB):
        spot = table[me * MB + s]

        @pl.when(table[COUNTS + me] > s)
        def _():
            for i in range(parts):
                rows = pl.ds(pl.multiple_of(spot * BLK + i * part_rows, part_rows), part_rows)
                k_out[rows, :] = fresh_ref[s * parts + i, :part_rows, :]
            for h in range(HEADS):
                tile = jnp.concatenate(
                    [fresh_ref[s * parts + i, part_rows:, lanes(h)] for i in range(parts)], axis=0
                )
                vt_out[spot, lanes(h), :] = tile.T


def stage(table, fresh, key_cache, value_cache):
    vmem = pl.BlockSpec(memory_space=pltpu.VMEM)
    hbm = pl.BlockSpec(memory_space=pltpu.HBM)
    pieces = NBLK // NEAR_BLOCKS
    return pl.pallas_call(
        stage_kernel,
        in_specs=[pl.BlockSpec(memory_space=pltpu.SMEM), vmem, hbm, hbm],
        out_specs=[vmem] * 2,
        scratch_shapes=[
            pltpu.VMEM((NBLK * BLK, WIDE), jnp.bfloat16),
            pltpu.SemaphoreType.DMA((pieces,)),
            pltpu.SemaphoreType.DMA((pieces,)),
        ],
        out_shape=[
            jax.ShapeDtypeStruct((NBLK * BLK, WIDE), jnp.bfloat16),
            jax.ShapeDtypeStruct((NBLK, WIDE, BLK), jnp.bfloat16),
        ],
        compiler_params=pltpu.CompilerParams(vmem_limit_bytes=STAGE_LIMIT),
        cost_estimate=pl.CostEstimate(flops=0, bytes_accessed=15_000_000, transcendentals=0),
        name="stage",
    )(table, fresh, key_cache, value_cache)


def near_kernel(q_ref, k_ref, vt_ref, o_out, s_out, acc, top, tot, sbuf, pbuf):
    acc[...] = jnp.zeros_like(acc)
    top[...] = jnp.full_like(top, LOW)
    tot[...] = jnp.zeros_like(tot)

    def chunk(step, carry):
        def score(h):
            high = None
            for b in range(NEAR_BLOCKS):
                part = lax.dot_general(
                    k_ref[pl.ds(pl.multiple_of((step * NEAR_BLOCKS + b) * BLK, BLK), BLK), lanes(h)],
                    q_ref[:, lanes(h)],
                    (((1,), (1,)), ((), ())),
                    preferred_element_type=jnp.float32,
                )
                sbuf[h % 2, b * BLK : (b + 1) * BLK, :] = part
                peak = eighths(part, jnp.maximum)
                high = peak if high is None else jnp.maximum(high, peak)
            return jnp.max(high, axis=0, keepdims=True)

        ahead = score(0)
        for h in range(HEADS):
            high = ahead
            if h + 1 < HEADS:
                ahead = score(h + 1)
            old = top[h : h + 1, :]
            new = jnp.maximum(old, high)
            shrink = jnp.exp2((old - new) * EXPO)
            top[h : h + 1, :] = new
            added = None
            for b in range(NEAR_BLOCKS):
                weights = jnp.exp2((sbuf[h % 2, b * BLK : (b + 1) * BLK, :] - new) * EXPO)
                pbuf[h % 2, b * BLK : (b + 1) * BLK, :] = weights.astype(jnp.bfloat16)
                part = eighths(weights, jnp.add)
                added = part if added is None else added + part
            tot[h : h + 1, :] = tot[h : h + 1, :] * shrink + jnp.sum(added, axis=0, keepdims=True)
            values = jnp.concatenate(
                [vt_ref[step * NEAR_BLOCKS + b, lanes(h), :] for b in range(NEAR_BLOCKS)], axis=1
            )
            acc[h] = acc[h] * shrink + jnp.dot(
                values, pbuf[h % 2], preferred_element_type=jnp.float32
            )
        return carry

    lax.fori_loop(0, NBLK // NEAR_BLOCKS, chunk, 0)
    for h in range(HEADS):
        total = tot[h : h + 1, :]
        part = acc[h] * (1.0 / total)
        level = top[h : h + 1, :] * EXPO + jnp.log2(total)
        for s in range(MB):
            o_out[s, :, lanes(h)] = part[:, s * BLK : (s + 1) * BLK].astype(jnp.bfloat16)
            s_out[s : s + 1, lanes(h)] = level[:, s * BLK : (s + 1) * BLK]


def near(q, keys, values):
    rows = MB * BLK
    vmem = pl.BlockSpec(memory_space=pltpu.VMEM)
    return pl.pallas_call(
        near_kernel,
        in_specs=[vmem] * 3,
        out_specs=[vmem] * 2,
        scratch_shapes=[
            pltpu.VMEM((HEADS, HD, rows), jnp.float32),
            pltpu.VMEM((8, rows), jnp.float32),
            pltpu.VMEM((8, rows), jnp.float32),
            pltpu.VMEM((2, NEAR_ROWS, rows), jnp.float32),
            pltpu.VMEM((2, NEAR_ROWS, rows), jnp.bfloat16),
        ],
        out_shape=[
            jax.ShapeDtypeStruct((MB, HD, WIDE), jnp.bfloat16),
            jax.ShapeDtypeStruct((8, WIDE), jnp.float32),
        ],
        compiler_params=params(),
        cost_estimate=pl.CostEstimate(
            flops=100_000_000, bytes_accessed=400_000, transcendentals=0
        ),
        name="near",
    )(q, keys, values)


def put_stats(stat, index, apart, h, level):
    high = level.astype(jnp.bfloat16).astype(jnp.float32)
    rest = level - high
    mid = rest.astype(jnp.bfloat16).astype(jnp.float32)
    row = lax.broadcasted_iota(jnp.int32, (stat.shape[0], HD), 0) - index
    tile = stat[:, lanes(h)]
    for place, piece in ((0, high), (apart, mid), (2 * apart, rest - mid)):
        tile = jnp.where(row == place, piece, tile)
    stat[:, lanes(h)] = tile


def frame_at(table, item, shift):
    me = table[ME]
    odd = table[CORE] == 1
    z = lax.shift_right_logical(me, 2) + jnp.where(odd, item, shift)
    x = (me & (SIDE - 1)) + jnp.where(odd, shift, item)
    return (z & (SIDE - 1)) * SIDE + (x & (SIDE - 1))


def far_kernel(shift, skip, table, q_ref, keys, values, *refs):
    out, done, stat = refs[-3:]
    done[...] = jnp.zeros_like(done)
    stat[...] = jnp.zeros_like(stat)
    me = table[ME]

    def step(i, carry):
        slot = i & (MB - 1)
        frame = frame_at(table, lax.shift_right_logical(i, 1), shift)
        count = table[RADIAL + jnp.maximum(jnp.abs(frame - me) - 1, 0)]
        start = table[frame * MB + slot] - lax.shift_right_logical(count, 1)
        start = jnp.where(start < 0, start + NBLK, start)
        spots = [start + j for j in range(CMAX)]
        spots = [jnp.where(spot >= NBLK, spot - NBLK, spot) for spot in spots]
        count = jnp.where(table[COUNTS + frame] > slot, count, 0)
        rows = pl.ds(pl.multiple_of(i * BLK, BLK), BLK)
        for n in range(1, CMAX + 1):

            @pl.when(count == n)
            def _():
                def score(h):
                    return [
                        lax.dot_general(
                            keys[pl.ds(pl.multiple_of(spots[j] * BLK, BLK), BLK), lanes(h)],
                            q_ref[rows, lanes(h)],
                            (((1,), (1,)), ((), ())),
                            preferred_element_type=jnp.float32,
                        )
                        for j in range(n)
                    ]

                scores = [score(h) for h in range(HEADS)]
                tops, totals, probs = [], [], []
                for h in range(HEADS):
                    peaks = [eighths(x, jnp.maximum) for x in scores[h]]
                    top = jnp.max(functools.reduce(jnp.maximum, peaks), axis=0, keepdims=True)
                    weights = [jnp.exp2((x - top) * EXPO) for x in scores[h]]
                    sums = [eighths(x, jnp.add) for x in weights]
                    totals.append(jnp.sum(functools.reduce(jnp.add, sums), axis=0, keepdims=True))
                    tops.append(top)
                    probs.append(jnp.concatenate([x.astype(jnp.bfloat16) for x in weights], axis=0))
                parts = [
                    jnp.dot(
                        jnp.concatenate([values[spots[j], lanes(h), :] for j in range(n)], axis=1),
                        probs[h],
                        preferred_element_type=jnp.float32,
                    )
                    for h in range(HEADS)
                ]
                for h in range(HEADS):
                    out[rows, lanes(h)] = (parts[h] * (1.0 / totals[h])).astype(jnp.bfloat16)
                    put_stats(stat, i, ITEMS, h, tops[h] * EXPO + jnp.log2(totals[h]))

        return carry

    lax.fori_loop(skip * MB, ITEMS, step, 0)
    out[SIDE * ROWS :, :] = stat[...].astype(jnp.bfloat16)


def far(table, queries, keys, values, shift, skip, after=()):
    smem = pl.BlockSpec(memory_space=pltpu.SMEM)
    vmem = pl.BlockSpec(memory_space=pltpu.VMEM)
    return pl.pallas_call(
        functools.partial(far_kernel, shift, skip),
        in_specs=[smem] + [vmem] * (3 + len(after)),
        out_specs=[vmem] * 2,
        scratch_shapes=[pltpu.VMEM((STAT, WIDE), jnp.float32)],
        out_shape=[
            jax.ShapeDtypeStruct((PAY, WIDE), jnp.bfloat16),
            jax.ShapeDtypeStruct((8, BLK), jnp.float32),
        ],
        compiler_params=params(),
        cost_estimate=pl.CostEstimate(
            flops=100_000_000, bytes_accessed=400_000, transcendentals=0
        ),
        name="far",
    )(table, queries, keys, values, *after)


def read_level(ref, base, index, apart):
    tile = ref[base:, :].astype(jnp.float32)
    return (
        tile[index : index + 1]
        + tile[apart + index : apart + index + 1]
        + tile[2 * apart + index : 2 * apart + index + 1]
    )


def read_part(ref, index):
    return ref[index * BLK : (index + 1) * BLK, :].astype(jnp.float32)


def merge(levels, parts):
    top = functools.reduce(jnp.maximum, levels)
    shares = [jnp.exp2(level - top) for level in levels]
    total = functools.reduce(jnp.add, shares)
    scale = 1.0 / total
    out = None
    for share, part in zip(shares, parts):
        term = part() * (share * scale)
        out = term if out is None else out + term
    return out, top + jnp.log2(total)


def first_merge_kernel(d, *refs):
    *sources, _, out, stat = refs
    if d == 0:
        near_ref, near_stat, *sources = sources
    stat[...] = jnp.zeros_like(stat)
    for slot in range(MB):
        index = d * MB + slot
        levels = [read_level(r, SIDE * ROWS, index, ITEMS) for r in sources]
        parts = [functools.partial(read_part, r, index) for r in sources]
        if d == 0:
            levels.append(near_stat[slot : slot + 1, :])
            parts.append(lambda: near_ref[slot].astype(jnp.float32))
        value, level = merge(levels, parts)
        out[slot * BLK : (slot + 1) * BLK, :] = value.astype(jnp.bfloat16)
        for h in range(HEADS):
            put_stats(stat, slot, MB, h, level[:, lanes(h)])
    out[ROWS:, :] = stat[...].astype(jnp.bfloat16)


def first_merge(d, near_part, near_stat, local, received, after):
    own = (near_part, near_stat) if d == 0 else (local,)
    return pl.pallas_call(
        functools.partial(first_merge_kernel, d),
        out_shape=jax.ShapeDtypeStruct((ROWS + ONE, WIDE), jnp.bfloat16),
        scratch_shapes=[pltpu.VMEM((ONE, WIDE), jnp.float32)],
        compiler_params=params(),
        cost_estimate=pl.CostEstimate(flops=4_000_000, bytes_accessed=400_000, transcendentals=0),
        name="first_merge",
    )(*own, *received, after)


def last_merge_kernel(table, *refs):
    *sources, out = refs
    for slot in range(MB):
        live = table[COUNTS + table[ME]] > slot

        @pl.when(live)
        def _():
            levels = [read_level(r, ROWS, slot, MB) for r in sources]
            parts = [functools.partial(read_part, r, slot) for r in sources]
            value, _ = merge(levels, parts)
            for h in range(HEADS):
                out[slot * BLK : (slot + 1) * BLK, lanes(h)] = value[:, lanes(h)].T.astype(jnp.bfloat16)

        @pl.when(jnp.logical_not(live))
        def _():
            out[slot * BLK : (slot + 1) * BLK, :] = jnp.zeros((BLK, WIDE), jnp.bfloat16)


def last_merge(table, parts):
    vmem = pl.BlockSpec(memory_space=pltpu.VMEM)
    return pl.pallas_call(
        last_merge_kernel,
        in_specs=[pl.BlockSpec(memory_space=pltpu.SMEM)] + [vmem] * len(parts),
        out_specs=vmem,
        out_shape=jax.ShapeDtypeStruct((ROWS, WIDE), jnp.bfloat16),
        compiler_params=params(),
        name="last_merge",
    )(table, *parts)


HEAD_SHARDS = 8


def give(x, k, step):
    pairs = []
    for z in range(SIDE):
        for c in range(SIDE):
            for head in range(HEAD_SHARDS):
                along_x = (head % 2 == 0) == (step == 1)
                to = (z, (c + k) % SIDE) if along_x else ((z + k) % SIDE, c)
                pairs.append(
                    ((z * SIDE + c) * HEAD_SHARDS + head, (to[0] * SIDE + to[1]) * HEAD_SHARDS + head)
                )
    return lax.ppermute(x, ("frame", "head"), pairs)


def fetch(x, k, step):
    return give(x, SIDE - k, step)


ORDER = (2, 1, 3)


def body(
    fresh_queries,
    fresh_keys,
    fresh_values,
    key_cache,
    value_cache,
    masked_blocks,
    masked_count,
    radial_counts,
):
    me = lax.axis_index("frame").astype(jnp.int32)
    core = lax.axis_index("head").astype(jnp.int32) % 2
    table = jnp.concatenate(
        [masked_blocks.reshape(-1), masked_count, radial_counts, me[None], core[None]]
    )
    q = lax.all_to_all(split_heads(fresh_queries[0]), "head", 0, 0, tiled=True).reshape(ROWS, WIDE)
    ring = [q] + [fetch(q, k, 1) for k in range(1, SIDE)]
    full = stack(*ring)
    queries = {k: fetch(full, k, 2) for k in ORDER}
    fresh = lax.all_to_all(
        split_heads(fresh_keys[0], fresh_values[0]), "head", 0, 0, tiled=True
    )
    keys, values = stage(table, fresh, key_cache[0], value_cache[0])
    part, done = far(table, queries[ORDER[0]], keys, values, ORDER[0], 0)
    back = [give(part, ORDER[0], 2)]
    for k in ORDER[1:]:
        part, _ = far(table, queries[k], keys, values, k, 0, (done,))
        back.append(give(part, k, 2))
    q, back[0] = lax.optimization_barrier((q, back[0]))
    local, _ = far(table, full, keys, values, 0, 1)
    near_part, near_stat = near(q, keys, values)
    near_stat, back[1], back[2] = lax.optimization_barrier((near_stat, back[1], back[2]))
    after, final = near_stat, {}
    for k in (1, 3, 2, 0):
        after = first_merge(k, near_part, near_stat, local, back, after)
        final[k] = give(after, k, 1) if k else after
    final = [final[k] for k in range(SIDE)]
    edited = last_merge(table, final).reshape(8, MB * BLK // 8, WIDE)
    edited = lax.all_to_all(edited, "head", 0, 0, tiled=True)
    return join_heads(edited)[None]


def solution(mesh):
    placed = (
        P("frame", "head", None),
        P("frame", "head", None),
        P("frame", "head", None),
        P("frame", None, "head"),
        P("frame", None, "head"),
        P(),
        P(),
        P(),
    )
    return jax.shard_map(
        body, mesh=mesh, in_specs=placed, out_specs=P("frame", "head", None), check_vma=False
    )
```
